512 devices in a mesh: dp: 8 (over y, x_hi), blk: 64 (over x_lo, z, core).
Axes of the slice: x: 4 (x_hi: 2, x_lo: 2; x = x_hi * 2 + x_lo), y: 4, z: 16, core: 2. Of those that a mesh axis runs over, the one named last changes fastest.
Arguments:
- gradients: bfloat16 [8, 1024, 64, 1024], P('dp', 'blk'), may hold values from -36 to 36
- left_stat: float32 [512, 128, 1024], P(('dp', 'blk')), may hold values from -300 to 3000
- right_stat: float32 [512, 128, 1024], P(('dp', 'blk')), may hold values from -300 to 3000
- left_root: bfloat16 [512, 128, 1024], P(('dp', 'blk')), may hold values from -1 to 4
- right_root: bfloat16 [512, 128, 1024], P(('dp', 'blk')), may hold values from -1 to 4
Outputs:
- update: bfloat16 [64, 1024, 1024], P('dp', None, 'blk')
- new_left: float32 [512, 128, 1024], P(('dp', 'blk'))
- new_right: float32 [512, 128, 1024], P(('dp', 'blk'))
The draws below stay inside these ranges and needn't reach their ends.
All inputs are finite; a program needn't handle non-finite values.
Results may differ from the reference program's by a relative error of at most 0.019.
Values may be sent and summed in bfloat16 or wider, within the bound.
A program may use at most 64 MiB of HBM per device.

```python
import math
import jax
import jax.numpy as jnp
from jax import lax

B = 1024
GROUP = 8
BLOCKS = 64
N_DP = 8


def spread_matrix(key, low_value, high_value, off_scale):
    first_key, second_key = jax.random.split(key)
    noise_part = jnp.clip(jax.random.normal(first_key, (BLOCKS, B, B), jnp.float32), -4.0, 4.0)
    symmetric = (noise_part + jnp.swapaxes(noise_part, 1, 2)) * (off_scale / math.sqrt(2.0 * B))
    diagonal = jax.random.uniform(second_key, (BLOCKS, B), jnp.float32, low_value, high_value)
    whole = symmetric + diagonal[:, :, None] * jnp.eye(B, dtype=jnp.float32)
    return whole.reshape(BLOCKS * GROUP, B // GROUP, B)


def stat_matrix(key, low_value, high_value, off_scale, off_limit):
    first_key, second_key = jax.random.split(key)
    noise_part = jnp.clip(jax.random.normal(first_key, (BLOCKS, B, B), jnp.float32), -4.0, 4.0)
    symmetric = (noise_part + jnp.swapaxes(noise_part, 1, 2)) * (off_scale / math.sqrt(2.0 * B))
    symmetric = jnp.clip(symmetric, -off_limit, off_limit)
    diagonal = jnp.exp(jax.random.uniform(second_key, (BLOCKS, B), jnp.float32, math.log(low_value), math.log(high_value)))
    pair_scale = jnp.sqrt(diagonal[:, :, None] * diagonal[:, None, :])
    identity = jnp.eye(B, dtype=jnp.float32)
    whole = symmetric * pair_scale * (1.0 - identity) + diagonal[:, :, None] * identity
    return whole.reshape(BLOCKS * GROUP, B // GROUP, B)


def draw_gradients(key, part):
    key = jax.random.fold_in(key, 10)
    keys = jax.random.split(key, 4)
    row_trend = jnp.exp(math.log(3.0) * jnp.arange(B, dtype=jnp.float32) / B)
    row_scale = jnp.exp(jax.random.uniform(keys[0], (B,), jnp.float32, 0.0, math.log(10.0))) * row_trend
    column_scale = jnp.exp(jax.random.uniform(keys[1], (B,), jnp.float32, 0.0, math.log(10.0)))
    block_scale = jnp.exp(jax.random.uniform(keys[2], (BLOCKS,), jnp.float32, math.log(0.5), math.log(2.0)))
    entries = jnp.clip(jax.random.normal(keys[3], (N_DP, B, BLOCKS, B), jnp.float32), -6.0, 6.0)
    values = entries * row_scale[None, :, None, None] * block_scale[None, None, :, None] * column_scale * 0.01
    return values.astype(jnp.bfloat16)


def draw_left_stat(key, part):
    key = jax.random.fold_in(key, 11)
    return stat_matrix(key, 30.0, 600.0, 0.3, 0.1)


def draw_right_stat(key, part):
    key = jax.random.fold_in(key, 12)
    return stat_matrix(key, 30.0, 600.0, 0.3, 0.1)


def draw_left_root(key, part):
    key = jax.random.fold_in(key, 13)
    return spread_matrix(key, 1.5, 3.0, 0.7).astype(jnp.bfloat16)


def draw_right_root(key, part):
    key = jax.random.fold_in(key, 14)
    return spread_matrix(key, 1.5, 3.0, 0.7).astype(jnp.bfloat16)


def setup_inputs(seed: int = 0) -> dict:
    seeds = jax.random.split(jax.random.key(seed), 6)
    gradients = draw_gradients(jax.random.fold_in(seeds[5], 71), 0)
    left_stat = draw_left_stat(jax.random.fold_in(seeds[5], 71), 0)
    right_stat = draw_right_stat(jax.random.fold_in(seeds[5], 71), 0)
    left_root = draw_left_root(jax.random.fold_in(seeds[5], 71), 0)
    right_root = draw_right_root(jax.random.fold_in(seeds[5], 71), 0)
    return {"gradients": gradients, "left_stat": left_stat, "right_stat": right_stat, "left_root": left_root, "right_root": right_root}


STAT_DECAY = 0.95
GRAFT_EPS = 1e-06

def block_step(replica_blocks, left_block, right_block, left_factor, right_factor):
    summed = lax.optimization_barrier(jnp.sum(replica_blocks.astype(jnp.float32), axis=0))
    gram_left = jnp.dot(summed, summed.T, precision=lax.Precision.HIGHEST)
    gram_right = jnp.dot(summed.T, summed, precision=lax.Precision.HIGHEST)
    new_left = STAT_DECAY * left_block + (1.0 - STAT_DECAY) * gram_left
    new_right = STAT_DECAY * right_block + (1.0 - STAT_DECAY) * gram_right
    summed_low = summed.astype(jnp.bfloat16)
    left_applied = jnp.dot(left_factor, summed_low, preferred_element_type=jnp.float32).astype(jnp.bfloat16)
    preconditioned = jnp.dot(left_applied, right_factor, preferred_element_type=jnp.float32)
    graft_scale = jnp.sqrt((jnp.sum(summed * summed) + GRAFT_EPS) / (jnp.sum(preconditioned * preconditioned) + GRAFT_EPS))
    return ((preconditioned * graft_scale).astype(jnp.bfloat16), new_left, new_right)

def reference(gradients, left_stat, right_stat, left_root, right_root):
    by_block = jnp.moveaxis(gradients, 2, 0)
    whole_shape = (BLOCKS, B, B)
    slab_shape = (BLOCKS * GROUP, B // GROUP, B)

    def apply_block(inputs):
        return block_step(inputs[0], inputs[1], inputs[2], inputs[3], inputs[4])
    updates, new_left, new_right = lax.map(apply_block, (by_block, left_stat.reshape(whole_shape), right_stat.reshape(whole_shape), left_root.reshape(whole_shape), right_root.reshape(whole_shape)))
    return (updates, new_left.reshape(slab_shape), new_right.reshape(slab_shape))
```

```python
import functools

import jax
import jax.numpy as jnp
from jax import lax
from jax.experimental import pallas as pl
from jax.experimental.pallas import tpu as pltpu
from jax.sharding import PartitionSpec as P

GROUP = 8
STAT_DECAY = 0.95
GRAFT_EPS = 1e-06
MESH = pl.DeviceIdType.MESH
F32 = jnp.float32
BF16 = jnp.bfloat16


def remote(src, dst, send, recv, **where):
    return pltpu.make_async_remote_copy(
        src_ref=src,
        dst_ref=dst,
        send_sem=send,
        recv_sem=recv,
        device_id=where,
        device_id_type=MESH,
    )


class LineGather:
    def __init__(self, view, group, member, send, recv):
        self.view, self.group, self.member = view, group, member
        self.send, self.recv = send, recv
        self.chip, self.core = member // 2, member % 2

    def copy(self, slot, target, way):
        return remote(
            self.view(slot),
            self.view(slot),
            self.send.at[slot, way],
            self.recv.at[slot],
            blk=self.group * GROUP + target,
        )

    def to_right(self, slot):
        return self.copy(slot, self.member + 2, 0)

    def to_left(self, slot):
        return self.copy(slot, self.member - 2, 1)

    def to_sibling(self, slot):
        return self.copy(slot, self.chip * 2 + 1 - self.core, 2)

    def steps(self, act_own, act_left, act_right):
        chip, core = self.chip, self.core
        act_own(self.member)
        for hop in range(1, 4):
            pl.when(chip >= hop)(functools.partial(act_left, (chip - hop) * 2 + core))
            pl.when(chip + hop <= 3)(functools.partial(act_right, (chip + hop) * 2 + core))

    def run(self):
        chip, core = self.chip, self.core

        def own(slot):
            pl.when(chip < 3)(lambda: self.to_right(slot).start())
            pl.when(chip > 0)(lambda: self.to_left(slot).start())
            self.to_sibling(slot).start()

        def from_left(slot):
            self.to_right(slot).wait_recv()
            pl.when(chip < 3)(lambda: self.to_right(slot).start())
            self.to_sibling(slot).start()

        def from_right(slot):
            self.to_left(slot).wait_recv()
            pl.when(chip > 0)(lambda: self.to_left(slot).start())
            self.to_sibling(slot).start()

        self.steps(own, from_left, from_right)
        for other in range(4):
            self.to_sibling(other * 2 + 1 - core).wait_recv()

    def drain(self):
        chip = self.chip

        def own(slot):
            pl.when(chip < 3)(lambda: self.to_right(slot).wait_send())
            pl.when(chip > 0)(lambda: self.to_left(slot).wait_send())
            self.to_sibling(slot).wait_send()

        def from_left(slot):
            pl.when(chip < 3)(lambda: self.to_right(slot).wait_send())
            self.to_sibling(slot).wait_send()

        def from_right(slot):
            pl.when(chip > 0)(lambda: self.to_left(slot).wait_send())
            self.to_sibling(slot).wait_send()

        self.steps(own, from_left, from_right)


def kernel(
    replicas,
    owners,
    grad_ref,
    left_ref,
    right_ref,
    lroot_ref,
    rroot_ref,
    update_ref,
    newl_ref,
    newr_ref,
    land,
    fsum,
    summed,
    gbuf,
    qbuf,
    proot,
    lstat,
    rstat,
    lapp,
    uflip,
    usend,
    uland,
    squares,
    ubuf,
    local_sem,
    rs_send,
    rs_recv,
    qg_send,
    qg_recv,
    a2a_send,
    a2a_recv,
    gg_send,
    gg_recv,
    sq_send,
    sq_recv,
    up_send,
    up_recv,
    out_sem,
):
    p = lax.axis_index("dp")
    b = lax.axis_index("blk")
    groups = owners // GROUP
    group, member = b // GROUP, b % GROUP
    width = grad_ref.shape[3]
    slab = width // GROUP
    tile = 256
    tiles = width // tile

    loads = [
        pltpu.make_async_copy(grad_ref.at[:, p], land.at[0], local_sem.at[0]),
        pltpu.make_async_copy(rroot_ref, qbuf.at[member], local_sem.at[1]),
        pltpu.make_async_copy(lroot_ref, proot, local_sem.at[2]),
        pltpu.make_async_copy(left_ref, lstat, local_sem.at[3]),
        pltpu.make_async_copy(right_ref, rstat, local_sem.at[4]),
    ]
    for load in loads:
        load.start()

    barrier = pltpu.get_barrier_semaphore()
    for off in range(1, replicas):
        pl.semaphore_signal(
            barrier, inc=1, device_id={"dp": (p + off) % replicas}, device_id_type=MESH
        )

    @pl.loop(1, owners)
    def _(off):
        pl.semaphore_signal(
            barrier, inc=1, device_id={"blk": (b + off) % owners}, device_id_type=MESH
        )

    pl.semaphore_wait(barrier, replicas - 1 + owners - 1)

    def reduce_copy(off):
        to = (p + off) % replicas
        return remote(
            grad_ref.at[:, to], land.at[off], rs_send.at[off], rs_recv.at[off], dp=to
        )

    for off in range(1, replicas):
        reduce_copy(off).start()

    loads[1].wait()
    qgather = LineGather(lambda s: qbuf.at[s], group, member, qg_send, qg_recv)
    qgather.run()

    loads[0].wait()
    for off in range(1, replicas):
        reduce_copy(off).wait_recv()

    row_count = land.shape[1]

    @pl.loop(0, row_count)
    def _(row):
        total = land[0, row].astype(F32)
        for off in range(1, replicas):
            total = total + land[off, row].astype(F32)
        place = pl.ds(pl.multiple_of(row * groups, groups), groups)
        for lane in range(width // 128):
            fsum[lane, place, :] = total[:, lane * 128 : (lane + 1) * 128]

    for block in range(groups):
        for lane in range(width // 128):
            summed[block, :, lane * 128 : (lane + 1) * 128] = fsum[
                lane, pl.ds(block, row_count, stride=groups), :
            ].astype(BF16)

    def spread_copy(off):
        to = (group + off) % groups
        return remote(
            summed.at[to],
            gbuf.at[group, member],
            a2a_send.at[off],
            a2a_recv.at[off],
            blk=to * GROUP + member,
        )

    for off in range(1, groups):
        spread_copy(off).start()
    own = pltpu.make_async_copy(summed.at[group], gbuf.at[group, member], local_sem.at[5])
    own.start()
    own.wait()
    for off in range(1, groups):
        spread_copy(off).wait_recv()

    ggather = LineGather(lambda s: gbuf.at[:, s], group, member, gg_send, gg_recv)
    ggather.run()

    loads[2].wait()
    left_factor = proot[...]

    @pl.loop(0, tiles)
    def _(step):
        cols = pl.ds(pl.multiple_of(step * tile, tile), tile)
        grad = gbuf[:, :, :, cols].reshape(width, tile)
        lapp[:, cols] = jnp.dot(left_factor, grad, preferred_element_type=F32).astype(BF16)

    rows = gbuf[member].reshape(slab, width)
    wide = rows.astype(F32)
    squares[member, 0:8] = jnp.sum(
        (wide * wide).reshape(slab // 8, 8, width // 128, 128), axis=(0, 2)
    )
    squares[member, 8:16] = jnp.zeros((8, 128), F32)
    applied = lapp[...]

    @pl.loop(0, tiles)
    def _(step):
        cols = pl.ds(pl.multiple_of(step * tile, tile), tile)
        part = jnp.dot(
            applied, qbuf[:, :, cols].reshape(width, tile), preferred_element_type=F32
        )
        flip = part.T
        uflip[cols, :] = flip
        squares[member, 8:16] += jnp.sum((flip * flip).reshape(tile // 8, 8, slab), axis=0)

    def square_copy(off):
        to = (member + off) % GROUP
        return remote(
            squares.at[member],
            squares.at[member],
            sq_send.at[off],
            sq_recv.at[off],
            blk=group * GROUP + to,
        )

    for off in range(1, GROUP):
        square_copy(off).start()

    loads[3].wait()

    @pl.loop(0, tiles)
    def _(step):
        cols = pl.ds(pl.multiple_of(step * tile, tile), tile)
        per = tile // (width // groups)
        other = gbuf[pl.ds(step * per, per)].reshape(tile, width)
        gram = lax.dot_general(
            rows, other, (((1,), (1,)), ((), ())), preferred_element_type=F32
        )
        lstat[:, cols] = STAT_DECAY * lstat[:, cols] + (1.0 - STAT_DECAY) * gram

    store_left = pltpu.make_async_copy(lstat, newl_ref, out_sem.at[0])
    store_left.start()

    for off in range(1, GROUP):
        square_copy(off).wait_recv()
    total = jnp.sum(squares[...], axis=0)
    grad_square = jnp.sum(total[0:8], keepdims=True)
    update_square = jnp.sum(total[8:16], keepdims=True)
    scale = jnp.sqrt((grad_square + GRAFT_EPS) / (update_square + GRAFT_EPS))
    usend[...] = (uflip[...] * scale).astype(BF16).reshape(usend.shape)

    def update_copy(off):
        to = (b + off) % owners
        return remote(usend.at[to], uland.at[group, member], up_send, up_recv, blk=to)

    @pl.loop(1, owners)
    def _(off):
        update_copy(off).start()

    mine = pltpu.make_async_copy(usend.at[b], uland.at[group, member], up_recv)
    mine.start()

    loads[4].wait()
    first = pl.ds(pl.multiple_of(member * slab, slab), slab)
    columns = gbuf[:, :, :, first].reshape(width, slab).T

    @pl.loop(0, tiles)
    def _(step):
        cols = pl.ds(pl.multiple_of(step * tile, tile), tile)
        grad = gbuf[:, :, :, cols].reshape(width, tile)
        gram = jnp.dot(columns, grad, preferred_element_type=F32)
        rstat[:, cols] = STAT_DECAY * rstat[:, cols] + (1.0 - STAT_DECAY) * gram

    store_right = pltpu.make_async_copy(rstat, newr_ref, out_sem.at[1])
    store_right.start()

    pltpu.make_async_copy(uland, uland, up_recv).wait()
    for block in range(groups):
        for part in range(GROUP):
            ubuf[block, :, part * slab : (part + 1) * slab] = uland[block, part]
    store_update = pltpu.make_async_copy(ubuf, update_ref, out_sem.at[2])
    store_update.start()

    for off in range(1, replicas):
        reduce_copy(off).wait_send()
    qgather.drain()
    for off in range(1, groups):
        spread_copy(off).wait_send()
    ggather.drain()
    for off in range(1, GROUP):
        square_copy(off).wait_send()
    others = usend.at[pl.ds(0, owners - 1)]
    pltpu.make_async_copy(others, others, up_send).wait()
    store_left.wait()
    store_right.wait()
    store_update.wait()


def on_device(replicas, owners, gradients, left_stat, right_stat, left_root, right_root):
    _, row_count, block_count, width = gradients.shape
    local = block_count // replicas
    slab = width // GROUP
    part = width // owners
    groups = owners // GROUP
    dma = pltpu.SemaphoreType.DMA
    update, new_left, new_right = pl.pallas_call(
        functools.partial(kernel, replicas, owners),
        out_shape=(
            jax.ShapeDtypeStruct((local, part, width), BF16),
            jax.ShapeDtypeStruct((slab, width), F32),
            jax.ShapeDtypeStruct((slab, width), F32),
        ),
        in_specs=[pl.BlockSpec(memory_space=pl.ANY)] * 5,
        out_specs=[pl.BlockSpec(memory_space=pl.ANY)] * 3,
        scratch_shapes=[
            pltpu.VMEM((replicas, row_count, local, width), BF16),
            pltpu.VMEM((width // 128, row_count * local, 128), F32),
            pltpu.VMEM((local, row_count, width), BF16),
            pltpu.VMEM((groups, GROUP, row_count, width), BF16),
            pltpu.VMEM((GROUP, slab, width), BF16),
            pltpu.VMEM((slab, width), BF16),
            pltpu.VMEM((slab, width), F32),
            pltpu.VMEM((slab, width), F32),
            pltpu.VMEM((slab, width), BF16),
            pltpu.VMEM((width, slab), F32),
            pltpu.VMEM((owners, part, slab), BF16),
            pltpu.VMEM((groups, GROUP, part, slab), BF16),
            pltpu.VMEM((GROUP, 16, 128), F32),
            pltpu.VMEM((local, part, width), BF16),
            dma((6,)),
            dma((replicas,)),
            dma((replicas,)),
            dma((GROUP, 3)),
            dma((GROUP,)),
            dma((groups,)),
            dma((groups,)),
            dma((GROUP, 3)),
            dma((GROUP,)),
            dma((GROUP,)),
            dma((GROUP,)),
            dma,
            dma,
            dma((3,)),
        ],
        compiler_params=pltpu.CompilerParams(
            collective_id=0, has_side_effects=True, vmem_limit_bytes=48 * 2**20
        ),
        cost_estimate=pl.CostEstimate(
            flops=8 * slab * width * width, bytes_accessed=8 * 2**20, transcendentals=0
        ),
    )(
        gradients.reshape(row_count, replicas, local, width),
        left_stat[0],
        right_stat[0],
        left_root[0],
        right_root[0],
    )
    return jnp.swapaxes(update, 1, 2), new_left[None], new_right[None]


def solution(mesh):
    specs = (P("dp", "blk", None, None),) + (P(("dp", "blk"), None, None),) * 4
    out_specs = (P("dp", None, "blk"), P(("dp", "blk"), None, None), P(("dp", "blk"), None, None))
    return jax.shard_map(
        functools.partial(on_device, mesh.shape["dp"], mesh.shape["blk"]),
        mesh=mesh,
        in_specs=specs,
        out_specs=out_specs,
        check_vma=False,
    )
```

```python
import functools

import jax
import jax.numpy as jnp
from jax import lax
from jax.experimental import pallas as pl
from jax.experimental.pallas import tpu as pltpu
from jax.sharding import PartitionSpec as P

GROUP = 8
STAT_DECAY = 0.95
GRAFT_EPS = 1e-06
MESH = pl.DeviceIdType.MESH
F32 = jnp.float32
BF16 = jnp.bfloat16


def remote(src, dst, send, recv, **where):
    return pltpu.make_async_remote_copy(
        src_ref=src,
        dst_ref=dst,
        send_sem=send,
        recv_sem=recv,
        device_id=where,
        device_id_type=MESH,
    )


class LineGather:
    def __init__(self, view, group, member, send, recv):
        self.view, self.group, self.member = view, group, member
        self.send, self.recv = send, recv
        self.chip, self.core = member // 2, member % 2

    def copy(self, slot, target, way):
        return remote(
            self.view(slot),
            self.view(slot),
            self.send.at[slot, way],
            self.recv.at[slot],
            blk=self.group * GROUP + target,
        )

    def to_right(self, slot):
        return self.copy(slot, self.member + 2, 0)

    def to_left(self, slot):
        return self.copy(slot, self.member - 2, 1)

    def to_sibling(self, slot):
        return self.copy(slot, self.chip * 2 + 1 - self.core, 2)

    def own(self):
        slot = self.member
        pl.when(self.chip < 3)(lambda: self.to_right(slot).start())
        pl.when(self.chip > 0)(lambda: self.to_left(slot).start())
        self.to_sibling(slot).start()

    def hop(self, hop):
        left, right = self.member - 2 * hop, self.member + 2 * hop

        @pl.when(self.chip >= hop)
        def _():
            self.to_right(left).wait_recv()
            pl.when(self.chip < 3)(lambda: self.to_right(left).start())
            self.to_sibling(left).start()

        @pl.when(self.chip + hop <= 3)
        def _():
            self.to_left(right).wait_recv()
            pl.when(self.chip > 0)(lambda: self.to_left(right).start())
            self.to_sibling(right).start()

    def finish(self):
        for other in range(4):
            self.to_sibling(other * 2 + 1 - self.core).wait_recv()

    def drain(self):
        chip = self.chip
        pl.when(chip < 3)(lambda: self.to_right(self.member).wait_send())
        pl.when(chip > 0)(lambda: self.to_left(self.member).wait_send())
        self.to_sibling(self.member).wait_send()
        for hop in range(1, 4):
            left, right = self.member - 2 * hop, self.member + 2 * hop

            @pl.when(chip >= hop)
            def _():
                pl.when(chip < 3)(lambda: self.to_right(left).wait_send())
                self.to_sibling(left).wait_send()

            @pl.when(chip + hop <= 3)
            def _():
                pl.when(chip > 0)(lambda: self.to_left(right).wait_send())
                self.to_sibling(right).wait_send()


def kernel(
    replicas,
    owners,
    grad_ref,
    left_ref,
    right_ref,
    lroot_ref,
    rroot_ref,
    update_ref,
    newl_ref,
    newr_ref,
    gown,
    yfar,
    ynear,
    ymix,
    yadd,
    xout,
    xpass,
    xland,
    fsum,
    summed,
    gbuf,
    qbuf,
    proot,
    lstat,
    rstat,
    lapp,
    uflip,
    usend,
    uland,
    squares,
    ubuf,
    local_sem,
    root_sem,
    y_send,
    y_recv,
    x_send,
    x_recv,
    qg_send,
    qg_recv,
    sp_send,
    gg_send,
    gg_recv,
    sib_send,
    sib_recv,
    sq_send,
    sq_recv,
    up_send,
    up_recv,
    out_sem,
):
    p = lax.axis_index("dp")
    b = lax.axis_index("blk")
    groups = owners // GROUP
    group, member = b // GROUP, b % GROUP
    chip, core = member // 2, member % 2
    y, xh = p // 2, p % 2
    xl, quarter = group // 4, group % 4
    row_count, width = grad_ref.shape[0], grad_ref.shape[3]
    half = row_count // 2
    slab = width // GROUP
    tile = 256
    tiles = width // tile

    loads = [
        pltpu.make_async_copy(grad_ref, gown, local_sem.at[0]),
        pltpu.make_async_copy(rroot_ref, qbuf.at[member], local_sem.at[1]),
        pltpu.make_async_copy(left_ref, lstat, local_sem.at[2]),
        pltpu.make_async_copy(right_ref, rstat, local_sem.at[3]),
    ]
    for block in range(GROUP):
        natural = (block // 4) * 4 + (block % 4 + quarter) % 4
        loads.append(
            pltpu.make_async_copy(
                lroot_ref.at[:, pl.ds(pl.multiple_of(natural * 128, 128), 128)],
                proot.at[:, pl.ds(block * 128, 128)],
                root_sem.at[block],
            )
        )
    loads[0].start()
    loads[1].start()

    flip = (b + owners // 2) % owners
    turn = y * 2 + 1 - xh
    near_a = {"dp": p, "blk": flip}
    near_b = {"dp": turn, "blk": flip}

    def at_y(step, which):
        return ((y + step) % 4) * 2 + which

    barrier = pltpu.get_barrier_semaphore()
    for peer in ({"dp": at_y(1, xh)}, {"dp": at_y(3, xh)}, near_b):
        pl.semaphore_signal(barrier, inc=1, device_id=peer, device_id_type=MESH)

    @pl.loop(1, owners)
    def _(off):
        pl.semaphore_signal(
            barrier, inc=1, device_id={"blk": (b + off) % owners}, device_id_type=MESH
        )

    pl.semaphore_wait(barrier, 3 + owners - 1)

    sides = (1 - xh, xh)
    steps = (1, 3)

    def rows_of(way):
        return pl.ds(way * half, half)

    def y_copy(kind, way, which):
        to = at_y(steps[way], xh)
        if kind == 0:
            src = grad_ref.at[rows_of(way), at_y(2, sides[which])]
            dst = yfar.at[way, which]
        elif kind == 1:
            src = grad_ref.at[rows_of(1 - way), at_y(steps[way], sides[which])]
            dst = ynear.at[way, which]
        else:
            src = yadd.at[way, which]
            dst = ymix.at[way, which]
        return remote(
            src, dst, y_send.at[kind, way, which], y_recv.at[kind, way, which], dp=to
        )

    def x_copy(stage, route):
        if stage == 0:
            where = (near_a, near_b)[route]
            src, dst = xout.at[route], xpass.at[route]
        else:
            where = (near_b, near_a)[route]
            src, dst = xpass.at[route], xland.at[route]
        return remote(src, dst, x_send.at[stage, route], x_recv.at[stage, route], **where)

    ways = (0, 1)
    for way in ways:
        y_copy(0, way, 0).start()
    for way in ways:
        y_copy(1, way, 0).start()
        y_copy(0, way, 1).start()

    loads[1].wait()
    qgather = LineGather(lambda s: qbuf.at[s], group, member, qg_send, qg_recv)
    qgather.own()
    for load in loads[2:]:
        load.start()
    loads[0].wait()

    for which in (0, 1):
        for way in ways:
            y_copy(0, way, which).wait_recv()

            @pl.loop(0, half)
            def _(row):
                mine = gown[way * half + row, at_y(steps[way], sides[which])]
                passed = yfar[way, which, row]
                yadd[way, which, row] = (mine.astype(F32) + passed.astype(F32)).astype(BF16)

            y_copy(2, way, which).start()
        if which == 0:
            for way in ways:
                y_copy(1, way, 1).start()
    qgather.hop(1)

    def y_total(part, which, row):
        return (
            gown[part * half + row, at_y(0, sides[which])].astype(F32)
            + ymix[part, which, row].astype(F32)
            + ynear[1 - part, which, row].astype(F32)
        )

    for part in ways:
        y_copy(2, part, 0).wait_recv()
        y_copy(1, 1 - part, 0).wait_recv()

        @pl.loop(0, half)
        def _(row):
            xout[part, row] = y_total(part, 0, row).astype(BF16)

        x_copy(0, part).start()
    for route in ways:
        x_copy(0, route).wait_recv()
        x_copy(1, route).start()
    qgather.hop(2)

    for part in ways:
        y_copy(2, part, 1).wait_recv()
        y_copy(1, 1 - part, 1).wait_recv()
        x_copy(1, part).wait_recv()

        @pl.loop(0, half)
        def _(row):
            total = y_total(part, 1, row) + xland[part, row].astype(F32)
            place = pl.ds(pl.multiple_of((part * half + row) * groups, groups), groups)
            for lane in range(width // 128):
                fsum[lane, place, :] = total[:, lane * 128 : (lane + 1) * 128]

    for block in range(groups):
        for lane in range(width // 128):
            summed[block, :, lane * 128 : (lane + 1) * 128] = fsum[
                lane, pl.ds(block, row_count, stride=groups), :
            ].astype(BF16)

    def spread_copy(across, ahead):
        to_quarter = (quarter + ahead) % 4
        to_xl = (xl + across) % 2
        slot = (chip - 4 * ahead) % 16
        if ahead == 0:
            entry = chip
        elif ahead == 1:
            entry = 0
        elif ahead == 3:
            entry = 3
        else:
            entry = jnp.where(chip <= 1, 3, 0)
        return remote(
            summed.at[to_xl * 4 + to_quarter],
            gbuf.at[xl, slot, core],
            sp_send.at[across, ahead],
            gg_recv.at[slot],
            blk=((to_xl * 4 + to_quarter) * 4 + entry) * 2 + core,
        )

    spreads = [spread_copy(across, ahead) for ahead in (2, 1, 3, 0) for across in (1, 0)]
    for spread in spreads[:-1]:
        spread.start()
    pltpu.make_async_copy(summed.at[group], gbuf.at[xl, chip, core], gg_recv.at[chip]).start()

    def pass_copy(slot, way):
        view = gbuf.at[:, slot, core]
        if way == 2:
            return remote(view, view, sib_send, sib_recv, blk=group * GROUP + chip * 2 + 1 - core)
        target = member + 2 if way == 0 else member - 2
        return remote(
            view, view, gg_send.at[way, slot], gg_recv.at[slot], blk=group * GROUP + target
        )

    def wait_slot(slot):
        view = gbuf.at[:, slot, core]
        pltpu.make_async_copy(view, view, gg_recv.at[slot]).wait()

    qgather.hop(3)

    wait_slot(chip)
    pl.when(chip < 3)(lambda: pass_copy(chip, 0).start())
    pl.when(chip > 0)(lambda: pass_copy(chip, 1).start())
    pass_copy(chip, 2).start()

    def passing(action):
        for step in range(1, 10):
            from_left = (chip - step + 16) % 16
            from_right = chip + step
            pl.when(step <= chip + 6)(functools.partial(action, from_left, 0, chip < 3))
            pl.when(step <= 9 - chip)(functools.partial(action, from_right, 1, chip > 0))

    def forward(slot, way, more):
        wait_slot(slot)
        pl.when(more)(lambda: pass_copy(slot, way).start())
        pass_copy(slot, 2).start()

    def sent(slot, way, more):
        pl.when(more)(lambda: pass_copy(slot, way).wait_send())

    passing(forward)
    qgather.finish()
    sibling = gbuf.at[:, :, 1 - core]
    pltpu.make_async_copy(sibling, sibling, sib_recv).wait()

    for load in loads[4:]:
        load.wait()
    left_factor = proot[...]

    @pl.loop(0, tiles)
    def _(step):
        cols = pl.ds(pl.multiple_of(step * tile, tile), tile)
        grad = gbuf[:, :, :, :, cols].reshape(width, tile)
        lapp[:, cols] = jnp.dot(left_factor, grad, preferred_element_type=F32).astype(BF16)

    my_rows = pl.ds((member % 4 - quarter + 4) % 4 * 4, 4)
    rows = gbuf[member // 4, my_rows].reshape(slab, width)
    wide = rows.astype(F32)
    squares[member, 0:8] = jnp.sum(
        (wide * wide).reshape(slab // 8, 8, width // 128, 128), axis=(0, 2)
    )
    squares[member, 8:16] = jnp.zeros((8, 128), F32)
    applied = lapp[...]

    @pl.loop(0, tiles)
    def _(step):
        cols = pl.ds(pl.multiple_of(step * tile, tile), tile)
        part = jnp.dot(
            applied, qbuf[:, :, cols].reshape(width, tile), preferred_element_type=F32
        )
        flipped = part.T
        uflip[cols, :] = flipped
        squares[member, 8:16] += jnp.sum(
            (flipped * flipped).reshape(tile // 8, 8, slab), axis=0
        )

    def square_copy(off):
        to = (member + off) % GROUP
        return remote(
            squares.at[member],
            squares.at[member],
            sq_send.at[off],
            sq_recv.at[off],
            blk=group * GROUP + to,
        )

    for off in range(1, GROUP):
        square_copy(off).start()

    loads[2].wait()

    @pl.loop(0, tiles)
    def _(step):
        first, slots = step // 2, pl.ds(step % 2 * 8, 8)
        other = gbuf[first, slots].reshape(tile, width)
        gram = lax.dot_general(
            rows, other, (((1,), (1,)), ((), ())), preferred_element_type=F32
        )
        for side in range(2):
            natural = first * 4 + (step % 2 * 2 + side + quarter) % 4
            cols = pl.ds(pl.multiple_of(natural * 128, 128), 128)
            lstat[:, cols] = (
                STAT_DECAY * lstat[:, cols]
                + (1.0 - STAT_DECAY) * gram[:, side * 128 : (side + 1) * 128]
            )

    store_left = pltpu.make_async_copy(lstat, newl_ref, out_sem.at[0])
    store_left.start()

    for off in range(1, GROUP):
        square_copy(off).wait_recv()
    total = jnp.sum(squares[...], axis=0)
    grad_square = jnp.sum(total[0:8], keepdims=True)
    update_square = jnp.sum(total[8:16], keepdims=True)
    scale = jnp.sqrt((grad_square + GRAFT_EPS) / (update_square + GRAFT_EPS))
    usend[...] = (uflip[...] * scale).astype(BF16).reshape(usend.shape)

    def update_copy(off):
        to = (b + off) % owners
        return remote(usend.at[to], uland.at[group, member], up_send, up_recv, blk=to)

    @pl.loop(1, owners)
    def _(off):
        update_copy(off).start()

    pltpu.make_async_copy(usend.at[b], uland.at[group, member], up_recv).start()

    loads[3].wait()
    first = pl.ds(pl.multiple_of(member * slab, slab), slab)
    columns = gbuf[:, :, :, :, first].reshape(width, slab).T

    @pl.loop(0, tiles)
    def _(step):
        cols = pl.ds(pl.multiple_of(step * tile, tile), tile)
        grad = gbuf[:, :, :, :, cols].reshape(width, tile)
        gram = jnp.dot(columns, grad, preferred_element_type=F32)
        rstat[:, cols] = STAT_DECAY * rstat[:, cols] + (1.0 - STAT_DECAY) * gram

    store_right = pltpu.make_async_copy(rstat, newr_ref, out_sem.at[1])
    store_right.start()

    for kind in range(3):
        for way in ways:
            for which in (0, 1):
                y_copy(kind, way, which).wait_send()
    for route in ways:
        x_copy(0, route).wait_send()
        x_copy(1, route).wait_send()
    qgather.drain()
    for spread in spreads[:-1]:
        spread.wait_send()
    pl.when(chip < 3)(lambda: pass_copy(chip, 0).wait_send())
    pl.when(chip > 0)(lambda: pass_copy(chip, 1).wait_send())
    passing(sent)
    lane = gbuf.at[:, :, core]
    pltpu.make_async_copy(lane, lane, sib_send).wait()
    for off in range(1, GROUP):
        square_copy(off).wait_send()

    pltpu.make_async_copy(uland, uland, up_recv).wait()
    for block in range(groups):
        for part in range(GROUP):
            ubuf[block, :, part * slab : (part + 1) * slab] = uland[block, part]
    store_update = pltpu.make_async_copy(ubuf, update_ref, out_sem.at[2])
    store_update.start()
    others = usend.at[pl.ds(0, owners - 1)]
    pltpu.make_async_copy(others, others, up_send).wait()
    store_left.wait()
    store_right.wait()
    store_update.wait()


def on_device(replicas, owners, gradients, left_stat, right_stat, left_root, right_root):
    _, row_count, block_count, width = gradients.shape
    local = block_count // replicas
    slab = width // GROUP
    part = width // owners
    groups = owners // GROUP
    dma = pltpu.SemaphoreType.DMA
    update, new_left, new_right = pl.pallas_call(
        functools.partial(kernel, replicas, owners),
        out_shape=(
            jax.ShapeDtypeStruct((local, part, width), BF16),
            jax.ShapeDtypeStruct((slab, width), F32),
            jax.ShapeDtypeStruct((slab, width), F32),
        ),
        in_specs=[pl.BlockSpec(memory_space=pl.ANY)] * 5,
        out_specs=[pl.BlockSpec(memory_space=pl.ANY)] * 3,
        scratch_shapes=[
            pltpu.VMEM((row_count, replicas, local, width), BF16),
            *[pltpu.VMEM((2, 2, row_count // 2, local, width), BF16)] * 4,
            *[pltpu.VMEM((2, row_count // 2, local, width), BF16)] * 3,
            pltpu.VMEM((width // 128, row_count * local, 128), F32),
            pltpu.VMEM((local, row_count, width), BF16),
            pltpu.VMEM((2, 16, 2, row_count, width), BF16),
            pltpu.VMEM((GROUP, slab, width), BF16),
            pltpu.VMEM((slab, width), BF16),
            pltpu.VMEM((slab, width), F32),
            pltpu.VMEM((slab, width), F32),
            pltpu.VMEM((slab, width), BF16),
            pltpu.VMEM((width, slab), F32),
            pltpu.VMEM((owners, part, slab), BF16),
            pltpu.VMEM((groups, GROUP, part, slab), BF16),
            pltpu.VMEM((GROUP, 16, 128), F32),
            pltpu.VMEM((local, part, width), BF16),
            dma((4,)),
            dma((GROUP,)),
            dma((3, 2, 2)),
            dma((3, 2, 2)),
            dma((2, 2)),
            dma((2, 2)),
            dma((GROUP, 3)),
            dma((GROUP,)),
            dma((2, 4)),
            dma((2, 16)),
            dma((16,)),
            dma,
            dma,
            dma((GROUP,)),
            dma((GROUP,)),
            dma,
            dma,
            dma((3,)),
        ],
        compiler_params=pltpu.CompilerParams(
            collective_id=0, has_side_effects=True, vmem_limit_bytes=60 * 2**20
        ),
        cost_estimate=pl.CostEstimate(
            flops=8 * slab * width * width, bytes_accessed=8 * 2**20, transcendentals=0
        ),
    )(
        gradients.reshape(row_count, replicas, local, width),
        left_stat[0],
        right_stat[0],
        left_root[0],
        right_root[0],
    )
    return jnp.swapaxes(update, 1, 2), new_left[None], new_right[None]


def solution(mesh):
    specs = (P("dp", "blk", None, None),) + (P(("dp", "blk"), None, None),) * 4
    out_specs = (P("dp", None, "blk"), P(("dp", "blk"), None, None), P(("dp", "blk"), None, None))
    return jax.shard_map(
        functools.partial(on_device, mesh.shape["dp"], mesh.shape["blk"]),
        mesh=mesh,
        in_specs=specs,
        out_specs=out_specs,
        check_vma=False,
    )
```

```python
import functools

import jax
import jax.numpy as jnp
from jax import lax
from jax.experimental import pallas as pl
from jax.experimental.pallas import tpu as pltpu
from jax.sharding import PartitionSpec as P

GROUP = 8
STAT_DECAY = 0.95
GRAFT_EPS = 1e-06
MESH = pl.DeviceIdType.MESH
F32 = jnp.float32
BF16 = jnp.bfloat16


def remote(src, dst, send, recv, **where):
    return pltpu.make_async_remote_copy(
        src_ref=src,
        dst_ref=dst,
        send_sem=send,
        recv_sem=recv,
        device_id=where,
        device_id_type=MESH,
    )


class LineGather:
    def __init__(self, view, group, member, send, recv):
        self.view, self.group, self.member = view, group, member
        self.send, self.recv = send, recv
        self.chip, self.core = member // 2, member % 2

    def copy(self, slot, target, way):
        return remote(
            self.view(slot),
            self.view(slot),
            self.send.at[slot, way],
            self.recv.at[slot],
            blk=self.group * GROUP + target,
        )

    def to_right(self, slot):
        return self.copy(slot, self.member + 2, 0)

    def to_left(self, slot):
        return self.copy(slot, self.member - 2, 1)

    def to_sibling(self, slot):
        return self.copy(slot, self.chip * 2 + 1 - self.core, 2)

    def own(self):
        slot = self.member
        pl.when(self.chip < 3)(lambda: self.to_right(slot).start())
        pl.when(self.chip > 0)(lambda: self.to_left(slot).start())
        self.to_sibling(slot).start()

    def hop(self, hop):
        left, right = self.member - 2 * hop, self.member + 2 * hop

        @pl.when(self.chip >= hop)
        def _():
            self.to_right(left).wait_recv()
            pl.when(self.chip < 3)(lambda: self.to_right(left).start())
            self.to_sibling(left).start()

        @pl.when(self.chip + hop <= 3)
        def _():
            self.to_left(right).wait_recv()
            pl.when(self.chip > 0)(lambda: self.to_left(right).start())
            self.to_sibling(right).start()

    def finish(self):
        for other in range(4):
            self.to_sibling(other * 2 + 1 - self.core).wait_recv()

    def drain(self):
        chip = self.chip
        pl.when(chip < 3)(lambda: self.to_right(self.member).wait_send())
        pl.when(chip > 0)(lambda: self.to_left(self.member).wait_send())
        self.to_sibling(self.member).wait_send()
        for hop in range(1, 4):
            left, right = self.member - 2 * hop, self.member + 2 * hop

            @pl.when(chip >= hop)
            def _():
                pl.when(chip < 3)(lambda: self.to_right(left).wait_send())
                self.to_sibling(left).wait_send()

            @pl.when(chip + hop <= 3)
            def _():
                pl.when(chip > 0)(lambda: self.to_left(right).wait_send())
                self.to_sibling(right).wait_send()


def meet(peers):
    barrier = pltpu.get_barrier_semaphore()
    for peer in peers:
        pl.semaphore_signal(barrier, inc=1, device_id=peer, device_id_type=MESH)
    pl.semaphore_wait(barrier, len(peers))


def sum_kernel(
    replicas,
    owners,
    grad_ref,
    rroot_ref,
    summed_ref,
    qbuf,
    gown,
    yfar,
    ynear,
    ymix,
    yadd,
    xout,
    xpass,
    xland,
    fsum,
    summed,
    local_sem,
    y_send,
    y_recv,
    x_send,
    x_recv,
    qg_send,
    qg_recv,
):
    p = lax.axis_index("dp")
    b = lax.axis_index("blk")
    groups = owners // GROUP
    group, member = b // GROUP, b % GROUP
    chip, core = member // 2, member % 2
    y, xh = p // 2, p % 2
    xl, quarter = group // 4, group % 4
    row_count, width = grad_ref.shape[0], grad_ref.shape[3]
    half = row_count // 2
    loads = [
        pltpu.make_async_copy(grad_ref, gown, local_sem.at[0]),
        pltpu.make_async_copy(rroot_ref, qbuf.at[member], local_sem.at[1]),
    ]
    for load in loads:
        load.start()

    flip = (b + owners // 2) % owners
    turn = y * 2 + 1 - xh
    near_a = {"dp": p, "blk": flip}
    near_b = {"dp": turn, "blk": flip}

    def at_y(step, which):
        return ((y + step) % 4) * 2 + which

    mates = [{"blk": group * GROUP + (member + off) % GROUP} for off in range(1, GROUP)]
    meet([{"dp": at_y(1, xh)}, {"dp": at_y(3, xh)}, {"blk": flip}, near_b] + mates)

    sides = (1 - xh, xh)
    steps = (1, 3)

    def rows_of(way):
        return pl.ds(way * half, half)

    def y_copy(kind, way, which):
        to = at_y(steps[way], xh)
        if kind == 0:
            src = grad_ref.at[rows_of(way), at_y(2, sides[which])]
            dst = yfar.at[way, which]
        elif kind == 1:
            src = grad_ref.at[rows_of(1 - way), at_y(steps[way], sides[which])]
            dst = ynear.at[way, which]
        else:
            src = yadd.at[way, which]
            dst = ymix.at[way, which]
        return remote(
            src, dst, y_send.at[kind, way, which], y_recv.at[kind, way, which], dp=to
        )

    def x_copy(stage, route):
        if stage == 0:
            where = (near_a, near_b)[route]
            src, dst = xout.at[route], xpass.at[route]
        else:
            where = (near_b, near_a)[route]
            src, dst = xpass.at[route], xland.at[route]
        return remote(src, dst, x_send.at[stage, route], x_recv.at[stage, route], **where)

    ways = (0, 1)
    for way in ways:
        y_copy(0, way, 0).start()
    for way in ways:
        y_copy(1, way, 0).start()
        y_copy(0, way, 1).start()

    loads[1].wait()
    qgather = LineGather(lambda s: qbuf.at[s], group, member, qg_send, qg_recv)
    qgather.own()
    loads[0].wait()

    for which in (0, 1):
        for way in ways:
            y_copy(0, way, which).wait_recv()

            @pl.loop(0, half)
            def _(row):
                mine = gown[way * half + row, at_y(steps[way], sides[which])]
                passed = yfar[way, which, row]
                yadd[way, which, row] = (mine.astype(F32) + passed.astype(F32)).astype(BF16)

            y_copy(2, way, which).start()
        if which == 0:
            for way in ways:
                y_copy(1, way, 1).start()
    qgather.hop(1)

    def y_total(part, which, row):
        return (
            gown[part * half + row, at_y(0, sides[which])].astype(F32)
            + ymix[part, which, row].astype(F32)
            + ynear[1 - part, which, row].astype(F32)
        )

    for part in ways:
        y_copy(2, part, 0).wait_recv()
        y_copy(1, 1 - part, 0).wait_recv()

        @pl.loop(0, half)
        def _(row):
            xout[part, row] = y_total(part, 0, row).astype(BF16)

        x_copy(0, part).start()
    for route in ways:
        x_copy(0, route).wait_recv()
        x_copy(1, route).start()
    qgather.hop(2)

    for part in ways:
        y_copy(2, part, 1).wait_recv()
        y_copy(1, 1 - part, 1).wait_recv()
        x_copy(1, part).wait_recv()

        @pl.loop(0, half)
        def _(row):
            total = y_total(part, 1, row) + xland[part, row].astype(F32)
            place = pl.ds(pl.multiple_of((part * half + row) * groups, groups), groups)
            for lane in range(width // 128):
                fsum[lane, place, :] = total[:, lane * 128 : (lane + 1) * 128]

    for block in range(groups):
        for lane in range(width // 128):
            summed[block, :, lane * 128 : (lane + 1) * 128] = fsum[
                lane, pl.ds(block, row_count, stride=groups), :
            ].astype(BF16)

    qgather.hop(3)
    store = pltpu.make_async_copy(summed, summed_ref, local_sem.at[2])
    store.start()
    qgather.finish()
    for kind in range(3):
        for way in ways:
            for which in (0, 1):
                y_copy(kind, way, which).wait_send()
    for route in ways:
        x_copy(0, route).wait_send()
        x_copy(1, route).wait_send()
    qgather.drain()
    store.wait()


def gather_kernel(
    replicas, owners, summed, gbuf, sp_send, gg_send, gg_recv, sib_send, sib_recv
):
    p = lax.axis_index("dp")
    b = lax.axis_index("blk")
    groups = owners // GROUP
    group, member = b // GROUP, b % GROUP
    chip, core = member // 2, member % 2
    y, xh = p // 2, p % 2
    xl, quarter = group // 4, group % 4

    meet([{"blk": (b + off) % owners} for off in range(1, owners)])

    def spread_copy(across, ahead):
        to_quarter = (quarter + ahead) % 4
        to_xl = (xl + across) % 2
        slot = (chip - 4 * ahead) % 16
        if ahead == 0:
            entry = chip
        elif ahead == 1:
            entry = 0
        elif ahead == 3:
            entry = 3
        else:
            entry = jnp.where(chip <= 1, 3, 0)
        return remote(
            summed.at[to_xl * 4 + to_quarter],
            gbuf.at[xl, slot, core],
            sp_send.at[across, ahead],
            gg_recv.at[slot],
            blk=((to_xl * 4 + to_quarter) * 4 + entry) * 2 + core,
        )

    spreads = [spread_copy(across, ahead) for ahead in (2, 1, 3, 0) for across in (1, 0)]
    for spread in spreads[:-1]:
        spread.start()
    pltpu.make_async_copy(summed.at[group], gbuf.at[xl, chip, core], gg_recv.at[chip]).start()

    def pass_copy(slot, way):
        view = gbuf.at[:, slot, core]
        if way == 2:
            return remote(view, view, sib_send, sib_recv, blk=group * GROUP + chip * 2 + 1 - core)
        target = member + 2 if way == 0 else member - 2
        return remote(
            view, view, gg_send.at[way, slot], gg_recv.at[slot], blk=group * GROUP + target
        )

    def wait_slot(slot):
        view = gbuf.at[:, slot, core]
        pltpu.make_async_copy(view, view, gg_recv.at[slot]).wait()

    wait_slot(chip)
    pl.when(chip < 3)(lambda: pass_copy(chip, 0).start())
    pl.when(chip > 0)(lambda: pass_copy(chip, 1).start())
    pass_copy(chip, 2).start()

    def passing(action):
        for step in range(1, 10):
            from_left = (chip - step + 16) % 16
            from_right = chip + step
            pl.when(step <= chip + 6)(functools.partial(action, from_left, 0, chip < 3))
            pl.when(step <= 9 - chip)(functools.partial(action, from_right, 1, chip > 0))

    def forward(slot, way, more):
        wait_slot(slot)
        pl.when(more)(lambda: pass_copy(slot, way).start())
        pass_copy(slot, 2).start()

    def sent(slot, way, more):
        pl.when(more)(lambda: pass_copy(slot, way).wait_send())

    passing(forward)
    sibling = gbuf.at[:, :, 1 - core]
    pltpu.make_async_copy(sibling, sibling, sib_recv).wait()
    for spread in spreads[:-1]:
        spread.wait_send()
    pl.when(chip < 3)(lambda: pass_copy(chip, 0).wait_send())
    pl.when(chip > 0)(lambda: pass_copy(chip, 1).wait_send())
    passing(sent)
    lane = gbuf.at[:, :, core]
    pltpu.make_async_copy(lane, lane, sib_send).wait()


def compute_kernel(
    owners,
    gbuf,
    qbuf,
    lroot_ref,
    left_ref,
    right_ref,
    newl_ref,
    newr_ref,
    uflip,
    squares,
    proot,
    lapp,
):
    b = lax.axis_index("blk")
    group, member = b // GROUP, b % GROUP
    quarter = group % 4
    width = gbuf.shape[4]
    slab = width // GROUP
    tile = 256
    tiles = width // tile
    for block in range(GROUP):
        natural = (block // 4) * 4 + (block % 4 + quarter) % 4
        cols = pl.ds(pl.multiple_of(natural * 128, 128), 128)
        proot[:, block * 128 : (block + 1) * 128] = lroot_ref[:, cols]
    left_factor = proot[...]

    @pl.loop(0, tiles)
    def _(step):
        cols = pl.ds(pl.multiple_of(step * tile, tile), tile)
        grad = gbuf[:, :, :, :, cols].reshape(width, tile)
        lapp[:, cols] = jnp.dot(left_factor, grad, preferred_element_type=F32).astype(BF16)

    my_rows = pl.ds((member % 4 - quarter + 4) % 4 * 4, 4)
    rows = gbuf[member // 4, my_rows].reshape(slab, width)
    wide = rows.astype(F32)
    squares[0:8] = jnp.sum(
        (wide * wide).reshape(slab // 8, 8, width // 128, 128), axis=(0, 2)
    )
    squares[8:16] = jnp.zeros((8, 128), F32)
    applied = lapp[...]

    @pl.loop(0, tiles)
    def _(step):
        cols = pl.ds(pl.multiple_of(step * tile, tile), tile)
        part = jnp.dot(
            applied, qbuf[:, :, cols].reshape(width, tile), preferred_element_type=F32
        )
        flipped = part.T
        uflip[cols, :] = flipped
        squares[8:16] += jnp.sum(
            (flipped * flipped).reshape(tile // 8, 8, slab), axis=0
        )

    @pl.loop(0, tiles)
    def _(step):
        first, slots = step // 2, pl.ds(step % 2 * 8, 8)
        other = gbuf[first, slots].reshape(tile, width)
        gram = lax.dot_general(
            rows, other, (((1,), (1,)), ((), ())), preferred_element_type=F32
        )
        for side in range(2):
            natural = first * 4 + (step % 2 * 2 + side + quarter) % 4
            cols = pl.ds(pl.multiple_of(natural * 128, 128), 128)
            newl_ref[:, cols] = (
                STAT_DECAY * left_ref[:, cols]
                + (1.0 - STAT_DECAY) * gram[:, side * 128 : (side + 1) * 128]
            )

    first = pl.ds(pl.multiple_of(member * slab, slab), slab)
    columns = gbuf[:, :, :, :, first].reshape(width, slab).T

    @pl.loop(0, tiles)
    def _(step):
        cols = pl.ds(pl.multiple_of(step * tile, tile), tile)
        grad = gbuf[:, :, :, :, cols].reshape(width, tile)
        gram = jnp.dot(columns, grad, preferred_element_type=F32)
        newr_ref[:, cols] = STAT_DECAY * right_ref[:, cols] + (1.0 - STAT_DECAY) * gram


def update_kernel(
    owners,
    uflip,
    square_ref,
    update_ref,
    squares,
    usend,
    uland,
    ubuf,
    sq_send,
    sq_recv,
    up_send,
    up_recv,
    out_sem,
):
    b = lax.axis_index("blk")
    groups = owners // GROUP
    group, member = b // GROUP, b % GROUP
    slab = usend.shape[2]
    meet([{"blk": (b + off) % owners} for off in range(1, owners)])

    squares[member] = square_ref[...]

    def square_copy(off):
        to = (member + off) % GROUP
        return remote(
            squares.at[member],
            squares.at[member],
            sq_send.at[off],
            sq_recv.at[off],
            blk=group * GROUP + to,
        )

    for off in range(1, GROUP):
        square_copy(off).start()

    for off in range(1, GROUP):
        square_copy(off).wait_recv()
    total = jnp.sum(squares[...], axis=0)
    grad_square = jnp.sum(total[0:8], keepdims=True)
    update_square = jnp.sum(total[8:16], keepdims=True)
    scale = jnp.sqrt((grad_square + GRAFT_EPS) / (update_square + GRAFT_EPS))
    usend[...] = (uflip[...] * scale).astype(BF16).reshape(usend.shape)

    def update_copy(off):
        to = (b + off) % owners
        return remote(usend.at[to], uland.at[group, member], up_send, up_recv, blk=to)

    @pl.loop(1, owners)
    def _(off):
        update_copy(off).start()

    pltpu.make_async_copy(usend.at[b], uland.at[group, member], up_recv).start()

    pltpu.make_async_copy(uland, uland, up_recv).wait()
    for block in range(groups):
        for part in range(GROUP):
            ubuf[block, :, part * slab : (part + 1) * slab] = uland[block, part]
    store_update = pltpu.make_async_copy(ubuf, update_ref, out_sem.at[2])
    store_update.start()
    others = usend.at[pl.ds(0, owners - 1)]
    pltpu.make_async_copy(others, others, up_send).wait()
    for off in range(1, GROUP):
        square_copy(off).wait_send()
    store_update.wait()


def on_device(replicas, owners, gradients, left_stat, right_stat, left_root, right_root):
    _, row_count, block_count, width = gradients.shape
    local = block_count // replicas
    slab = width // GROUP
    part = width // owners
    groups = owners // GROUP
    dma = pltpu.SemaphoreType.DMA
    anywhere = pl.BlockSpec(memory_space=pl.ANY)
    vmem = pl.BlockSpec(memory_space=pltpu.VMEM)
    struct = jax.ShapeDtypeStruct

    def params(number):
        return pltpu.CompilerParams(
            collective_id=number, has_side_effects=True, vmem_limit_bytes=24 * 2**20
        )

    summed, right_full = pl.pallas_call(
        functools.partial(sum_kernel, replicas, owners),
        out_shape=(
            struct((local, row_count, width), BF16),
            struct((GROUP, slab, width), BF16),
        ),
        in_specs=[anywhere] * 2,
        out_specs=[anywhere] * 2,
        scratch_shapes=[
            pltpu.VMEM((row_count, replicas, local, width), BF16),
            *[pltpu.VMEM((2, 2, row_count // 2, local, width), BF16)] * 4,
            *[pltpu.VMEM((2, row_count // 2, local, width), BF16)] * 3,
            pltpu.VMEM((width // 128, row_count * local, 128), F32),
            pltpu.VMEM((local, row_count, width), BF16),
            dma((3,)),
            dma((3, 2, 2)),
            dma((3, 2, 2)),
            dma((2, 2)),
            dma((2, 2)),
            dma((GROUP, 3)),
            dma((GROUP,)),
        ],
        compiler_params=params(0),
    )(gradients.reshape(row_count, replicas, local, width), right_root[0])

    whole = pl.pallas_call(
        functools.partial(gather_kernel, replicas, owners),
        out_shape=struct((2, 16, 2, row_count, width), BF16),
        in_specs=[anywhere],
        out_specs=anywhere,
        scratch_shapes=[dma((2, 4)), dma((2, 16)), dma((16,)), dma, dma],
        compiler_params=params(1),
    )(summed)

    new_left, new_right, uflip, square = pl.pallas_call(
        functools.partial(compute_kernel, owners),
        out_shape=(
            struct((slab, width), F32),
            struct((slab, width), F32),
            struct((width, slab), F32),
            struct((16, 128), F32),
        ),
        in_specs=[vmem] * 5,
        out_specs=[vmem] * 4,
        scratch_shapes=[pltpu.VMEM((slab, width), BF16)] * 2,
        compiler_params=pltpu.CompilerParams(vmem_limit_bytes=24 * 2**20),
    )(whole, right_full, left_root[0], left_stat[0], right_stat[0])

    update = pl.pallas_call(
        functools.partial(update_kernel, owners),
        out_shape=struct((local, part, width), BF16),
        in_specs=[vmem] * 2,
        out_specs=anywhere,
        scratch_shapes=[
            pltpu.VMEM((GROUP, 16, 128), F32),
            pltpu.VMEM((owners, part, slab), BF16),
            pltpu.VMEM((groups, GROUP, part, slab), BF16),
            pltpu.VMEM((local, part, width), BF16),
            dma((GROUP,)),
            dma((GROUP,)),
            dma,
            dma,
            dma((3,)),
        ],
        compiler_params=params(2),
    )(uflip, square)
    return jnp.swapaxes(update, 1, 2), new_left[None], new_right[None]


def solution(mesh):
    specs = (P("dp", "blk", None, None),) + (P(("dp", "blk"), None, None),) * 4
    out_specs = (P("dp", None, "blk"), P(("dp", "blk"), None, None), P(("dp", "blk"), None, None))
    return jax.shard_map(
        functools.partial(on_device, mesh.shape["dp"], mesh.shape["blk"]),
        mesh=mesh,
        in_specs=specs,
        out_specs=out_specs,
        check_vma=False,
    )
```

```python
import functools

import jax
import jax.numpy as jnp
from jax import lax
from jax.experimental import pallas as pl
from jax.experimental.pallas import tpu as pltpu
from jax.sharding import PartitionSpec as P

GROUP = 8
STAT_DECAY = 0.95
GRAFT_EPS = 1e-06
MESH = pl.DeviceIdType.MESH
F32 = jnp.float32
BF16 = jnp.bfloat16


def remote(src, dst, send, recv, **where):
    return pltpu.make_async_remote_copy(
        src_ref=src,
        dst_ref=dst,
        send_sem=send,
        recv_sem=recv,
        device_id=where,
        device_id_type=MESH,
    )


class LineGather:
    def __init__(self, view, group, member, send, recv):
        self.view, self.group, self.member = view, group, member
        self.send, self.recv = send, recv
        self.chip, self.core = member // 2, member % 2

    def copy(self, slot, target, way):
        return remote(
            self.view(slot),
            self.view(slot),
            self.send.at[slot, way],
            self.recv.at[slot],
            blk=self.group * GROUP + target,
        )

    def to_right(self, slot):
        return self.copy(slot, self.member + 2, 0)

    def to_left(self, slot):
        return self.copy(slot, self.member - 2, 1)

    def to_sibling(self, slot):
        return self.copy(slot, self.chip * 2 + 1 - self.core, 2)

    def own(self):
        slot = self.member
        pl.when(self.chip < 3)(lambda: self.to_right(slot).start())
        pl.when(self.chip > 0)(lambda: self.to_left(slot).start())
        self.to_sibling(slot).start()

    def hop(self, hop):
        left, right = self.member - 2 * hop, self.member + 2 * hop

        @pl.when(self.chip >= hop)
        def _():
            self.to_right(left).wait_recv()
            pl.when(self.chip < 3)(lambda: self.to_right(left).start())
            self.to_sibling(left).start()

        @pl.when(self.chip + hop <= 3)
        def _():
            self.to_left(right).wait_recv()
            pl.when(self.chip > 0)(lambda: self.to_left(right).start())
            self.to_sibling(right).start()

    def finish(self):
        for other in range(4):
            self.to_sibling(other * 2 + 1 - self.core).wait_recv()

    def drain(self):
        chip = self.chip
        pl.when(chip < 3)(lambda: self.to_right(self.member).wait_send())
        pl.when(chip > 0)(lambda: self.to_left(self.member).wait_send())
        self.to_sibling(self.member).wait_send()
        for hop in range(1, 4):
            left, right = self.member - 2 * hop, self.member + 2 * hop

            @pl.when(chip >= hop)
            def _():
                pl.when(chip < 3)(lambda: self.to_right(left).wait_send())
                self.to_sibling(left).wait_send()

            @pl.when(chip + hop <= 3)
            def _():
                pl.when(chip > 0)(lambda: self.to_left(right).wait_send())
                self.to_sibling(right).wait_send()


def kernel(
    replicas,
    owners,
    grad_ref,
    left_ref,
    right_ref,
    lroot_ref,
    rroot_ref,
    update_ref,
    newl_ref,
    newr_ref,
    gown,
    yfar,
    ynear,
    ymix,
    yadd,
    xout,
    xpass,
    xland,
    fsum,
    summed,
    gbuf,
    qbuf,
    proot,
    lstat,
    rstat,
    lacc,
    lapp,
    usend,
    uland,
    squares,
    scales,
    ubuf,
    local_sem,
    root_sem,
    y_send,
    y_recv,
    x_send,
    x_recv,
    qg_send,
    qg_recv,
    sp_send,
    gg_send,
    gg_recv,
    sib_send,
    sib_recv,
    sq_send,
    sq_recv,
    sc_send,
    sc_recv,
    up_send,
    up_recv,
    out_sem,
):
    p = lax.axis_index("dp")
    b = lax.axis_index("blk")
    groups = owners // GROUP
    group, member = b // GROUP, b % GROUP
    chip, core = member // 2, member % 2
    y, xh = p // 2, p % 2
    xl, quarter = group // 4, group % 4
    row_count, width = grad_ref.shape[0], grad_ref.shape[3]
    half = row_count // 2
    slab = width // GROUP
    tile = 256
    tiles = width // tile

    loads = [
        pltpu.make_async_copy(grad_ref, gown, local_sem.at[0]),
        pltpu.make_async_copy(rroot_ref, qbuf.at[member], local_sem.at[1]),
        pltpu.make_async_copy(left_ref, lstat, local_sem.at[2]),
        pltpu.make_async_copy(right_ref, rstat, local_sem.at[3]),
    ]
    for block in range(GROUP):
        natural = (block % 2) * 4 + (block // 2 + quarter) % 4
        loads.append(
            pltpu.make_async_copy(
                lroot_ref.at[:, pl.ds(pl.multiple_of(natural * 128, 128), 128)],
                proot.at[:, pl.ds(block * 128, 128)],
                root_sem.at[block],
            )
        )
    loads[0].start()
    loads[1].start()

    flip = (b + owners // 2) % owners
    turn = y * 2 + 1 - xh
    near_a = {"dp": p, "blk": flip}
    near_b = {"dp": turn, "blk": flip}

    def at_y(step, which):
        return ((y + step) % 4) * 2 + which

    barrier = pltpu.get_barrier_semaphore()
    for peer in ({"dp": at_y(1, xh)}, {"dp": at_y(3, xh)}, near_b):
        pl.semaphore_signal(barrier, inc=1, device_id=peer, device_id_type=MESH)

    @pl.loop(1, owners)
    def _(off):
        pl.semaphore_signal(
            barrier, inc=1, device_id={"blk": (b + off) % owners}, device_id_type=MESH
        )

    pl.semaphore_wait(barrier, 3 + owners - 1)

    sides = (1 - xh, xh)
    steps = (1, 3)

    def rows_of(way):
        return pl.ds(way * half, half)

    def y_copy(kind, way, which):
        to = at_y(steps[way], xh)
        if kind == 0:
            src = grad_ref.at[rows_of(way), at_y(2, sides[which])]
            dst = yfar.at[way, which]
        elif kind == 1:
            src = grad_ref.at[rows_of(1 - way), at_y(steps[way], sides[which])]
            dst = ynear.at[way, which]
        else:
            src = yadd.at[way, which]
            dst = ymix.at[way, which]
        return remote(
            src, dst, y_send.at[kind, way, which], y_recv.at[kind, way, which], dp=to
        )

    def x_copy(stage, route):
        if stage == 0:
            where = (near_a, near_b)[route]
            src, dst = xout.at[route], xpass.at[route]
        else:
            where = (near_b, near_a)[route]
            src, dst = xpass.at[route], xland.at[route]
        return remote(src, dst, x_send.at[stage, route], x_recv.at[stage, route], **where)

    ways = (0, 1)
    for way in ways:
        y_copy(0, way, 0).start()
    for way in ways:
        y_copy(1, way, 0).start()
        y_copy(0, way, 1).start()

    loads[1].wait()
    qgather = LineGather(lambda s: qbuf.at[s], group, member, qg_send, qg_recv)
    qgather.own()
    for load in loads[2:]:
        load.start()
    loads[0].wait()

    for which in (0, 1):
        for way in ways:
            y_copy(0, way, which).wait_recv()

            @pl.loop(0, half)
            def _(row):
                mine = gown[way * half + row, at_y(steps[way], sides[which])]
                passed = yfar[way, which, row]
                yadd[way, which, row] = (mine.astype(F32) + passed.astype(F32)).astype(BF16)

            y_copy(2, way, which).start()
        if which == 0:
            for way in ways:
                y_copy(1, way, 1).start()
    qgather.hop(1)

    def y_total(part, which, row):
        return (
            gown[part * half + row, at_y(0, sides[which])].astype(F32)
            + ymix[part, which, row].astype(F32)
            + ynear[1 - part, which, row].astype(F32)
        )

    for part in ways:
        y_copy(2, part, 0).wait_recv()
        y_copy(1, 1 - part, 0).wait_recv()

        @pl.loop(0, half)
        def _(row):
            xout[part, row] = y_total(part, 0, row).astype(BF16)

        x_copy(0, part).start()
    for route in ways:
        x_copy(0, route).wait_recv()
        x_copy(1, route).start()
    qgather.hop(2)

    for part in ways:
        y_copy(2, part, 1).wait_recv()
        y_copy(1, 1 - part, 1).wait_recv()
        x_copy(1, part).wait_recv()

        @pl.loop(0, half)
        def _(row):
            total = y_total(part, 1, row) + xland[part, row].astype(F32)
            place = pl.ds(pl.multiple_of((part * half + row) * groups, groups), groups)
            for lane in range(width // 128):
                fsum[lane, place, :] = total[:, lane * 128 : (lane + 1) * 128]

    for block in range(groups):
        for lane in range(width // 128):
            summed[block, :, lane * 128 : (lane + 1) * 128] = fsum[
                lane, pl.ds(block, row_count, stride=groups), :
            ].astype(BF16)

    def spread_copy(across, ahead):
        to_quarter = (quarter + ahead) % 4
        to_xl = (xl + across) % 2
        slot = (chip - 4 * ahead) % 16
        if ahead == 0:
            entry = chip
        elif ahead == 1:
            entry = 0
        elif ahead == 3:
            entry = 3
        else:
            entry = jnp.where(chip <= 1, 3, 0)
        return remote(
            summed.at[to_xl * 4 + to_quarter],
            gbuf.at[slot // 4, xl, slot % 4, core],
            sp_send.at[across, ahead],
            gg_recv.at[slot],
            blk=((to_xl * 4 + to_quarter) * 4 + entry) * 2 + core,
        )

    def slot_view(slot, which=core):
        return gbuf.at[slot // 4, :, slot % 4, which]

    spreads = [spread_copy(1, 0)]
    spreads += [spread_copy(across, ahead) for ahead in (2, 1, 3) for across in (1, 0)]
    for spread in spreads:
        spread.start()
    own_slot = gbuf.at[0, xl, chip, core]
    pltpu.make_async_copy(summed.at[group], own_slot, gg_recv.at[chip]).start()

    def pass_copy(slot, way):
        view = slot_view(slot)
        if way == 2:
            return remote(view, view, sib_send.at[slot], sib_recv.at[slot], blk=group * GROUP + chip * 2 + 1 - core)
        target = member + 2 if way == 0 else member - 2
        return remote(
            view, view, gg_send.at[way, slot], gg_recv.at[slot], blk=group * GROUP + target
        )

    def wait_slot(slot):
        view = slot_view(slot)
        pltpu.make_async_copy(view, view, gg_recv.at[slot]).wait()

    qgather.hop(3)

    wait_slot(chip)
    pl.when(chip < 3)(lambda: pass_copy(chip, 0).start())
    pl.when(chip > 0)(lambda: pass_copy(chip, 1).start())
    pass_copy(chip, 2).start()

    def passing(action, between=None):
        for step in range(1, 10):
            from_left = (chip - step + 16) % 16
            from_right = chip + step
            pl.when(step <= chip + 6)(functools.partial(action, from_left, 0, chip < 3))
            pl.when(step <= 9 - chip)(functools.partial(action, from_right, 1, chip > 0))
            if between is not None:
                between(step)

    def forward(slot, way, more):
        wait_slot(slot)
        pl.when(more)(lambda: pass_copy(slot, way).start())
        pass_copy(slot, 2).start()

    def sent(slot, way, more):
        pl.when(more)(lambda: pass_copy(slot, way).wait_send())

    def apply_quad(quad, first):
        for slot in range(quad * 4, quad * 4 + 4):
            view = slot_view(slot, 1 - core)
            pltpu.make_async_copy(view, view, sib_recv.at[slot]).wait()
        factor = proot[:, quad * 256 : (quad + 1) * 256]

        @pl.loop(0, tiles)
        def _(step):
            cols = pl.ds(pl.multiple_of(step * tile, tile), tile)
            grad = gbuf[quad, :, :, :, :, cols].reshape(256, tile)
            part = jnp.dot(factor, grad, preferred_element_type=F32)
            if not first:
                part = part + lacc[:, cols]
            if quad == 2:
                lapp[:, cols] = part.astype(BF16)
            else:
                lacc[:, cols] = part

    def compute(step):
        if step == 4:
            for load in loads[4:]:
                load.wait()
            apply_quad(0, True)
        elif step == 7:
            apply_quad(1, False)
        elif step == 8:
            apply_quad(3, False)

    passing(forward, compute)
    qgather.finish()
    apply_quad(2, False)

    applied = lapp[...]
    squares[member] = jnp.zeros((16, 128), F32)
    per_tile = owners // tiles

    def update_copy(to):
        return remote(usend.at[to], uland.at[group, member], up_send, up_recv, blk=to)

    mine = pltpu.make_async_copy(usend.at[b], uland.at[group, member], up_recv)
    for turn_tile in (1, 2, 3, 0):
        number = (b // per_tile + turn_tile) % tiles
        cols = pl.ds(pl.multiple_of(number * tile, tile), tile)
        part = jnp.dot(
            applied, qbuf[:, :, cols].reshape(width, tile), preferred_element_type=F32
        )
        flipped = part.T
        usend[pl.ds(number * per_tile, per_tile)] = flipped.astype(BF16).reshape(
            per_tile, tile // per_tile, slab
        )
        squares[member, 8:16] += jnp.sum(
            (flipped * flipped).reshape(tile // 8, 8, slab), axis=0
        )
        if turn_tile == 0:
            mine.start()

        @pl.loop(1 if turn_tile == 0 else 0, per_tile)
        def _(off):
            update_copy(number * per_tile + (b + off) % per_tile).start()

    my_quad = (member % 4 - quarter + 4) % 4
    rows = gbuf[my_quad, member // 4].reshape(slab, width)
    wide = rows.astype(F32)
    squares[member, 0:8] = jnp.sum(
        (wide * wide).reshape(slab // 8, 8, width // 128, 128), axis=(0, 2)
    )

    def square_copy(off):
        to = (member + off) % GROUP
        return remote(
            squares.at[member],
            squares.at[member],
            sq_send.at[off],
            sq_recv.at[off],
            blk=group * GROUP + to,
        )

    for off in range(1, GROUP):
        square_copy(off).start()

    loads[2].wait()

    @pl.loop(0, tiles)
    def _(step):
        other = gbuf[step].reshape(tile, width)
        gram = lax.dot_general(
            rows, other, (((1,), (1,)), ((), ())), preferred_element_type=F32
        )
        for side in range(2):
            natural = side * 4 + (step + quarter) % 4
            cols = pl.ds(pl.multiple_of(natural * 128, 128), 128)
            lstat[:, cols] = (
                STAT_DECAY * lstat[:, cols]
                + (1.0 - STAT_DECAY) * gram[:, side * 128 : (side + 1) * 128]
            )

    store_left = pltpu.make_async_copy(lstat, newl_ref, out_sem.at[0])
    store_left.start()

    for off in range(1, GROUP):
        square_copy(off).wait_recv()
    total = jnp.sum(squares[...], axis=0)
    grad_square = jnp.sum(total[0:8], keepdims=True)
    update_square = jnp.sum(total[8:16], keepdims=True)
    scale = jnp.sqrt((grad_square + GRAFT_EPS) / (update_square + GRAFT_EPS))
    scales[group] = jnp.broadcast_to(scale, (8, 128))

    def scale_copy(off):
        to = (group + off) % groups
        return remote(
            scales.at[group],
            scales.at[group],
            sc_send.at[off],
            sc_recv.at[off],
            blk=to * GROUP + member,
        )

    for off in range(1, groups):
        scale_copy(off).start()

    loads[3].wait()
    first = pl.ds(pl.multiple_of(member * slab, slab), slab)
    columns = gbuf[:, :, :, :, :, first].reshape(width, slab).T

    @pl.loop(0, tiles)
    def _(step):
        cols = pl.ds(pl.multiple_of(step * tile, tile), tile)
        grad = gbuf[:, :, :, :, :, cols].reshape(width, tile)
        gram = jnp.dot(columns, grad, preferred_element_type=F32)
        rstat[:, cols] = STAT_DECAY * rstat[:, cols] + (1.0 - STAT_DECAY) * gram

    store_right = pltpu.make_async_copy(rstat, newr_ref, out_sem.at[1])
    store_right.start()

    for kind in range(3):
        for way in ways:
            for which in (0, 1):
                y_copy(kind, way, which).wait_send()
    for route in ways:
        x_copy(0, route).wait_send()
        x_copy(1, route).wait_send()
    qgather.drain()
    for spread in spreads:
        spread.wait_send()
    pl.when(chip < 3)(lambda: pass_copy(chip, 0).wait_send())
    pl.when(chip > 0)(lambda: pass_copy(chip, 1).wait_send())
    passing(sent)
    for slot in range(16):
        pass_copy(slot, 2).wait_send()
    for off in range(1, GROUP):
        square_copy(off).wait_send()
    for off in range(1, groups):
        scale_copy(off).wait_send()
        scale_copy(off).wait_recv()

    pltpu.make_async_copy(uland, uland, up_recv).wait()
    for block in range(groups):
        factor = scales[block, 0:1]
        for part in range(GROUP):
            ubuf[block, :, part * slab : (part + 1) * slab] = (
                uland[block, part].astype(F32) * factor
            ).astype(BF16)
    store_update = pltpu.make_async_copy(ubuf, update_ref, out_sem.at[2])
    store_update.start()
    others = usend.at[pl.ds(0, owners - 1)]
    pltpu.make_async_copy(others, others, up_send).wait()
    store_left.wait()
    store_right.wait()
    store_update.wait()


def on_device(replicas, owners, gradients, left_stat, right_stat, left_root, right_root):
    _, row_count, block_count, width = gradients.shape
    local = block_count // replicas
    slab = width // GROUP
    part = width // owners
    groups = owners // GROUP
    dma = pltpu.SemaphoreType.DMA
    update, new_left, new_right = pl.pallas_call(
        functools.partial(kernel, replicas, owners),
        out_shape=(
            jax.ShapeDtypeStruct((local, part, width), BF16),
            jax.ShapeDtypeStruct((slab, width), F32),
            jax.ShapeDtypeStruct((slab, width), F32),
        ),
        in_specs=[pl.BlockSpec(memory_space=pltpu.HBM)] * 5,
        out_specs=[pl.BlockSpec(memory_space=pl.ANY)] * 3,
        scratch_shapes=[
            pltpu.VMEM((row_count, replicas, local, width), BF16),
            *[pltpu.VMEM((2, 2, row_count // 2, local, width), BF16)] * 4,
            *[pltpu.VMEM((2, row_count // 2, local, width), BF16)] * 3,
            pltpu.VMEM((width // 128, row_count * local, 128), F32),
            pltpu.VMEM((local, row_count, width), BF16),
            pltpu.VMEM((4, 2, 4, 2, row_count, width), BF16),
            pltpu.VMEM((GROUP, slab, width), BF16),
            pltpu.VMEM((slab, width), BF16),
            pltpu.VMEM((slab, width), F32),
            pltpu.VMEM((slab, width), F32),
            pltpu.VMEM((slab, width), F32),
            pltpu.VMEM((slab, width), BF16),
            pltpu.VMEM((owners, part, slab), BF16),
            pltpu.VMEM((groups, GROUP, part, slab), BF16),
            pltpu.VMEM((GROUP, 16, 128), F32),
            pltpu.VMEM((groups, 8, 128), F32),
            pltpu.VMEM((local, part, width), BF16),
            dma((4,)),
            dma((GROUP,)),
            dma((3, 2, 2)),
            dma((3, 2, 2)),
            dma((2, 2)),
            dma((2, 2)),
            dma((GROUP, 3)),
            dma((GROUP,)),
            dma((2, 4)),
            dma((2, 16)),
            dma((16,)),
            dma((16,)),
            dma((16,)),
            dma((GROUP,)),
            dma((GROUP,)),
            dma((groups,)),
            dma((groups,)),
            dma,
            dma,
            dma((3,)),
        ],
        compiler_params=pltpu.CompilerParams(
            collective_id=0, has_side_effects=True, vmem_limit_bytes=40 * 2**20
        ),
        cost_estimate=pl.CostEstimate(
            flops=8 * slab * width * width, bytes_accessed=8 * 2**20, transcendentals=0
        ),
    )(
        *(
            pltpu.with_memory_space_constraint(x, pltpu.HBM)
            for x in (
                gradients.reshape(row_count, replicas, local, width),
                left_stat[0],
                right_stat[0],
                left_root[0],
                right_root[0],
            )
        )
    )
    return jnp.swapaxes(update, 1, 2), new_left[None], new_right[None]


def solution(mesh):
    specs = (P("dp", "blk", None, None),) + (P(("dp", "blk"), None, None),) * 4
    out_specs = (P("dp", None, "blk"), P(("dp", "blk"), None, None), P(("dp", "blk"), None, None))
    return jax.shard_map(
        functools.partial(on_device, mesh.shape["dp"], mesh.shape["blk"]),
        mesh=mesh,
        in_specs=specs,
        out_specs=out_specs,
        check_vma=False,
    )
```

```python
import functools

import jax
import jax.numpy as jnp
from jax import lax
from jax.experimental import pallas as pl
from jax.experimental.pallas import tpu as pltpu
from jax.sharding import PartitionSpec as P

GROUP = 8
STAT_DECAY = 0.95
GRAFT_EPS = 1e-06
MESH = pl.DeviceIdType.MESH
F32 = jnp.float32
BF16 = jnp.bfloat16


def remote(src, dst, send, recv, **where):
    return pltpu.make_async_remote_copy(
        src_ref=src,
        dst_ref=dst,
        send_sem=send,
        recv_sem=recv,
        device_id=where,
        device_id_type=MESH,
    )


class LineGather:
    def __init__(self, view, first, chip, send, recv):
        self.view, self.first, self.chip = view, first, chip
        self.send, self.recv = send, recv

    def copy(self, slot, way):
        target = self.chip + (1 if way == 0 else -1)
        return remote(
            self.view(slot),
            self.view(slot),
            self.send.at[slot, way],
            self.recv.at[slot],
            blk=self.first + 2 * target,
        )

    def own(self):
        pl.when(self.chip < 3)(lambda: self.copy(self.chip, 0).start())
        pl.when(self.chip > 0)(lambda: self.copy(self.chip, 1).start())

    def hop(self, hop):
        left, right = self.chip - hop, self.chip + hop

        @pl.when(left >= 0)
        def _():
            self.copy(left, 0).wait_recv()
            pl.when(self.chip < 3)(lambda: self.copy(left, 0).start())

        @pl.when(right <= 3)
        def _():
            self.copy(right, 1).wait_recv()
            pl.when(self.chip > 0)(lambda: self.copy(right, 1).start())

    def drain(self):
        chip = self.chip
        pl.when(chip < 3)(lambda: self.copy(chip, 0).wait_send())
        pl.when(chip > 0)(lambda: self.copy(chip, 1).wait_send())
        for hop in range(1, 4):
            left, right = chip - hop, chip + hop
            pl.when((left >= 0) & (chip < 3))(lambda: self.copy(left, 0).wait_send())
            pl.when((right <= 3) & (chip > 0))(lambda: self.copy(right, 1).wait_send())


def kernel(
    replicas,
    owners,
    grad_ref,
    left_ref,
    right_ref,
    lroot_ref,
    rroot_ref,
    update_ref,
    newl_ref,
    newr_ref,
    gown,
    yfar,
    ynear,
    ymix,
    yadd,
    xout,
    xpass,
    xland,
    fsum,
    summed,
    gbuf,
    qbuf,
    proot,
    lstat,
    rstat,
    lacc,
    lapp,
    usend,
    uland,
    squares,
    scales,
    ubuf,
    local_sem,
    root_sem,
    y_send,
    y_recv,
    x_send,
    x_recv,
    pair_send,
    pair_recv,
    qg_send,
    qg_recv,
    sp_send,
    gg_send,
    gg_recv,
    sib_send,
    sib_recv,
    sq_send,
    sq_recv,
    sc_send,
    sc_recv,
    up_send,
    up_recv,
    out_sem,
):
    p = lax.axis_index("dp")
    b = lax.axis_index("blk")
    groups = owners // GROUP
    group, member = b // GROUP, b % GROUP
    chip, core = member // 2, member % 2
    y, xh = p // 2, p % 2
    xl, quarter = group // 4, group % 4
    row_count, width = grad_ref.shape[0], grad_ref.shape[3]
    half = row_count // 2
    slab = width // GROUP
    tile = 256
    tiles = width // tile

    pair = group * GROUP + chip * 2
    sibling = pair + 1 - core

    def half_of(which):
        return pl.ds(pl.multiple_of(which * (width // 2), width // 2), width // 2)

    def part_of(which):
        return pl.ds(pl.multiple_of(which * slab, slab), slab)

    loads = [
        pltpu.make_async_copy(grad_ref, gown, local_sem.at[0]),
        pltpu.make_async_copy(
            rroot_ref.at[:, half_of(core)], qbuf.at[chip, part_of(core)], local_sem.at[1]
        ),
        pltpu.make_async_copy(left_ref, lstat, local_sem.at[2]),
        pltpu.make_async_copy(right_ref, rstat, local_sem.at[3]),
    ]
    for block in range(GROUP):
        natural = (block % 2) * 4 + (block // 2 + quarter) % 4
        loads.append(
            pltpu.make_async_copy(
                lroot_ref.at[:, pl.ds(pl.multiple_of(natural * 128, 128), 128)],
                proot.at[part_of(core), pl.ds(block * 128, 128)],
                root_sem.at[block],
            )
        )
    for load in loads:
        load.start()

    flip = (b + owners // 2) % owners
    turn = y * 2 + 1 - xh
    near_a = {"dp": p, "blk": flip}
    near_b = {"dp": turn, "blk": flip}

    def at_y(step, which):
        return ((y + step) % 4) * 2 + which

    barrier = pltpu.get_barrier_semaphore()
    for peer in ({"dp": at_y(1, xh)}, {"dp": at_y(3, xh)}, near_b):
        pl.semaphore_signal(barrier, inc=1, device_id=peer, device_id_type=MESH)

    @pl.loop(1, owners)
    def _(off):
        pl.semaphore_signal(
            barrier, inc=1, device_id={"blk": (b + off) % owners}, device_id_type=MESH
        )

    pl.semaphore_wait(barrier, 3 + owners - 1)

    sides = (1 - xh, xh)
    steps = (1, 3)

    def rows_of(way):
        return pl.ds(way * half, half)

    def y_copy(kind, way, which):
        to = at_y(steps[way], xh)
        if kind == 0:
            src = grad_ref.at[rows_of(way), at_y(2, sides[which])]
            dst = yfar.at[way, which]
        elif kind == 1:
            src = grad_ref.at[rows_of(1 - way), at_y(steps[way], sides[which])]
            dst = ynear.at[way, which]
        else:
            src = yadd.at[way, which]
            dst = ymix.at[way, which]
        return remote(
            src, dst, y_send.at[kind, way, which], y_recv.at[kind, way, which], dp=to
        )

    def x_copy(stage, route):
        if stage == 0:
            where = (near_a, near_b)[route]
            src, dst = xout.at[route], xpass.at[route]
        else:
            where = (near_b, near_a)[route]
            src, dst = xpass.at[route], xland.at[route]
        return remote(src, dst, x_send.at[stage, route], x_recv.at[stage, route], **where)

    ways = (0, 1)
    for which in (0, 1):
        for way in ways:
            y_copy(0, way, which).start()

    root_swap = remote(
        rroot_ref.at[:, half_of(1 - core)],
        qbuf.at[chip, part_of(core)],
        pair_send.at[0],
        pair_recv.at[0],
        blk=sibling,
    )
    root_swap.start()
    for load in loads[4:]:
        load.wait()
    factor_swap = remote(
        proot.at[part_of(core)],
        proot.at[part_of(core)],
        pair_send.at[1],
        pair_recv.at[1],
        blk=sibling,
    )
    factor_swap.start()
    loads[1].wait()
    root_swap.wait_recv()
    qgather = LineGather(
        lambda s: qbuf.at[s], group * GROUP + core, chip, qg_send, qg_recv
    )
    qgather.own()
    loads[0].wait()

    def y_add(way, which):
        y_copy(0, way, which).wait_recv()

        @pl.loop(0, half)
        def _(row):
            mine = gown[way * half + row, at_y(steps[way], sides[which])]
            passed = yfar[way, which, row]
            yadd[way, which, row] = (mine.astype(F32) + passed.astype(F32)).astype(BF16)

    for way in ways:
        y_add(way, 0)
        y_copy(2, way, 0).start()
    for way in ways:
        y_copy(1, way, 0).start()
    for way in ways:
        y_add(way, 1)

    def y_total(part, which, row):
        return (
            gown[part * half + row, at_y(0, sides[which])].astype(F32)
            + ymix[part, which, row].astype(F32)
            + ynear[1 - part, which, row].astype(F32)
        )

    for part in ways:
        y_copy(2, part, 0).wait_recv()
        y_copy(1, 1 - part, 0).wait_recv()

        @pl.loop(0, half)
        def _(row):
            xout[part, row] = y_total(part, 0, row).astype(BF16)

        x_copy(0, part).start()
    for kind in (2, 1):
        for way in ways:
            y_copy(kind, way, 1).start()
    qgather.hop(1)
    for route in ways:
        x_copy(0, route).wait_recv()
        x_copy(1, route).start()
    qgather.hop(2)

    for part in ways:
        y_copy(2, part, 1).wait_recv()
        y_copy(1, 1 - part, 1).wait_recv()
        x_copy(1, part).wait_recv()

        @pl.loop(0, half)
        def _(row):
            total = y_total(part, 1, row) + xland[part, row].astype(F32)
            place = pl.ds(pl.multiple_of((part * half + row) * groups, groups), groups)
            for lane in range(width // 128):
                fsum[lane, place, :] = total[:, lane * 128 : (lane + 1) * 128]

    for block in range(groups):
        for lane in range(width // 128):
            summed[block, :, lane * 128 : (lane + 1) * 128] = fsum[
                lane, pl.ds(block, row_count, stride=groups), :
            ].astype(BF16)

    def spread_copy(across, ahead):
        to_quarter = (quarter + ahead) % 4
        to_xl = (xl + across) % 2
        slot = (chip - 4 * ahead) % 16
        if ahead == 0:
            entry = chip
        elif ahead == 1:
            entry = 0
        elif ahead == 3:
            entry = 3
        else:
            entry = jnp.where(chip <= 1, 3, 0)
        return remote(
            summed.at[to_xl * 4 + to_quarter],
            gbuf.at[slot // 4, xl, slot % 4, core],
            sp_send.at[across, ahead],
            gg_recv.at[slot],
            blk=((to_xl * 4 + to_quarter) * 4 + entry) * 2 + core,
        )

    def slot_view(slot, which=core):
        return gbuf.at[slot // 4, :, slot % 4, which]

    reach = {1: 4 - chip, 3: chip + 1, 2: jnp.where((chip == 1) | (chip == 2), 6, 5)}

    def spread_to(distance, action):
        for ahead, lowest, highest in ((1, 1, 4), (3, 1, 4), (2, 5, 6)):
            if lowest <= distance <= highest:

                @pl.when(reach[ahead] == distance)
                def _():
                    for across in (0, 1):
                        action(spread_copy(across, ahead))

    spread_copy(1, 0).start()
    spread_to(1, lambda copy: copy.start())
    spread_to(2, lambda copy: copy.start())
    own_slot = gbuf.at[0, xl, chip, core]
    pltpu.make_async_copy(summed.at[group], own_slot, gg_recv.at[chip]).start()

    def pass_copy(slot, way):
        view = slot_view(slot)
        target = member + 2 if way == 0 else member - 2
        return remote(
            view, view, gg_send.at[way, slot], gg_recv.at[slot], blk=group * GROUP + target
        )

    def cross_slot(slot):
        view = slot_view(slot)
        return remote(view, view, sib_send.at[slot], sib_recv.at[slot], blk=sibling)

    def cross_quad(quad):
        view = gbuf.at[quad, :, :, core]
        return remote(view, view, sib_send.at[quad], sib_recv.at[quad], blk=sibling)

    def wait_slot(slot):
        view = slot_view(slot)
        pltpu.make_async_copy(view, view, gg_recv.at[slot]).wait()

    wait_slot(chip)
    pl.when(chip < 3)(lambda: pass_copy(chip, 0).start())
    pl.when(chip > 0)(lambda: pass_copy(chip, 1).start())

    def passing(action, between=None):
        for step in range(1, 10):
            from_left = (chip - step + 16) % 16
            from_right = chip + step
            pl.when(step <= chip + 6)(functools.partial(action, from_left, 0, chip < 3))
            pl.when(step <= 9 - chip)(functools.partial(action, from_right, 1, chip > 0))
            if between is not None:
                between(step)

    def forward(slot, way, more):
        wait_slot(slot)
        pl.when(more)(lambda: pass_copy(slot, way).start())
        pl.when(slot // 4 == 2)(lambda: cross_slot(slot).start())

    def sent(slot, way, more):
        pl.when(more)(lambda: pass_copy(slot, way).wait_send())

    def apply_quad(quad, first):
        if quad == 2:
            for slot in range(8, 12):
                view = slot_view(slot, 1 - core)
                pltpu.make_async_copy(view, view, sib_recv.at[slot]).wait()
        else:
            view = gbuf.at[quad, :, :, 1 - core]
            pltpu.make_async_copy(view, view, sib_recv.at[quad]).wait()
        factor = proot[:, quad * 256 : (quad + 1) * 256]

        @pl.loop(0, tiles)
        def _(step):
            cols = pl.ds(pl.multiple_of(step * tile, tile), tile)
            grad = gbuf[quad, :, :, :, :, cols].reshape(256, tile)
            part = jnp.dot(factor, grad, preferred_element_type=F32)
            if not first:
                part = part + lacc[:, cols]
            if quad == 2:
                lapp[:, cols] = part.astype(BF16)
            else:
                lacc[:, cols] = part

    def compute(step):
        if step <= 4:
            spread_to(step + 2, lambda copy: copy.start())
        if step == 3:
            cross_quad(0).start()
        elif step == 5:
            factor_swap.wait_recv()
            apply_quad(0, True)
        elif step == 7:
            cross_quad(1).start()
            cross_quad(3).start()
        elif step == 9:
            apply_quad(1, False)
            apply_quad(3, False)

    passing(forward, compute)
    apply_quad(2, False)
    qgather.hop(3)

    applied = lapp[...]
    squares[member] = jnp.zeros((16, 128), F32)
    ends = owners // 2
    per_tile = ends // 2

    def update_copy(end):
        return remote(
            usend.at[end], uland.at[group, chip], up_send, up_recv, blk=core * ends + end
        )

    mine = pltpu.make_async_copy(usend.at[b % ends], uland.at[group, chip], up_recv)
    for turn_tile in (1, 0):
        number = (b % ends // per_tile + turn_tile) % 2
        cols = pl.ds(pl.multiple_of(number * tile, tile), tile)
        part = jnp.dot(
            applied, qbuf[:, :, cols].reshape(width, tile), preferred_element_type=F32
        )
        flipped = part.T
        usend[pl.ds(number * per_tile, per_tile)] = flipped.astype(BF16).reshape(
            per_tile, tile // per_tile, 2 * slab
        )
        squares[member, 8:16] += jnp.sum(
            (flipped * flipped).reshape(tile // 8, 8, 2, slab), axis=(0, 2)
        )
        if turn_tile == 0:
            pl.when(xl == core)(lambda: mine.start())
            pl.when(xl != core)(lambda: update_copy(b % ends).start())

        @pl.loop(1 if turn_tile == 0 else 0, per_tile)
        def _(off):
            update_copy(number * per_tile + (b + off) % per_tile).start()

    my_quad = (member % 4 - quarter + 4) % 4
    rows = gbuf[my_quad, member // 4].reshape(slab, width)
    wide = rows.astype(F32)
    squares[member, 0:8] = jnp.sum(
        (wide * wide).reshape(slab // 8, 8, width // 128, 128), axis=(0, 2)
    )

    def square_copy(off):
        to = (member + off) % GROUP
        return remote(
            squares.at[member],
            squares.at[member],
            sq_send.at[off],
            sq_recv.at[off],
            blk=group * GROUP + to,
        )

    for off in range(1, GROUP):
        square_copy(off).start()

    loads[2].wait()

    @pl.loop(0, tiles)
    def _(step):
        other = gbuf[step].reshape(tile, width)
        gram = lax.dot_general(
            rows, other, (((1,), (1,)), ((), ())), preferred_element_type=F32
        )
        for side in range(2):
            natural = side * 4 + (step + quarter) % 4
            cols = pl.ds(pl.multiple_of(natural * 128, 128), 128)
            lstat[:, cols] = (
                STAT_DECAY * lstat[:, cols]
                + (1.0 - STAT_DECAY) * gram[:, side * 128 : (side + 1) * 128]
            )

    store_left = pltpu.make_async_copy(lstat, newl_ref, out_sem.at[0])
    store_left.start()

    for off in range(1, GROUP):
        square_copy(off).wait_recv()
    total = jnp.sum(squares[...], axis=0)
    grad_square = jnp.sum(total[0:8], keepdims=True)
    update_square = jnp.sum(total[8:16], keepdims=True)
    scale = jnp.sqrt((grad_square + GRAFT_EPS) / (update_square + GRAFT_EPS))
    scales[group] = jnp.broadcast_to(scale, (8, 128))

    def scale_copy(off):
        to = (group + off) % groups
        return remote(
            scales.at[group],
            scales.at[group],
            sc_send.at[off],
            sc_recv.at[off],
            blk=to * GROUP + member,
        )

    for off in range(1, groups):
        scale_copy(off).start()

    loads[3].wait()
    first = pl.ds(pl.multiple_of(member * slab, slab), slab)
    columns = gbuf[:, :, :, :, :, first].reshape(width, slab).T

    @pl.loop(0, tiles)
    def _(step):
        cols = pl.ds(pl.multiple_of(step * tile, tile), tile)
        grad = gbuf[:, :, :, :, :, cols].reshape(width, tile)
        gram = jnp.dot(columns, grad, preferred_element_type=F32)
        rstat[:, cols] = STAT_DECAY * rstat[:, cols] + (1.0 - STAT_DECAY) * gram

    store_right = pltpu.make_async_copy(rstat, newr_ref, out_sem.at[1])
    store_right.start()

    for kind in range(3):
        for way in ways:
            for which in (0, 1):
                y_copy(kind, way, which).wait_send()
    for route in ways:
        x_copy(0, route).wait_send()
        x_copy(1, route).wait_send()
    qgather.drain()
    root_swap.wait_send()
    factor_swap.wait_send()
    spread_copy(1, 0).wait_send()
    for distance in range(1, 7):
        spread_to(distance, lambda copy: copy.wait_send())
    pl.when(chip < 3)(lambda: pass_copy(chip, 0).wait_send())
    pl.when(chip > 0)(lambda: pass_copy(chip, 1).wait_send())
    passing(sent)
    for quad in (0, 1, 3):
        cross_quad(quad).wait_send()
    for slot in range(8, 12):
        cross_slot(slot).wait_send()
    for off in range(1, GROUP):
        square_copy(off).wait_send()
    for off in range(1, groups):
        scale_copy(off).wait_send()
        scale_copy(off).wait_recv()

    pltpu.make_async_copy(uland, uland, up_recv).wait()
    for block in range(groups):
        factor = scales[block, 0:1]
        for part in range(GROUP):
            piece = uland[block, part // 2, :, part % 2 * slab : (part % 2 + 1) * slab]
            ubuf[block, :, part * slab : (part + 1) * slab] = (
                piece.astype(F32) * factor
            ).astype(BF16)
    store_update = pltpu.make_async_copy(ubuf, update_ref, out_sem.at[2])
    store_update.start()
    others = usend.at[pl.ds(0, ends - 1)]
    pl.when(xl == core)(lambda: pltpu.make_async_copy(others, others, up_send).wait())
    pl.when(xl != core)(lambda: pltpu.make_async_copy(usend, usend, up_send).wait())
    store_left.wait()
    store_right.wait()
    store_update.wait()


def on_device(replicas, owners, gradients, left_stat, right_stat, left_root, right_root):
    _, row_count, block_count, width = gradients.shape
    local = block_count // replicas
    slab = width // GROUP
    part = width // owners
    groups = owners // GROUP
    dma = pltpu.SemaphoreType.DMA
    update, new_left, new_right = pl.pallas_call(
        functools.partial(kernel, replicas, owners),
        out_shape=(
            jax.ShapeDtypeStruct((local, part, width), BF16),
            jax.ShapeDtypeStruct((slab, width), F32),
            jax.ShapeDtypeStruct((slab, width), F32),
        ),
        in_specs=[pl.BlockSpec(memory_space=pltpu.HBM)] * 5,
        out_specs=[pl.BlockSpec(memory_space=pl.ANY)] * 3,
        scratch_shapes=[
            pltpu.VMEM((row_count, replicas, local, width), BF16),
            *[pltpu.VMEM((2, 2, row_count // 2, local, width), BF16)] * 4,
            *[pltpu.VMEM((2, row_count // 2, local, width), BF16)] * 3,
            pltpu.VMEM((width // 128, row_count * local, 128), F32),
            pltpu.VMEM((local, row_count, width), BF16),
            pltpu.VMEM((4, 2, 4, 2, row_count, width), BF16),
            pltpu.VMEM((4, 2 * slab, width // 2), BF16),
            pltpu.VMEM((2 * slab, width), BF16),
            pltpu.VMEM((slab, width), F32),
            pltpu.VMEM((slab, width), F32),
            pltpu.VMEM((2 * slab, width), F32),
            pltpu.VMEM((2 * slab, width), BF16),
            pltpu.VMEM((owners // 2, part, 2 * slab), BF16),
            pltpu.VMEM((groups, 4, part, 2 * slab), BF16),
            pltpu.VMEM((GROUP, 16, 128), F32),
            pltpu.VMEM((groups, 8, 128), F32),
            pltpu.VMEM((local, part, width), BF16),
            dma((4,)),
            dma((GROUP,)),
            dma((3, 2, 2)),
            dma((3, 2, 2)),
            dma((2, 2)),
            dma((2, 2)),
            dma((2,)),
            dma((2,)),
            dma((4, 2)),
            dma((4,)),
            dma((2, 4)),
            dma((2, 16)),
            dma((16,)),
            dma((16,)),
            dma((16,)),
            dma((GROUP,)),
            dma((GROUP,)),
            dma((groups,)),
            dma((groups,)),
            dma,
            dma,
            dma((3,)),
        ],
        compiler_params=pltpu.CompilerParams(
            collective_id=0, has_side_effects=True, vmem_limit_bytes=40 * 2**20
        ),
        cost_estimate=pl.CostEstimate(
            flops=8 * slab * width * width, bytes_accessed=8 * 2**20, transcendentals=0
        ),
    )(
        *(
            pltpu.with_memory_space_constraint(x, pltpu.HBM)
            for x in (
                gradients.reshape(row_count, replicas, local, width),
                left_stat[0],
                right_stat[0],
                left_root[0],
                right_root[0],
            )
        )
    )
    return jnp.swapaxes(update, 1, 2), new_left[None], new_right[None]


def solution(mesh):
    specs = (P("dp", "blk", None, None),) + (P(("dp", "blk"), None, None),) * 4
    out_specs = (P("dp", None, "blk"), P(("dp", "blk"), None, None), P(("dp", "blk"), None, None))
    return jax.shard_map(
        functools.partial(on_device, mesh.shape["dp"], mesh.shape["blk"]),
        mesh=mesh,
        in_specs=specs,
        out_specs=out_specs,
        check_vma=False,
    )
```

```python
import functools

import jax
import jax.numpy as jnp
from jax import lax
from jax.experimental import pallas as pl
from jax.experimental.pallas import tpu as pltpu
from jax.sharding import PartitionSpec as P

GROUP = 8
STAT_DECAY = 0.95
GRAFT_EPS = 1e-06
MESH = pl.DeviceIdType.MESH
F32 = jnp.float32
BF16 = jnp.bfloat16


def remote(src, dst, send, recv, **where):
    return pltpu.make_async_remote_copy(
        src_ref=src,
        dst_ref=dst,
        send_sem=send,
        recv_sem=recv,
        device_id=where,
        device_id_type=MESH,
    )


class LineGather:
    def __init__(self, view, first, chip, send, recv):
        self.view, self.first, self.chip = view, first, chip
        self.send, self.recv = send, recv

    def copy(self, slot, way):
        target = self.chip + (1 if way == 0 else -1)
        return remote(
            self.view(slot),
            self.view(slot),
            self.send.at[slot, way],
            self.recv.at[slot],
            blk=self.first + 2 * target,
        )

    def own(self):
        pl.when(self.chip < 3)(lambda: self.copy(self.chip, 0).start())
        pl.when(self.chip > 0)(lambda: self.copy(self.chip, 1).start())

    def hop(self, hop):
        left, right = self.chip - hop, self.chip + hop

        @pl.when(left >= 0)
        def _():
            self.copy(left, 0).wait_recv()
            pl.when(self.chip < 3)(lambda: self.copy(left, 0).start())

        @pl.when(right <= 3)
        def _():
            self.copy(right, 1).wait_recv()
            pl.when(self.chip > 0)(lambda: self.copy(right, 1).start())

    def drain(self):
        chip = self.chip
        pl.when(chip < 3)(lambda: self.copy(chip, 0).wait_send())
        pl.when(chip > 0)(lambda: self.copy(chip, 1).wait_send())
        for hop in range(1, 4):
            left, right = chip - hop, chip + hop
            pl.when((left >= 0) & (chip < 3))(lambda: self.copy(left, 0).wait_send())
            pl.when((right <= 3) & (chip > 0))(lambda: self.copy(right, 1).wait_send())


def kernel(
    replicas,
    owners,
    grad_ref,
    left_ref,
    right_ref,
    lroot_ref,
    rroot_ref,
    update_ref,
    newl_ref,
    newr_ref,
    land,
    fsum,
    summed,
    gbuf,
    qbuf,
    proot,
    lstat,
    rstat,
    lapp,
    usend,
    uland,
    squares,
    scales,
    ubuf,
    local_sem,
    own_sem,
    root_sem,
    rs_send,
    rs_recv,
    pair_send,
    pair_recv,
    qg_send,
    qg_recv,
    sp_send,
    gg_send,
    gg_recv,
    sib_send,
    sib_recv,
    sq_send,
    sq_recv,
    sc_send,
    sc_recv,
    up_send,
    up_recv,
    out_sem,
):
    p = lax.axis_index("dp")
    b = lax.axis_index("blk")
    groups = owners // GROUP
    group, member = b // GROUP, b % GROUP
    chip, core = member // 2, member % 2
    xl, quarter = group // 4, group % 4
    row_count, width = grad_ref.shape[0], grad_ref.shape[3]
    half = width // 2
    slab = width // GROUP
    tile = 256
    tiles = width // tile

    pair = group * GROUP + chip * 2
    sibling = pair + 1 - core

    def half_of(which):
        return pl.ds(pl.multiple_of(which * (width // 2), width // 2), width // 2)

    def part_of(which):
        return pl.ds(pl.multiple_of(which * slab, slab), slab)

    loads = [
        pltpu.make_async_copy(
            rroot_ref.at[:, half_of(core)], qbuf.at[chip, part_of(core)], local_sem.at[0]
        ),
        pltpu.make_async_copy(left_ref, lstat, local_sem.at[1]),
        pltpu.make_async_copy(right_ref, rstat, local_sem.at[2]),
    ]
    own_land = [
        pltpu.make_async_copy(
            grad_ref.at[:, p, :, pl.ds(part * half, half)], land.at[part, 0], own_sem.at[part]
        )
        for part in (0, 1)
    ]
    for block in range(GROUP):
        natural = (block % 2) * 4 + (block // 2 + quarter) % 4
        loads.append(
            pltpu.make_async_copy(
                lroot_ref.at[:, pl.ds(pl.multiple_of(natural * 128, 128), 128)],
                proot.at[part_of(core), pl.ds(block * 128, 128)],
                root_sem.at[block],
            )
        )
    for load in loads + own_land:
        load.start()

    barrier = pltpu.get_barrier_semaphore()
    for off in range(1, replicas):
        pl.semaphore_signal(
            barrier, inc=1, device_id={"dp": (p + off) % replicas}, device_id_type=MESH
        )

    @pl.loop(1, owners)
    def _(off):
        pl.semaphore_signal(
            barrier, inc=1, device_id={"blk": (b + off) % owners}, device_id_type=MESH
        )

    pl.semaphore_wait(barrier, replicas - 1 + owners - 1)

    def reduce_copy(part, off):
        to = (p + off) % replicas
        return remote(
            grad_ref.at[:, to, :, pl.ds(part * half, half)],
            land.at[part, off],
            rs_send.at[part, off],
            rs_recv.at[part, off],
            dp=to,
        )

    for off in range(1, replicas):
        reduce_copy(0, off).start()

    root_swap = remote(
        rroot_ref.at[:, half_of(1 - core)],
        qbuf.at[chip, part_of(core)],
        pair_send.at[0],
        pair_recv.at[0],
        blk=sibling,
    )
    root_swap.start()
    for load in loads[3:]:
        load.wait()
    factor_swap = remote(
        proot.at[part_of(core)],
        proot.at[part_of(core)],
        pair_send.at[1],
        pair_recv.at[1],
        blk=sibling,
    )
    factor_swap.start()
    loads[0].wait()
    root_swap.wait_recv()
    qgather = LineGather(
        lambda s: qbuf.at[s], group * GROUP + core, chip, qg_send, qg_recv
    )
    qgather.own()

    def sum_part(part):
        own_land[part].wait()

        @pl.loop(0, row_count)
        def _(row):
            total = land[part, 0, row].astype(F32)
            for off in range(1, replicas):
                total = total + land[part, off, row].astype(F32)
            place = pl.ds(pl.multiple_of(row * groups, groups), groups)
            for lane in range(half // 128):
                fsum[lane, place, :] = total[:, lane * 128 : (lane + 1) * 128]

        for block in range(groups):
            for lane in range(half // 128):
                summed[part, block, :, lane * 128 : (lane + 1) * 128] = fsum[
                    lane, pl.ds(block, row_count, stride=groups), :
                ].astype(BF16)

    for off in range(1, 5):
        reduce_copy(0, off).wait_recv()
    for off in range(1, replicas):
        reduce_copy(1, off).start()
    for off in range(5, replicas):
        reduce_copy(0, off).wait_recv()
    sum_part(0)

    def spread_copy(part, across, ahead):
        to_quarter = (quarter + ahead) % 4
        to_xl = (xl + across) % 2
        slot = (chip - 4 * ahead) % 16
        if ahead == 0:
            entry = chip
        elif ahead == 1:
            entry = 0
        elif ahead == 3:
            entry = 3
        else:
            entry = jnp.where(chip <= 1, 3, 0)
        return remote(
            summed.at[part, to_xl * 4 + to_quarter],
            gbuf.at[part, slot // 4, xl, slot % 4, core],
            sp_send.at[part, across, ahead],
            gg_recv.at[part, slot],
            blk=((to_xl * 4 + to_quarter) * 4 + entry) * 2 + core,
        )

    def slot_view(part, slot):
        return gbuf.at[part, slot // 4, :, slot % 4, core]

    spread_order = [(1, 0)] + [(across, ahead) for ahead in (1, 3, 2) for across in (1, 0)]

    def spread_part(part):
        for across, ahead in spread_order:
            spread_copy(part, across, ahead).start()
        pltpu.make_async_copy(
            summed.at[part, group], gbuf.at[part, 0, xl, chip, core], gg_recv.at[part, chip]
        ).start()

    def pass_copy(part, slot, way):
        view = slot_view(part, slot)
        target = member + 2 if way == 0 else member - 2
        return remote(
            view,
            view,
            gg_send.at[part, way, slot],
            gg_recv.at[part, slot],
            blk=group * GROUP + target,
        )

    def cross_quad(part, quad):
        view = gbuf.at[part, quad, :, :, core]
        return remote(
            view, view, sib_send.at[part, quad], sib_recv.at[part, quad], blk=sibling
        )

    def wait_slot(part, slot):
        view = slot_view(part, slot)
        pltpu.make_async_copy(view, view, gg_recv.at[part, slot]).wait()

    def at_step(step, action):
        if step == 0:
            action(chip, 0, chip < 3, False)
            action(chip, 1, chip > 0, False)
            return
        from_left = (chip - step + 16) % 16
        from_right = chip + step
        pl.when(step <= chip + 6)(lambda: action(from_left, 0, chip < 3, True))
        pl.when(step <= 9 - chip)(lambda: action(from_right, 1, chip > 0, True))

    def hand_on(part, step):
        def forward(slot, way, more, arrives):
            if arrives:
                wait_slot(part, slot)
            pl.when(more)(lambda: pass_copy(part, slot, way).start())

        if step == 0:
            wait_slot(part, chip)
        at_step(step, forward)
        if step == 3:
            cross_quad(part, 0).start()
        elif step == 7:
            cross_quad(part, 1).start()
            cross_quad(part, 3).start()
        elif step == 9:
            cross_quad(part, 2).start()

    def handed_on(part, step):
        def sent(slot, way, more, arrives):
            pl.when(more)(lambda: pass_copy(part, slot, way).wait_send())

        at_step(step, sent)

    def apply_part(part):
        for quad in range(4):
            view = gbuf.at[part, quad, :, :, 1 - core]
            pltpu.make_async_copy(view, view, sib_recv.at[part, quad]).wait()

        @pl.loop(0, half // tile)
        def _(step):
            cols = pl.ds(pl.multiple_of(step * tile, tile), tile)
            grad = gbuf[part, :, :, :, :, :, cols].reshape(width, tile)
            to = pl.ds(pl.multiple_of(part * half + step * tile, tile), tile)
            lapp[:, to] = jnp.dot(proot[...], grad, preferred_element_type=F32).astype(BF16)

    spread_part(0)
    qgather.hop(1)
    for step in range(3):
        hand_on(0, step)
    qgather.hop(2)
    for off in range(1, replicas):
        reduce_copy(1, off).wait_recv()
    sum_part(1)
    spread_part(1)
    factor_swap.wait_recv()
    for step in range(3, 10):
        hand_on(0, step)
        hand_on(1, step - 3)
    hand_on(1, 7)
    apply_part(0)
    hand_on(1, 8)
    hand_on(1, 9)
    qgather.hop(3)
    apply_part(1)

    applied = lapp[...]
    squares[member] = jnp.zeros((16, 128), F32)
    ends = owners // 2
    per_tile = ends // 2

    def update_copy(end):
        return remote(
            usend.at[end], uland.at[group, chip], up_send, up_recv, blk=core * ends + end
        )

    mine = pltpu.make_async_copy(usend.at[b % ends], uland.at[group, chip], up_recv)
    for turn_tile in (1, 0):
        number = (b % ends // per_tile + turn_tile) % 2
        cols = pl.ds(pl.multiple_of(number * tile, tile), tile)
        part = jnp.dot(
            applied, qbuf[:, :, cols].reshape(width, tile), preferred_element_type=F32
        )
        flipped = part.T
        usend[pl.ds(number * per_tile, per_tile)] = flipped.astype(BF16).reshape(
            per_tile, tile // per_tile, 2 * slab
        )
        squares[member, 8:16] += jnp.sum(
            (flipped * flipped).reshape(tile // 8, 8, 2, slab), axis=(0, 2)
        )
        if turn_tile == 0:
            pl.when(xl == core)(lambda: mine.start())
            pl.when(xl != core)(lambda: update_copy(b % ends).start())

        @pl.loop(1 if turn_tile == 0 else 0, per_tile)
        def _(off):
            update_copy(number * per_tile + (b + off) % per_tile).start()

    my_quad = (member % 4 - quarter + 4) % 4
    squares[member, 0:8] = jnp.zeros((8, 128), F32)
    for part in (0, 1):
        wide = gbuf[part, my_quad, member // 4].reshape(slab, half).astype(F32)
        squares[member, 0:8] += jnp.sum(
            (wide * wide).reshape(slab // 8, 8, half // 128, 128), axis=(0, 2)
        )

    def square_copy(off):
        to = (member + off) % GROUP
        return remote(
            squares.at[member],
            squares.at[member],
            sq_send.at[off],
            sq_recv.at[off],
            blk=group * GROUP + to,
        )

    for off in range(1, GROUP):
        square_copy(off).start()

    loads[1].wait()

    @pl.loop(0, tiles)
    def _(step):
        gram = jnp.zeros((slab, tile), F32)
        for part in (0, 1):
            gram = gram + lax.dot_general(
                gbuf[part, my_quad, member // 4].reshape(slab, half),
                gbuf[part, step].reshape(tile, half),
                (((1,), (1,)), ((), ())),
                preferred_element_type=F32,
            )
        for side in range(2):
            natural = side * 4 + (step + quarter) % 4
            cols = pl.ds(pl.multiple_of(natural * 128, 128), 128)
            lstat[:, cols] = (
                STAT_DECAY * lstat[:, cols]
                + (1.0 - STAT_DECAY) * gram[:, side * 128 : (side + 1) * 128]
            )

    store_left = pltpu.make_async_copy(lstat, newl_ref, out_sem.at[0])
    store_left.start()

    for off in range(1, GROUP):
        square_copy(off).wait_recv()
    total = jnp.sum(squares[...], axis=0)
    grad_square = jnp.sum(total[0:8], keepdims=True)
    update_square = jnp.sum(total[8:16], keepdims=True)
    scale = jnp.sqrt((grad_square + GRAFT_EPS) / (update_square + GRAFT_EPS))
    scales[group] = jnp.broadcast_to(scale, (8, 128))

    def scale_copy(off):
        to = (group + off) % groups
        return remote(
            scales.at[group],
            scales.at[group],
            sc_send.at[off],
            sc_recv.at[off],
            blk=to * GROUP + member,
        )

    for off in range(1, groups):
        scale_copy(off).start()

    loads[2].wait()
    first = pl.ds(pl.multiple_of(member % 4 * slab, slab), slab)
    columns = gbuf[member // 4, :, :, :, :, :, first].reshape(width, slab).T

    for part in (0, 1):

        @pl.loop(0, half // tile)
        def _(step):
            cols = pl.ds(pl.multiple_of(step * tile, tile), tile)
            to = pl.ds(pl.multiple_of(part * half + step * tile, tile), tile)
            grad = gbuf[part, :, :, :, :, :, cols].reshape(width, tile)
            gram = jnp.dot(columns, grad, preferred_element_type=F32)
            rstat[:, to] = STAT_DECAY * rstat[:, to] + (1.0 - STAT_DECAY) * gram

    store_right = pltpu.make_async_copy(rstat, newr_ref, out_sem.at[1])
    store_right.start()

    for part in (0, 1):
        for off in range(1, replicas):
            reduce_copy(part, off).wait_send()
        for across, ahead in spread_order:
            spread_copy(part, across, ahead).wait_send()
        for step in range(10):
            handed_on(part, step)
        for quad in range(4):
            cross_quad(part, quad).wait_send()
    qgather.drain()
    root_swap.wait_send()
    factor_swap.wait_send()
    for off in range(1, GROUP):
        square_copy(off).wait_send()
    for off in range(1, groups):
        scale_copy(off).wait_send()
        scale_copy(off).wait_recv()

    pltpu.make_async_copy(uland, uland, up_recv).wait()
    for block in range(groups):
        factor = scales[block, 0:1]
        for part in range(GROUP):
            piece = uland[block, part // 2, :, part % 2 * slab : (part % 2 + 1) * slab]
            ubuf[block, :, part * slab : (part + 1) * slab] = (
                piece.astype(F32) * factor
            ).astype(BF16)
    store_update = pltpu.make_async_copy(ubuf, update_ref, out_sem.at[2])
    store_update.start()
    others = usend.at[pl.ds(0, ends - 1)]
    pl.when(xl == core)(lambda: pltpu.make_async_copy(others, others, up_send).wait())
    pl.when(xl != core)(lambda: pltpu.make_async_copy(usend, usend, up_send).wait())
    store_left.wait()
    store_right.wait()
    store_update.wait()


def on_device(replicas, owners, gradients, left_stat, right_stat, left_root, right_root):
    _, row_count, block_count, width = gradients.shape
    local = block_count // replicas
    slab = width // GROUP
    part = width // owners
    groups = owners // GROUP
    half = width // 2
    dma = pltpu.SemaphoreType.DMA
    update, new_left, new_right = pl.pallas_call(
        functools.partial(kernel, replicas, owners),
        out_shape=(
            jax.ShapeDtypeStruct((local, part, width), BF16),
            jax.ShapeDtypeStruct((slab, width), F32),
            jax.ShapeDtypeStruct((slab, width), F32),
        ),
        in_specs=[pl.BlockSpec(memory_space=pltpu.HBM)] * 5,
        out_specs=[pl.BlockSpec(memory_space=pl.ANY)] * 3,
        scratch_shapes=[
            pltpu.VMEM((2, replicas, row_count, local, half), BF16),
            pltpu.VMEM((half // 128, row_count * local, 128), F32),
            pltpu.VMEM((2, local, row_count, half), BF16),
            pltpu.VMEM((2, 4, 2, 4, 2, row_count, half), BF16),
            pltpu.VMEM((4, 2 * slab, width // 2), BF16),
            pltpu.VMEM((2 * slab, width), BF16),
            pltpu.VMEM((slab, width), F32),
            pltpu.VMEM((slab, width), F32),
            pltpu.VMEM((2 * slab, width), BF16),
            pltpu.VMEM((owners // 2, part, 2 * slab), BF16),
            pltpu.VMEM((groups, 4, part, 2 * slab), BF16),
            pltpu.VMEM((GROUP, 16, 128), F32),
            pltpu.VMEM((groups, 8, 128), F32),
            pltpu.VMEM((local, part, width), BF16),
            dma((3,)),
            dma((2,)),
            dma((GROUP,)),
            dma((2, replicas)),
            dma((2, replicas)),
            dma((2,)),
            dma((2,)),
            dma((4, 2)),
            dma((4,)),
            dma((2, 2, 4)),
            dma((2, 2, 16)),
            dma((2, 16)),
            dma((2, 4)),
            dma((2, 4)),
            dma((GROUP,)),
            dma((GROUP,)),
            dma((groups,)),
            dma((groups,)),
            dma,
            dma,
            dma((3,)),
        ],
        compiler_params=pltpu.CompilerParams(
            collective_id=0, has_side_effects=True, vmem_limit_bytes=40 * 2**20
        ),
        cost_estimate=pl.CostEstimate(
            flops=8 * slab * width * width, bytes_accessed=8 * 2**20, transcendentals=0
        ),
    )(
        *(
            pltpu.with_memory_space_constraint(x, pltpu.HBM)
            for x in (
                gradients.reshape(row_count, replicas, local, width),
                left_stat[0],
                right_stat[0],
                left_root[0],
                right_root[0],
            )
        )
    )
    return jnp.swapaxes(update, 1, 2), new_left[None], new_right[None]


def solution(mesh):
    specs = (P("dp", "blk", None, None),) + (P(("dp", "blk"), None, None),) * 4
    out_specs = (P("dp", None, "blk"), P(("dp", "blk"), None, None), P(("dp", "blk"), None, None))
    return jax.shard_map(
        functools.partial(on_device, mesh.shape["dp"], mesh.shape["blk"]),
        mesh=mesh,
        in_specs=specs,
        out_specs=out_specs,
        check_vma=False,
    )
```

```python
import functools

import jax
import jax.numpy as jnp
from jax import lax
from jax.experimental import pallas as pl
from jax.experimental.pallas import tpu as pltpu
from jax.sharding import PartitionSpec as P

GROUP = 8
STAT_DECAY = 0.95
GRAFT_EPS = 1e-06
MESH = pl.DeviceIdType.MESH
F32 = jnp.float32
BF16 = jnp.bfloat16


def remote(src, dst, send, recv, **where):
    return pltpu.make_async_remote_copy(
        src_ref=src,
        dst_ref=dst,
        send_sem=send,
        recv_sem=recv,
        device_id=where,
        device_id_type=MESH,
    )


class LineGather:
    def __init__(self, view, first, chip, send, recv):
        self.view, self.first, self.chip = view, first, chip
        self.send, self.recv = send, recv

    def copy(self, slot, way):
        target = self.chip + (1 if way == 0 else -1)
        return remote(
            self.view(slot),
            self.view(slot),
            self.send.at[slot, way],
            self.recv.at[slot],
            blk=self.first + 2 * target,
        )

    def own(self):
        pl.when(self.chip < 3)(lambda: self.copy(self.chip, 0).start())
        pl.when(self.chip > 0)(lambda: self.copy(self.chip, 1).start())

    def hop(self, hop):
        left, right = self.chip - hop, self.chip + hop

        @pl.when(left >= 0)
        def _():
            self.copy(left, 0).wait_recv()
            pl.when(self.chip < 3)(lambda: self.copy(left, 0).start())

        @pl.when(right <= 3)
        def _():
            self.copy(right, 1).wait_recv()
            pl.when(self.chip > 0)(lambda: self.copy(right, 1).start())

    def drain(self):
        chip = self.chip
        pl.when(chip < 3)(lambda: self.copy(chip, 0).wait_send())
        pl.when(chip > 0)(lambda: self.copy(chip, 1).wait_send())
        for hop in range(1, 4):
            left, right = chip - hop, chip + hop
            pl.when((left >= 0) & (chip < 3))(lambda: self.copy(left, 0).wait_send())
            pl.when((right <= 3) & (chip > 0))(lambda: self.copy(right, 1).wait_send())


def kernel(
    replicas,
    owners,
    grad_ref,
    left_ref,
    right_ref,
    lroot_ref,
    rroot_ref,
    update_ref,
    newl_ref,
    newr_ref,
    gown,
    yfar,
    ynear,
    ymix,
    yadd,
    xout,
    xpass,
    xland,
    fsum,
    summed,
    gbuf,
    qbuf,
    proot,
    lstat,
    rstat,
    lacc,
    lapp,
    usend,
    uland,
    squares,
    scales,
    ubuf,
    local_sem,
    root_sem,
    y_send,
    y_recv,
    x_send,
    x_recv,
    pair_send,
    pair_recv,
    qg_send,
    qg_recv,
    sp_send,
    gg_send,
    gg_recv,
    sib_send,
    sib_recv,
    sq_send,
    sq_recv,
    sc_send,
    sc_recv,
    up_send,
    up_recv,
    out_sem,
):
    p = lax.axis_index("dp")
    b = lax.axis_index("blk")
    groups = owners // GROUP
    group, member = b // GROUP, b % GROUP
    chip, core = member // 2, member % 2
    y, xh = p // 2, p % 2
    xl, quarter = group // 4, group % 4
    row_count, width = grad_ref.shape[0], grad_ref.shape[3]
    half = row_count // 2
    slab = width // GROUP
    tile = 256
    tiles = width // tile

    pair = group * GROUP + chip * 2
    sibling = pair + 1 - core

    def half_of(which):
        return pl.ds(pl.multiple_of(which * (width // 2), width // 2), width // 2)

    def part_of(which):
        return pl.ds(pl.multiple_of(which * slab, slab), slab)

    loads = [
        pltpu.make_async_copy(grad_ref, gown, local_sem.at[0]),
        pltpu.make_async_copy(
            rroot_ref.at[:, half_of(core)], qbuf.at[chip, part_of(core)], local_sem.at[1]
        ),
        pltpu.make_async_copy(left_ref, lstat, local_sem.at[2]),
        pltpu.make_async_copy(right_ref, rstat, local_sem.at[3]),
    ]
    for block in range(GROUP):
        natural = (block % 2) * 4 + (block // 2 + quarter) % 4
        loads.append(
            pltpu.make_async_copy(
                lroot_ref.at[:, pl.ds(pl.multiple_of(natural * 128, 128), 128)],
                proot.at[part_of(core), pl.ds(block * 128, 128)],
                root_sem.at[block],
            )
        )
    for load in loads:
        load.start()

    flip = (b + owners // 2) % owners
    turn = y * 2 + 1 - xh
    near_a = {"dp": p, "blk": flip}
    near_b = {"dp": turn, "blk": flip}

    def at_y(step, which):
        return ((y + step) % 4) * 2 + which

    barrier = pltpu.get_barrier_semaphore()
    for peer in ({"dp": at_y(1, xh)}, {"dp": at_y(3, xh)}, near_b):
        pl.semaphore_signal(barrier, inc=1, device_id=peer, device_id_type=MESH)

    @pl.loop(1, owners)
    def _(off):
        pl.semaphore_signal(
            barrier, inc=1, device_id={"blk": (b + off) % owners}, device_id_type=MESH
        )

    pl.semaphore_wait(barrier, 3 + owners - 1)

    sides = (1 - xh, xh)
    steps = (1, 3)

    def rows_of(way):
        return pl.ds(way * half, half)

    def y_copy(kind, way, which):
        to = at_y(steps[way], xh)
        if kind == 0:
            src = grad_ref.at[rows_of(way), at_y(2, sides[which])]
            dst = yfar.at[way, which]
        elif kind == 1:
            src = grad_ref.at[rows_of(1 - way), at_y(steps[way], sides[which])]
            dst = ynear.at[way, which]
        else:
            src = yadd.at[way, which]
            dst = ymix.at[way, which]
        return remote(
            src, dst, y_send.at[kind, way, which], y_recv.at[kind, way, which], dp=to
        )

    def x_copy(stage, route):
        if stage == 0:
            where = (near_a, near_b)[route]
            src, dst = xout.at[route], xpass.at[route]
        else:
            where = (near_b, near_a)[route]
            src, dst = xpass.at[route], xland.at[route]
        return remote(src, dst, x_send.at[stage, route], x_recv.at[stage, route], **where)

    ways = (0, 1)
    for way in ways:
        y_copy(0, way, 0).start()
    for way in ways:
        y_copy(1, way, 0).start()
        y_copy(0, way, 1).start()

    root_swap = remote(
        rroot_ref.at[:, half_of(1 - core)],
        qbuf.at[chip, part_of(core)],
        pair_send.at[0],
        pair_recv.at[0],
        blk=sibling,
    )
    root_swap.start()
    for load in loads[4:]:
        load.wait()
    factor_swap = remote(
        proot.at[part_of(core)],
        proot.at[part_of(core)],
        pair_send.at[1],
        pair_recv.at[1],
        blk=sibling,
    )
    factor_swap.start()
    loads[1].wait()
    root_swap.wait_recv()
    qgather = LineGather(
        lambda s: qbuf.at[s], group * GROUP + core, chip, qg_send, qg_recv
    )
    qgather.own()
    loads[0].wait()

    def y_add(way, which):
        y_copy(0, way, which).wait_recv()

        @pl.loop(0, half)
        def _(row):
            mine = gown[way * half + row, at_y(steps[way], sides[which])]
            passed = yfar[way, which, row]
            yadd[way, which, row] = (mine.astype(F32) + passed.astype(F32)).astype(BF16)

    for way in ways:
        y_add(way, 0)
        y_copy(2, way, 0).start()
    for way in ways:
        y_copy(1, way, 1).start()
    for way in ways:
        y_add(way, 1)
        y_copy(2, way, 1).start()

    def y_total(part, which, row):
        return (
            gown[part * half + row, at_y(0, sides[which])].astype(F32)
            + ymix[part, which, row].astype(F32)
            + ynear[1 - part, which, row].astype(F32)
        )

    for part in ways:
        y_copy(2, part, 0).wait_recv()
        y_copy(1, 1 - part, 0).wait_recv()

        @pl.loop(0, half)
        def _(row):
            xout[part, row] = y_total(part, 0, row).astype(BF16)

        x_copy(0, part).start()
    qgather.hop(1)
    for route in ways:
        x_copy(0, route).wait_recv()
        x_copy(1, route).start()
    qgather.hop(2)

    for part in ways:
        y_copy(2, part, 1).wait_recv()
        y_copy(1, 1 - part, 1).wait_recv()
        x_copy(1, part).wait_recv()

        @pl.loop(0, half)
        def _(row):
            total = y_total(part, 1, row) + xland[part, row].astype(F32)
            place = pl.ds(pl.multiple_of((part * half + row) * groups, groups), groups)
            for lane in range(width // 128):
                fsum[lane, place, :] = total[:, lane * 128 : (lane + 1) * 128]

    for block in range(groups):
        for lane in range(width // 128):
            summed[block, :, lane * 128 : (lane + 1) * 128] = fsum[
                lane, pl.ds(block, row_count, stride=groups), :
            ].astype(BF16)

    def spread_copy(across, ahead):
        to_quarter = (quarter + ahead) % 4
        to_xl = (xl + across) % 2
        slot = (chip - 4 * ahead) % 16
        if ahead == 0:
            entry = chip
        elif ahead == 1:
            entry = 0
        elif ahead == 3:
            entry = 3
        else:
            entry = jnp.where(chip <= 1, 3, 0)
        return remote(
            summed.at[to_xl * 4 + to_quarter],
            gbuf.at[slot // 4, xl, slot % 4, core],
            sp_send.at[across, ahead],
            gg_recv.at[slot],
            blk=((to_xl * 4 + to_quarter) * 4 + entry) * 2 + core,
        )

    def slot_view(slot, which=core):
        return gbuf.at[slot // 4, :, slot % 4, which]

    spreads = [spread_copy(1, 0)]
    spreads += [spread_copy(across, ahead) for ahead in (2, 1, 3) for across in (1, 0)]
    for spread in spreads:
        spread.start()
    own_slot = gbuf.at[0, xl, chip, core]
    pltpu.make_async_copy(summed.at[group], own_slot, gg_recv.at[chip]).start()

    def pass_copy(slot, way):
        view = slot_view(slot)
        target = member + 2 if way == 0 else member - 2
        return remote(
            view, view, gg_send.at[way, slot], gg_recv.at[slot], blk=group * GROUP + target
        )

    def cross_slot(slot):
        view = slot_view(slot)
        return remote(view, view, sib_send.at[slot], sib_recv.at[slot], blk=sibling)

    def cross_quad(quad):
        view = gbuf.at[quad, :, :, core]
        return remote(view, view, sib_send.at[quad], sib_recv.at[quad], blk=sibling)

    def wait_slot(slot):
        view = slot_view(slot)
        pltpu.make_async_copy(view, view, gg_recv.at[slot]).wait()

    wait_slot(chip)
    pl.when(chip < 3)(lambda: pass_copy(chip, 0).start())
    pl.when(chip > 0)(lambda: pass_copy(chip, 1).start())

    def passing(action, between=None):
        for step in range(1, 10):
            from_left = (chip - step + 16) % 16
            from_right = chip + step
            pl.when(step <= chip + 6)(functools.partial(action, from_left, 0, chip < 3))
            pl.when(step <= 9 - chip)(functools.partial(action, from_right, 1, chip > 0))
            if between is not None:
                between(step)

    def forward(slot, way, more):
        wait_slot(slot)
        pl.when(more)(lambda: pass_copy(slot, way).start())
        pl.when(slot // 4 == 2)(lambda: cross_slot(slot).start())

    def sent(slot, way, more):
        pl.when(more)(lambda: pass_copy(slot, way).wait_send())

    def apply_quad(quad, first):
        if quad == 2:
            for slot in range(8, 12):
                view = slot_view(slot, 1 - core)
                pltpu.make_async_copy(view, view, sib_recv.at[slot]).wait()
        else:
            view = gbuf.at[quad, :, :, 1 - core]
            pltpu.make_async_copy(view, view, sib_recv.at[quad]).wait()
        factor = proot[:, quad * 256 : (quad + 1) * 256]

        @pl.loop(0, tiles)
        def _(step):
            cols = pl.ds(pl.multiple_of(step * tile, tile), tile)
            grad = gbuf[quad, :, :, :, :, cols].reshape(256, tile)
            part = jnp.dot(factor, grad, preferred_element_type=F32)
            if not first:
                part = part + lacc[:, cols]
            if quad == 2:
                lapp[:, cols] = part.astype(BF16)
            else:
                lacc[:, cols] = part

    def compute(step):
        if step == 3:
            cross_quad(0).start()
        elif step == 5:
            factor_swap.wait_recv()
            apply_quad(0, True)
        elif step == 7:
            cross_quad(1).start()
            cross_quad(3).start()
        elif step == 9:
            apply_quad(1, False)
            apply_quad(3, False)

    passing(forward, compute)
    apply_quad(2, False)
    qgather.hop(3)

    applied = lapp[...]
    squares[member] = jnp.zeros((16, 128), F32)
    ends = owners // 2
    per_tile = ends // 2

    def update_copy(end):
        return remote(
            usend.at[end], uland.at[group, chip], up_send, up_recv, blk=core * ends + end
        )

    mine = pltpu.make_async_copy(usend.at[b % ends], uland.at[group, chip], up_recv)
    for turn_tile in (1, 0):
        number = (b % ends // per_tile + turn_tile) % 2
        cols = pl.ds(pl.multiple_of(number * tile, tile), tile)
        part = jnp.dot(
            applied, qbuf[:, :, cols].reshape(width, tile), preferred_element_type=F32
        )
        flipped = part.T
        usend[pl.ds(number * per_tile, per_tile)] = flipped.astype(BF16).reshape(
            per_tile, tile // per_tile, 2 * slab
        )
        squares[member, 8:16] += jnp.sum(
            (flipped * flipped).reshape(tile // 8, 8, 2, slab), axis=(0, 2)
        )
        if turn_tile == 0:
            pl.when(xl == core)(lambda: mine.start())
            pl.when(xl != core)(lambda: update_copy(b % ends).start())

        @pl.loop(1 if turn_tile == 0 else 0, per_tile)
        def _(off):
            update_copy(number * per_tile + (b + off) % per_tile).start()

    my_quad = (member % 4 - quarter + 4) % 4
    rows = gbuf[my_quad, member // 4].reshape(slab, width)
    wide = rows.astype(F32)
    squares[member, 0:8] = jnp.sum(
        (wide * wide).reshape(slab // 8, 8, width // 128, 128), axis=(0, 2)
    )

    def square_copy(off):
        to = (member + off) % GROUP
        return remote(
            squares.at[member],
            squares.at[member],
            sq_send.at[off],
            sq_recv.at[off],
            blk=group * GROUP + to,
        )

    for off in range(1, GROUP):
        square_copy(off).start()

    loads[2].wait()

    @pl.loop(0, tiles)
    def _(step):
        other = gbuf[step].reshape(tile, width)
        gram = lax.dot_general(
            rows, other, (((1,), (1,)), ((), ())), preferred_element_type=F32
        )
        for side in range(2):
            natural = side * 4 + (step + quarter) % 4
            cols = pl.ds(pl.multiple_of(natural * 128, 128), 128)
            lstat[:, cols] = (
                STAT_DECAY * lstat[:, cols]
                + (1.0 - STAT_DECAY) * gram[:, side * 128 : (side + 1) * 128]
            )

    store_left = pltpu.make_async_copy(lstat, newl_ref, out_sem.at[0])
    store_left.start()

    for off in range(1, GROUP):
        square_copy(off).wait_recv()
    total = jnp.sum(squares[...], axis=0)
    grad_square = jnp.sum(total[0:8], keepdims=True)
    update_square = jnp.sum(total[8:16], keepdims=True)
    scale = jnp.sqrt((grad_square + GRAFT_EPS) / (update_square + GRAFT_EPS))
    scales[group] = jnp.broadcast_to(scale, (8, 128))

    def scale_copy(off):
        to = (group + off) % groups
        return remote(
            scales.at[group],
            scales.at[group],
            sc_send.at[off],
            sc_recv.at[off],
            blk=to * GROUP + member,
        )

    for off in range(1, groups):
        scale_copy(off).start()

    loads[3].wait()
    first = pl.ds(pl.multiple_of(member * slab, slab), slab)
    columns = gbuf[:, :, :, :, :, first].reshape(width, slab).T

    @pl.loop(0, tiles)
    def _(step):
        cols = pl.ds(pl.multiple_of(step * tile, tile), tile)
        grad = gbuf[:, :, :, :, :, cols].reshape(width, tile)
        gram = jnp.dot(columns, grad, preferred_element_type=F32)
        rstat[:, cols] = STAT_DECAY * rstat[:, cols] + (1.0 - STAT_DECAY) * gram

    store_right = pltpu.make_async_copy(rstat, newr_ref, out_sem.at[1])
    store_right.start()

    for kind in range(3):
        for way in ways:
            for which in (0, 1):
                y_copy(kind, way, which).wait_send()
    for route in ways:
        x_copy(0, route).wait_send()
        x_copy(1, route).wait_send()
    qgather.drain()
    root_swap.wait_send()
    factor_swap.wait_send()
    for spread in spreads:
        spread.wait_send()
    pl.when(chip < 3)(lambda: pass_copy(chip, 0).wait_send())
    pl.when(chip > 0)(lambda: pass_copy(chip, 1).wait_send())
    passing(sent)
    for quad in (0, 1, 3):
        cross_quad(quad).wait_send()
    for slot in range(8, 12):
        cross_slot(slot).wait_send()
    for off in range(1, GROUP):
        square_copy(off).wait_send()
    for off in range(1, groups):
        scale_copy(off).wait_send()
        scale_copy(off).wait_recv()

    pltpu.make_async_copy(uland, uland, up_recv).wait()
    for block in range(groups):
        factor = scales[block, 0:1]
        for part in range(GROUP):
            piece = uland[block, part // 2, :, part % 2 * slab : (part % 2 + 1) * slab]
            ubuf[block, :, part * slab : (part + 1) * slab] = (
                piece.astype(F32) * factor
            ).astype(BF16)
    store_update = pltpu.make_async_copy(ubuf, update_ref, out_sem.at[2])
    store_update.start()
    others = usend.at[pl.ds(0, ends - 1)]
    pl.when(xl == core)(lambda: pltpu.make_async_copy(others, others, up_send).wait())
    pl.when(xl != core)(lambda: pltpu.make_async_copy(usend, usend, up_send).wait())
    store_left.wait()
    store_right.wait()
    store_update.wait()


def on_device(replicas, owners, gradients, left_stat, right_stat, left_root, right_root):
    _, row_count, block_count, width = gradients.shape
    local = block_count // replicas
    slab = width // GROUP
    part = width // owners
    groups = owners // GROUP
    dma = pltpu.SemaphoreType.DMA
    update, new_left, new_right = pl.pallas_call(
        functools.partial(kernel, replicas, owners),
        out_shape=(
            jax.ShapeDtypeStruct((local, part, width), BF16),
            jax.ShapeDtypeStruct((slab, width), F32),
            jax.ShapeDtypeStruct((slab, width), F32),
        ),
        in_specs=[pl.BlockSpec(memory_space=pltpu.HBM)] * 5,
        out_specs=[pl.BlockSpec(memory_space=pl.ANY)] * 3,
        scratch_shapes=[
            pltpu.VMEM((row_count, replicas, local, width), BF16),
            *[pltpu.VMEM((2, 2, row_count // 2, local, width), BF16)] * 4,
            *[pltpu.VMEM((2, row_count // 2, local, width), BF16)] * 3,
            pltpu.VMEM((width // 128, row_count * local, 128), F32),
            pltpu.VMEM((local, row_count, width), BF16),
            pltpu.VMEM((4, 2, 4, 2, row_count, width), BF16),
            pltpu.VMEM((4, 2 * slab, width // 2), BF16),
            pltpu.VMEM((2 * slab, width), BF16),
            pltpu.VMEM((slab, width), F32),
            pltpu.VMEM((slab, width), F32),
            pltpu.VMEM((2 * slab, width), F32),
            pltpu.VMEM((2 * slab, width), BF16),
            pltpu.VMEM((owners // 2, part, 2 * slab), BF16),
            pltpu.VMEM((groups, 4, part, 2 * slab), BF16),
            pltpu.VMEM((GROUP, 16, 128), F32),
            pltpu.VMEM((groups, 8, 128), F32),
            pltpu.VMEM((local, part, width), BF16),
            dma((4,)),
            dma((GROUP,)),
            dma((3, 2, 2)),
            dma((3, 2, 2)),
            dma((2, 2)),
            dma((2, 2)),
            dma((2,)),
            dma((2,)),
            dma((4, 2)),
            dma((4,)),
            dma((2, 4)),
            dma((2, 16)),
            dma((16,)),
            dma((16,)),
            dma((16,)),
            dma((GROUP,)),
            dma((GROUP,)),
            dma((groups,)),
            dma((groups,)),
            dma,
            dma,
            dma((3,)),
        ],
        compiler_params=pltpu.CompilerParams(
            collective_id=0, has_side_effects=True, vmem_limit_bytes=40 * 2**20
        ),
        cost_estimate=pl.CostEstimate(
            flops=8 * slab * width * width, bytes_accessed=8 * 2**20, transcendentals=0
        ),
    )(
        *(
            pltpu.with_memory_space_constraint(x, pltpu.HBM)
            for x in (
                gradients.reshape(row_count, replicas, local, width),
                left_stat[0],
                right_stat[0],
                left_root[0],
                right_root[0],
            )
        )
    )
    return jnp.swapaxes(update, 1, 2), new_left[None], new_right[None]


def solution(mesh):
    specs = (P("dp", "blk", None, None),) + (P(("dp", "blk"), None, None),) * 4
    out_specs = (P("dp", None, "blk"), P(("dp", "blk"), None, None), P(("dp", "blk"), None, None))
    return jax.shard_map(
        functools.partial(on_device, mesh.shape["dp"], mesh.shape["blk"]),
        mesh=mesh,
        in_specs=specs,
        out_specs=out_specs,
        check_vma=False,
    )
```

```python
import functools

import jax
import jax.numpy as jnp
from jax import lax
from jax.experimental import pallas as pl
from jax.experimental.pallas import tpu as pltpu
from jax.sharding import PartitionSpec as P

GROUP = 8
STAT_DECAY = 0.95
GRAFT_EPS = 1e-06
MESH = pl.DeviceIdType.MESH
F32 = jnp.float32
BF16 = jnp.bfloat16


def remote(src, dst, send, recv, **where):
    return pltpu.make_async_remote_copy(
        src_ref=src,
        dst_ref=dst,
        send_sem=send,
        recv_sem=recv,
        device_id=where,
        device_id_type=MESH,
    )


class LineGather:
    def __init__(self, view, first, chip, send, recv):
        self.view, self.first, self.chip = view, first, chip
        self.send, self.recv = send, recv

    def copy(self, slot, way):
        target = self.chip + (1 if way == 0 else -1)
        return remote(
            self.view(slot),
            self.view(slot),
            self.send.at[slot, way],
            self.recv.at[slot],
            blk=self.first + 2 * target,
        )

    def own(self):
        pl.when(self.chip < 3)(lambda: self.copy(self.chip, 0).start())
        pl.when(self.chip > 0)(lambda: self.copy(self.chip, 1).start())

    def hop(self, hop):
        left, right = self.chip - hop, self.chip + hop

        @pl.when(left >= 0)
        def _():
            self.copy(left, 0).wait_recv()
            pl.when(self.chip < 3)(lambda: self.copy(left, 0).start())

        @pl.when(right <= 3)
        def _():
            self.copy(right, 1).wait_recv()
            pl.when(self.chip > 0)(lambda: self.copy(right, 1).start())

    def drain(self):
        chip = self.chip
        pl.when(chip < 3)(lambda: self.copy(chip, 0).wait_send())
        pl.when(chip > 0)(lambda: self.copy(chip, 1).wait_send())
        for hop in range(1, 4):
            left, right = chip - hop, chip + hop
            pl.when((left >= 0) & (chip < 3))(lambda: self.copy(left, 0).wait_send())
            pl.when((right <= 3) & (chip > 0))(lambda: self.copy(right, 1).wait_send())


class GroupGather:
    def __init__(self, view, group, member, send, recv):
        self.view, self.group, self.member = view, group, member
        self.send, self.recv = send, recv
        self.chip, self.core = member // 2, member % 2

    def copy(self, slot, target, way):
        return remote(
            self.view(slot),
            self.view(slot),
            self.send.at[slot, way],
            self.recv.at[slot],
            blk=self.group * GROUP + target,
        )

    def to_right(self, slot):
        return self.copy(slot, self.member + 2, 0)

    def to_left(self, slot):
        return self.copy(slot, self.member - 2, 1)

    def to_sibling(self, slot):
        return self.copy(slot, self.chip * 2 + 1 - self.core, 2)

    def own(self):
        slot = self.member
        pl.when(self.chip < 3)(lambda: self.to_right(slot).start())
        pl.when(self.chip > 0)(lambda: self.to_left(slot).start())
        self.to_sibling(slot).start()

    def hop(self, hop):
        left, right = self.member - 2 * hop, self.member + 2 * hop

        @pl.when(self.chip >= hop)
        def _():
            self.to_right(left).wait_recv()
            pl.when(self.chip < 3)(lambda: self.to_right(left).start())
            self.to_sibling(left).start()

        @pl.when(self.chip + hop <= 3)
        def _():
            self.to_left(right).wait_recv()
            pl.when(self.chip > 0)(lambda: self.to_left(right).start())
            self.to_sibling(right).start()

    def finish(self):
        for other in range(4):
            self.to_sibling(other * 2 + 1 - self.core).wait_recv()

    def drain(self):
        chip = self.chip
        pl.when(chip < 3)(lambda: self.to_right(self.member).wait_send())
        pl.when(chip > 0)(lambda: self.to_left(self.member).wait_send())
        self.to_sibling(self.member).wait_send()
        for hop in range(1, 4):
            left, right = self.member - 2 * hop, self.member + 2 * hop

            @pl.when(chip >= hop)
            def _():
                pl.when(chip < 3)(lambda: self.to_right(left).wait_send())
                self.to_sibling(left).wait_send()

            @pl.when(chip + hop <= 3)
            def _():
                pl.when(chip > 0)(lambda: self.to_left(right).wait_send())
                self.to_sibling(right).wait_send()


def kernel(
    replicas,
    owners,
    grad_ref,
    left_ref,
    right_ref,
    lroot_ref,
    rroot_ref,
    update_ref,
    newl_ref,
    newr_ref,
    gown,
    yfar,
    ynear,
    ymix,
    yadd,
    xout,
    xpass,
    xland,
    fsum,
    summed,
    gbuf,
    qbuf,
    proot,
    lstat,
    rstat,
    lacc,
    lapp,
    usend,
    uland,
    squares,
    scales,
    ubuf,
    local_sem,
    root_sem,
    y_send,
    y_recv,
    x_send,
    x_recv,
    pair_send,
    pair_recv,
    qg_send,
    qg_recv,
    sp_send,
    sp_recv,
    gg_send,
    gg_recv,
    sq_send,
    sq_recv,
    sc_send,
    sc_recv,
    up_send,
    up_recv,
    out_sem,
):
    p = lax.axis_index("dp")
    b = lax.axis_index("blk")
    groups = owners // GROUP
    group, member = b // GROUP, b % GROUP
    chip, core = member // 2, member % 2
    y, xh = p // 2, p % 2
    xl, quarter = group // 4, group % 4
    row_count, width = grad_ref.shape[0], grad_ref.shape[3]
    half = row_count // 2
    slab = width // GROUP
    tile = 256
    tiles = width // tile

    pair = group * GROUP + chip * 2
    sibling = pair + 1 - core

    def half_of(which):
        return pl.ds(pl.multiple_of(which * (width // 2), width // 2), width // 2)

    def part_of(which):
        return pl.ds(pl.multiple_of(which * slab, slab), slab)

    loads = [
        pltpu.make_async_copy(grad_ref, gown, local_sem.at[0]),
        pltpu.make_async_copy(
            rroot_ref.at[:, half_of(core)], qbuf.at[chip, part_of(core)], local_sem.at[1]
        ),
        pltpu.make_async_copy(left_ref, lstat, local_sem.at[2]),
        pltpu.make_async_copy(right_ref, rstat, local_sem.at[3]),
    ]
    for block in range(GROUP):
        natural = (block % 2) * 4 + (quarter - block // 2 + 4) % 4
        loads.append(
            pltpu.make_async_copy(
                lroot_ref.at[:, pl.ds(pl.multiple_of(natural * 128, 128), 128)],
                proot.at[part_of(core), pl.ds(block * 128, 128)],
                root_sem.at[block],
            )
        )
    for load in loads:
        load.start()

    flip = (b + owners // 2) % owners
    turn = y * 2 + 1 - xh
    near_a = {"dp": p, "blk": flip}
    near_b = {"dp": turn, "blk": flip}

    def at_y(step, which):
        return ((y + step) % 4) * 2 + which

    barrier = pltpu.get_barrier_semaphore()
    for peer in ({"dp": at_y(1, xh)}, {"dp": at_y(3, xh)}, near_b):
        pl.semaphore_signal(barrier, inc=1, device_id=peer, device_id_type=MESH)

    @pl.loop(1, owners)
    def _(off):
        pl.semaphore_signal(
            barrier, inc=1, device_id={"blk": (b + off) % owners}, device_id_type=MESH
        )

    pl.semaphore_wait(barrier, 3 + owners - 1)

    sides = (1 - xh, xh)
    steps = (1, 3)

    def rows_of(way):
        return pl.ds(way * half, half)

    def y_copy(kind, way, which):
        to = at_y(steps[way], xh)
        if kind == 0:
            src = grad_ref.at[rows_of(way), at_y(2, sides[which])]
            dst = yfar.at[way, which]
        elif kind == 1:
            src = grad_ref.at[rows_of(1 - way), at_y(steps[way], sides[which])]
            dst = ynear.at[way, which]
        else:
            src = yadd.at[way, which]
            dst = ymix.at[way, which]
        return remote(
            src, dst, y_send.at[kind, way, which], y_recv.at[kind, way, which], dp=to
        )

    def x_copy(stage, route):
        if stage == 0:
            where = (near_a, near_b)[route]
            src, dst = xout.at[route], xpass.at[route]
        else:
            where = (near_b, near_a)[route]
            src, dst = xpass.at[route], xland.at[route]
        return remote(src, dst, x_send.at[stage, route], x_recv.at[stage, route], **where)

    ways = (0, 1)
    for way in ways:
        y_copy(0, way, 0).start()
    for way in ways:
        y_copy(1, way, 0).start()
        y_copy(0, way, 1).start()

    root_swap = remote(
        rroot_ref.at[:, half_of(1 - core)],
        qbuf.at[chip, part_of(core)],
        pair_send.at[0],
        pair_recv.at[0],
        blk=sibling,
    )
    root_swap.start()
    for load in loads[4:]:
        load.wait()
    factor_swap = remote(
        proot.at[part_of(core)],
        proot.at[part_of(core)],
        pair_send.at[1],
        pair_recv.at[1],
        blk=sibling,
    )
    factor_swap.start()
    loads[1].wait()
    root_swap.wait_recv()
    qgather = LineGather(
        lambda s: qbuf.at[s], group * GROUP + core, chip, qg_send, qg_recv
    )
    qgather.own()
    loads[0].wait()

    def y_add(way, which):
        y_copy(0, way, which).wait_recv()

        @pl.loop(0, half)
        def _(row):
            mine = gown[way * half + row, at_y(steps[way], sides[which])]
            passed = yfar[way, which, row]
            yadd[way, which, row] = (mine.astype(F32) + passed.astype(F32)).astype(BF16)

    for way in ways:
        y_add(way, 0)
        y_copy(2, way, 0).start()
    for way in ways:
        y_copy(1, way, 1).start()
    for way in ways:
        y_add(way, 1)
        y_copy(2, way, 1).start()

    def y_total(part, which, row):
        return (
            gown[part * half + row, at_y(0, sides[which])].astype(F32)
            + ymix[part, which, row].astype(F32)
            + ynear[1 - part, which, row].astype(F32)
        )

    for part in ways:
        y_copy(2, part, 0).wait_recv()
        y_copy(1, 1 - part, 0).wait_recv()

        @pl.loop(0, half)
        def _(row):
            xout[part, row] = y_total(part, 0, row).astype(BF16)

        x_copy(0, part).start()
    qgather.hop(1)
    for route in ways:
        x_copy(0, route).wait_recv()
        x_copy(1, route).start()
    qgather.hop(2)

    for part in ways:
        y_copy(2, part, 1).wait_recv()
        y_copy(1, 1 - part, 1).wait_recv()
        x_copy(1, part).wait_recv()

        @pl.loop(0, half)
        def _(row):
            total = y_total(part, 1, row) + xland[part, row].astype(F32)
            place = pl.ds(pl.multiple_of((part * half + row) * groups, groups), groups)
            for lane in range(width // 128):
                fsum[lane, place, :] = total[:, lane * 128 : (lane + 1) * 128]

    for block in range(groups):
        for lane in range(width // 128):
            summed[block, :, lane * 128 : (lane + 1) * 128] = fsum[
                lane, pl.ds(block, row_count, stride=groups), :
            ].astype(BF16)

    def spread_copy(across, ahead):
        to = (xl + across) % 2 * 4 + (quarter + ahead) % 4
        return remote(
            summed.at[to],
            gbuf.at[ahead, xl, chip, core],
            sp_send.at[across, ahead],
            sp_recv.at[ahead // 2],
            blk=to * GROUP + member,
        )

    spreads = [spread_copy(1, 0)]
    spreads += [spread_copy(across, ahead) for ahead in (1, 3, 2) for across in (1, 0)]
    for spread in spreads:
        spread.start()
    own_slot = gbuf.at[0, xl, chip, core]
    pltpu.make_async_copy(summed.at[group], own_slot, sp_recv.at[0]).start()

    def part_view(part, slot):
        return gbuf.at[pl.ds(2 * part, 2), :, slot // 2, slot % 2]

    gathers = [
        GroupGather(
            functools.partial(part_view, part),
            group,
            member,
            gg_send.at[part],
            gg_recv.at[part],
        )
        for part in (0, 1)
    ]
    for part in (0, 1):
        view = part_view(part, member)
        pltpu.make_async_copy(view, view, sp_recv.at[part]).wait()
        gathers[part].own()
    for hop in (1, 2, 3):
        for part in (0, 1):
            gathers[part].hop(hop)

    factor_swap.wait_recv()
    for part in (0, 1):
        gathers[part].finish()
        factor = proot[:, part * 512 : (part + 1) * 512]

        @pl.loop(0, tiles)
        def _(step):
            cols = pl.ds(pl.multiple_of(step * tile, tile), tile)
            grad = gbuf[2 * part : 2 * part + 2, :, :, :, :, cols].reshape(512, tile)
            product = jnp.dot(factor, grad, preferred_element_type=F32)
            if part == 0:
                lacc[:, cols] = product
            else:
                lapp[:, cols] = (product + lacc[:, cols]).astype(BF16)

    qgather.hop(3)

    applied = lapp[...]
    squares[member] = jnp.zeros((16, 128), F32)
    ends = owners // 2
    per_tile = ends // 2

    def update_copy(end):
        return remote(
            usend.at[end], uland.at[group, chip], up_send, up_recv, blk=core * ends + end
        )

    mine = pltpu.make_async_copy(usend.at[b % ends], uland.at[group, chip], up_recv)
    for turn_tile in (1, 0):
        number = (b % ends // per_tile + turn_tile) % 2
        cols = pl.ds(pl.multiple_of(number * tile, tile), tile)
        part = jnp.dot(
            applied, qbuf[:, :, cols].reshape(width, tile), preferred_element_type=F32
        )
        flipped = part.T
        usend[pl.ds(number * per_tile, per_tile)] = flipped.astype(BF16).reshape(
            per_tile, tile // per_tile, 2 * slab
        )
        squares[member, 8:16] += jnp.sum(
            (flipped * flipped).reshape(tile // 8, 8, 2, slab), axis=(0, 2)
        )
        if turn_tile == 0:
            pl.when(xl == core)(lambda: mine.start())
            pl.when(xl != core)(lambda: update_copy(b % ends).start())

        @pl.loop(1 if turn_tile == 0 else 0, per_tile)
        def _(off):
            update_copy(number * per_tile + (b + off) % per_tile).start()

    my_quad = (quarter - member % 4 + 4) % 4
    rows = gbuf[my_quad, member // 4].reshape(slab, width)
    wide = rows.astype(F32)
    squares[member, 0:8] = jnp.sum(
        (wide * wide).reshape(slab // 8, 8, width // 128, 128), axis=(0, 2)
    )

    def square_copy(off):
        to = (member + off) % GROUP
        return remote(
            squares.at[member],
            squares.at[member],
            sq_send.at[off],
            sq_recv.at[off],
            blk=group * GROUP + to,
        )

    for off in range(1, GROUP):
        square_copy(off).start()

    loads[2].wait()

    @pl.loop(0, tiles)
    def _(step):
        other = gbuf[step].reshape(tile, width)
        gram = lax.dot_general(
            rows, other, (((1,), (1,)), ((), ())), preferred_element_type=F32
        )
        for side in range(2):
            natural = side * 4 + (quarter - step + 4) % 4
            cols = pl.ds(pl.multiple_of(natural * 128, 128), 128)
            lstat[:, cols] = (
                STAT_DECAY * lstat[:, cols]
                + (1.0 - STAT_DECAY) * gram[:, side * 128 : (side + 1) * 128]
            )

    store_left = pltpu.make_async_copy(lstat, newl_ref, out_sem.at[0])
    store_left.start()

    for off in range(1, GROUP):
        square_copy(off).wait_recv()
    total = jnp.sum(squares[...], axis=0)
    grad_square = jnp.sum(total[0:8], keepdims=True)
    update_square = jnp.sum(total[8:16], keepdims=True)
    scale = jnp.sqrt((grad_square + GRAFT_EPS) / (update_square + GRAFT_EPS))
    scales[group] = jnp.broadcast_to(scale, (8, 128))

    def scale_copy(off):
        to = (group + off) % groups
        return remote(
            scales.at[group],
            scales.at[group],
            sc_send.at[off],
            sc_recv.at[off],
            blk=to * GROUP + member,
        )

    for off in range(1, groups):
        scale_copy(off).start()

    loads[3].wait()
    first = pl.ds(pl.multiple_of(member * slab, slab), slab)
    columns = gbuf[:, :, :, :, :, first].reshape(width, slab).T

    @pl.loop(0, tiles)
    def _(step):
        cols = pl.ds(pl.multiple_of(step * tile, tile), tile)
        grad = gbuf[:, :, :, :, :, cols].reshape(width, tile)
        gram = jnp.dot(columns, grad, preferred_element_type=F32)
        rstat[:, cols] = STAT_DECAY * rstat[:, cols] + (1.0 - STAT_DECAY) * gram

    store_right = pltpu.make_async_copy(rstat, newr_ref, out_sem.at[1])
    store_right.start()

    for kind in range(3):
        for way in ways:
            for which in (0, 1):
                y_copy(kind, way, which).wait_send()
    for route in ways:
        x_copy(0, route).wait_send()
        x_copy(1, route).wait_send()
    qgather.drain()
    root_swap.wait_send()
    factor_swap.wait_send()
    for spread in spreads:
        spread.wait_send()
    for part in (0, 1):
        gathers[part].drain()
    for off in range(1, GROUP):
        square_copy(off).wait_send()
    for off in range(1, groups):
        scale_copy(off).wait_send()
        scale_copy(off).wait_recv()

    pltpu.make_async_copy(uland, uland, up_recv).wait()
    for block in range(groups):
        factor = scales[block, 0:1]
        for part in range(GROUP):
            piece = uland[block, part // 2, :, part % 2 * slab : (part % 2 + 1) * slab]
            ubuf[block, :, part * slab : (part + 1) * slab] = (
                piece.astype(F32) * factor
            ).astype(BF16)
    store_update = pltpu.make_async_copy(ubuf, update_ref, out_sem.at[2])
    store_update.start()
    others = usend.at[pl.ds(0, ends - 1)]
    pl.when(xl == core)(lambda: pltpu.make_async_copy(others, others, up_send).wait())
    pl.when(xl != core)(lambda: pltpu.make_async_copy(usend, usend, up_send).wait())
    store_left.wait()
    store_right.wait()
    store_update.wait()


def on_device(replicas, owners, gradients, left_stat, right_stat, left_root, right_root):
    _, row_count, block_count, width = gradients.shape
    local = block_count // replicas
    slab = width // GROUP
    part = width // owners
    groups = owners // GROUP
    dma = pltpu.SemaphoreType.DMA
    update, new_left, new_right = pl.pallas_call(
        functools.partial(kernel, replicas, owners),
        out_shape=(
            jax.ShapeDtypeStruct((local, part, width), BF16),
            jax.ShapeDtypeStruct((slab, width), F32),
            jax.ShapeDtypeStruct((slab, width), F32),
        ),
        in_specs=[pl.BlockSpec(memory_space=pltpu.HBM)] * 5,
        out_specs=[pl.BlockSpec(memory_space=pl.ANY)] * 3,
        scratch_shapes=[
            pltpu.VMEM((row_count, replicas, local, width), BF16),
            *[pltpu.VMEM((2, 2, row_count // 2, local, width), BF16)] * 4,
            *[pltpu.VMEM((2, row_count // 2, local, width), BF16)] * 3,
            pltpu.VMEM((width // 128, row_count * local, 128), F32),
            pltpu.VMEM((local, row_count, width), BF16),
            pltpu.VMEM((4, 2, 4, 2, row_count, width), BF16),
            pltpu.VMEM((4, 2 * slab, width // 2), BF16),
            pltpu.VMEM((2 * slab, width), BF16),
            pltpu.VMEM((slab, width), F32),
            pltpu.VMEM((slab, width), F32),
            pltpu.VMEM((2 * slab, width), F32),
            pltpu.VMEM((2 * slab, width), BF16),
            pltpu.VMEM((owners // 2, part, 2 * slab), BF16),
            pltpu.VMEM((groups, 4, part, 2 * slab), BF16),
            pltpu.VMEM((GROUP, 16, 128), F32),
            pltpu.VMEM((groups, 8, 128), F32),
            pltpu.VMEM((local, part, width), BF16),
            dma((4,)),
            dma((GROUP,)),
            dma((3, 2, 2)),
            dma((3, 2, 2)),
            dma((2, 2)),
            dma((2, 2)),
            dma((2,)),
            dma((2,)),
            dma((4, 2)),
            dma((4,)),
            dma((2, 4)),
            dma((2,)),
            dma((2, GROUP, 3)),
            dma((2, GROUP)),
            dma((GROUP,)),
            dma((GROUP,)),
            dma((groups,)),
            dma((groups,)),
            dma,
            dma,
            dma((3,)),
        ],
        compiler_params=pltpu.CompilerParams(
            collective_id=0, has_side_effects=True, vmem_limit_bytes=40 * 2**20
        ),
        cost_estimate=pl.CostEstimate(
            flops=8 * slab * width * width, bytes_accessed=8 * 2**20, transcendentals=0
        ),
    )(
        *(
            pltpu.with_memory_space_constraint(x, pltpu.HBM)
            for x in (
                gradients.reshape(row_count, replicas, local, width),
                left_stat[0],
                right_stat[0],
                left_root[0],
                right_root[0],
            )
        )
    )
    return jnp.swapaxes(update, 1, 2), new_left[None], new_right[None]


def solution(mesh):
    specs = (P("dp", "blk", None, None),) + (P(("dp", "blk"), None, None),) * 4
    out_specs = (P("dp", None, "blk"), P(("dp", "blk"), None, None), P(("dp", "blk"), None, None))
    return jax.shard_map(
        functools.partial(on_device, mesh.shape["dp"], mesh.shape["blk"]),
        mesh=mesh,
        in_specs=specs,
        out_specs=out_specs,
        check_vma=False,
    )
```

```python
import functools

import jax
import jax.numpy as jnp
from jax import lax
from jax.experimental import pallas as pl
from jax.experimental.pallas import tpu as pltpu
from jax.sharding import PartitionSpec as P

GROUP = 8
STAT_DECAY = 0.95
GRAFT_EPS = 1e-06
MESH = pl.DeviceIdType.MESH
F32 = jnp.float32
BF16 = jnp.bfloat16


def remote(src, dst, send, recv, **where):
    return pltpu.make_async_remote_copy(
        src_ref=src,
        dst_ref=dst,
        send_sem=send,
        recv_sem=recv,
        device_id=where,
        device_id_type=MESH,
    )


class LineGather:
    def __init__(self, view, first, chip, send, recv):
        self.view, self.first, self.chip = view, first, chip
        self.send, self.recv = send, recv

    def copy(self, slot, way):
        target = self.chip + (1 if way == 0 else -1)
        return remote(
            self.view(slot),
            self.view(slot),
            self.send.at[slot, way],
            self.recv.at[slot],
            blk=self.first + 2 * target,
        )

    def own(self):
        pl.when(self.chip < 3)(lambda: self.copy(self.chip, 0).start())
        pl.when(self.chip > 0)(lambda: self.copy(self.chip, 1).start())

    def hop(self, hop):
        left, right = self.chip - hop, self.chip + hop

        @pl.when(left >= 0)
        def _():
            self.copy(left, 0).wait_recv()
            pl.when(self.chip < 3)(lambda: self.copy(left, 0).start())

        @pl.when(right <= 3)
        def _():
            self.copy(right, 1).wait_recv()
            pl.when(self.chip > 0)(lambda: self.copy(right, 1).start())

    def drain(self):
        chip = self.chip
        pl.when(chip < 3)(lambda: self.copy(chip, 0).wait_send())
        pl.when(chip > 0)(lambda: self.copy(chip, 1).wait_send())
        for hop in range(1, 4):
            left, right = chip - hop, chip + hop
            pl.when((left >= 0) & (chip < 3))(lambda: self.copy(left, 0).wait_send())
            pl.when((right <= 3) & (chip > 0))(lambda: self.copy(right, 1).wait_send())


class GroupGather:
    def __init__(self, view, group, member, send, recv):
        self.view, self.group, self.member = view, group, member
        self.send, self.recv = send, recv
        self.chip, self.core = member // 2, member % 2

    def copy(self, slot, target, way):
        return remote(
            self.view(slot),
            self.view(slot),
            self.send.at[slot, way],
            self.recv.at[slot],
            blk=self.group * GROUP + target,
        )

    def to_right(self, slot):
        return self.copy(slot, self.member + 2, 0)

    def to_left(self, slot):
        return self.copy(slot, self.member - 2, 1)

    def to_sibling(self, slot):
        return self.copy(slot, self.chip * 2 + 1 - self.core, 2)

    def own(self):
        slot = self.member
        pl.when(self.chip < 3)(lambda: self.to_right(slot).start())
        pl.when(self.chip > 0)(lambda: self.to_left(slot).start())
        self.to_sibling(slot).start()

    def hop(self, hop):
        left, right = self.member - 2 * hop, self.member + 2 * hop

        @pl.when(self.chip >= hop)
        def _():
            self.to_right(left).wait_recv()
            pl.when(self.chip < 3)(lambda: self.to_right(left).start())
            self.to_sibling(left).start()

        @pl.when(self.chip + hop <= 3)
        def _():
            self.to_left(right).wait_recv()
            pl.when(self.chip > 0)(lambda: self.to_left(right).start())
            self.to_sibling(right).start()

    def finish(self):
        for other in range(4):
            self.to_sibling(other * 2 + 1 - self.core).wait_recv()

    def drain(self):
        chip = self.chip
        pl.when(chip < 3)(lambda: self.to_right(self.member).wait_send())
        pl.when(chip > 0)(lambda: self.to_left(self.member).wait_send())
        self.to_sibling(self.member).wait_send()
        for hop in range(1, 4):
            left, right = self.member - 2 * hop, self.member + 2 * hop

            @pl.when(chip >= hop)
            def _():
                pl.when(chip < 3)(lambda: self.to_right(left).wait_send())
                self.to_sibling(left).wait_send()

            @pl.when(chip + hop <= 3)
            def _():
                pl.when(chip > 0)(lambda: self.to_left(right).wait_send())
                self.to_sibling(right).wait_send()


def kernel(
    replicas,
    owners,
    grad_ref,
    left_ref,
    right_ref,
    lroot_ref,
    rroot_ref,
    update_ref,
    newl_ref,
    newr_ref,
    gown,
    yfar,
    ynear,
    ymix,
    yadd,
    xout,
    xpass,
    xland,
    fsum,
    summed,
    gbuf,
    qbuf,
    proot,
    lstat,
    rstat,
    lacc,
    lapp,
    usend,
    uland,
    squares,
    scales,
    ubuf,
    local_sem,
    root_sem,
    y_send,
    y_recv,
    x_send,
    x_recv,
    pair_send,
    pair_recv,
    qg_send,
    qg_recv,
    sp_send,
    sp_recv,
    gg_send,
    gg_recv,
    sq_send,
    sq_recv,
    sc_send,
    sc_recv,
    up_send,
    up_recv,
    out_sem,
):
    p = lax.axis_index("dp")
    b = lax.axis_index("blk")
    groups = owners // GROUP
    group, member = b // GROUP, b % GROUP
    chip, core = member // 2, member % 2
    y, xh = p // 2, p % 2
    xl, quarter = group // 4, group % 4
    row_count, width = grad_ref.shape[0], grad_ref.shape[3]
    half = row_count // 2
    slab = width // GROUP
    tile = 256
    tiles = width // tile

    pair = group * GROUP + chip * 2
    sibling = pair + 1 - core

    def half_of(which):
        return pl.ds(pl.multiple_of(which * (width // 2), width // 2), width // 2)

    def part_of(which):
        return pl.ds(pl.multiple_of(which * slab, slab), slab)

    loads = [
        pltpu.make_async_copy(grad_ref, gown, local_sem.at[0]),
        pltpu.make_async_copy(
            rroot_ref.at[:, half_of(core)], qbuf.at[chip, part_of(core)], local_sem.at[1]
        ),
        pltpu.make_async_copy(left_ref, lstat, local_sem.at[2]),
        pltpu.make_async_copy(right_ref, rstat, local_sem.at[3]),
    ]
    for block in range(GROUP):
        natural = (block % 2) * 4 + (quarter - block // 2 + 4) % 4
        loads.append(
            pltpu.make_async_copy(
                lroot_ref.at[:, pl.ds(pl.multiple_of(natural * 128, 128), 128)],
                proot.at[part_of(core), pl.ds(block * 128, 128)],
                root_sem.at[block],
            )
        )
    for load in loads:
        load.start()

    flip = (b + owners // 2) % owners
    turn = y * 2 + 1 - xh
    near_a = {"dp": p, "blk": flip}
    near_b = {"dp": turn, "blk": flip}

    def at_y(step, which):
        return ((y + step) % 4) * 2 + which

    barrier = pltpu.get_barrier_semaphore()
    partners = [{"dp": at_y(1, xh)}, {"dp": at_y(3, xh)}, near_b]
    partners += [{"blk": group * GROUP + (member + off) % GROUP} for off in range(1, GROUP)]
    partners += [{"blk": (group + off) % groups * GROUP + member} for off in range(1, groups)]
    for partner in partners:
        pl.semaphore_signal(barrier, inc=1, device_id=partner, device_id_type=MESH)
    pl.semaphore_wait(barrier, len(partners))

    sides = (1 - xh, xh)
    steps = (1, 3)

    def rows_of(way):
        return pl.ds(way * half, half)

    def y_copy(kind, way, which):
        to = at_y(steps[way], xh)
        if kind == 0:
            src = grad_ref.at[rows_of(way), at_y(2, sides[which])]
            dst = yfar.at[way, which]
        elif kind == 1:
            src = grad_ref.at[rows_of(1 - way), at_y(steps[way], sides[which])]
            dst = ynear.at[way, which]
        else:
            src = yadd.at[way, which]
            dst = ymix.at[way, which]
        return remote(
            src, dst, y_send.at[kind, way, which], y_recv.at[kind, way, which], dp=to
        )

    def x_copy(stage, route):
        if stage == 0:
            where = (near_a, near_b)[route]
            src, dst = xout.at[route], xpass.at[route]
        else:
            where = (near_b, near_a)[route]
            src, dst = xpass.at[route], xland.at[route]
        return remote(src, dst, x_send.at[stage, route], x_recv.at[stage, route], **where)

    ways = (0, 1)
    for way in ways:
        y_copy(0, way, 0).start()
    for way in ways:
        y_copy(1, way, 0).start()
        y_copy(0, way, 1).start()

    root_swap = remote(
        rroot_ref.at[:, half_of(1 - core)],
        qbuf.at[chip, part_of(core)],
        pair_send.at[0],
        pair_recv.at[0],
        blk=sibling,
    )
    root_swap.start()
    for load in loads[4:]:
        load.wait()
    factor_swap = remote(
        proot.at[part_of(core)],
        proot.at[part_of(core)],
        pair_send.at[1],
        pair_recv.at[1],
        blk=sibling,
    )
    factor_swap.start()
    loads[1].wait()
    root_swap.wait_recv()
    qgather = LineGather(
        lambda s: qbuf.at[s], group * GROUP + core, chip, qg_send, qg_recv
    )
    qgather.own()
    loads[0].wait()

    def y_add(way, which):
        y_copy(0, way, which).wait_recv()

        @pl.loop(0, half)
        def _(row):
            mine = gown[way * half + row, at_y(steps[way], sides[which])]
            passed = yfar[way, which, row]
            yadd[way, which, row] = (mine.astype(F32) + passed.astype(F32)).astype(BF16)

    for way in ways:
        y_add(way, 0)
        y_copy(2, way, 0).start()
    for way in ways:
        y_copy(1, way, 1).start()
    for way in ways:
        y_add(way, 1)
        y_copy(2, way, 1).start()

    def y_total(part, which, row):
        return (
            gown[part * half + row, at_y(0, sides[which])].astype(F32)
            + ymix[part, which, row].astype(F32)
            + ynear[1 - part, which, row].astype(F32)
        )

    for part in ways:
        y_copy(2, part, 0).wait_recv()
        y_copy(1, 1 - part, 0).wait_recv()

        @pl.loop(0, half)
        def _(row):
            xout[part, row] = y_total(part, 0, row).astype(BF16)

        x_copy(0, part).start()
    qgather.hop(1)
    for route in ways:
        x_copy(0, route).wait_recv()
        x_copy(1, route).start()
    qgather.hop(2)

    for part in ways:
        y_copy(2, part, 1).wait_recv()
        y_copy(1, 1 - part, 1).wait_recv()
        x_copy(1, part).wait_recv()

        @pl.loop(0, half)
        def _(row):
            total = y_total(part, 1, row) + xland[part, row].astype(F32)
            place = pl.ds(pl.multiple_of((part * half + row) * groups, groups), groups)
            for lane in range(width // 128):
                fsum[lane, place, :] = total[:, lane * 128 : (lane + 1) * 128]

    for block in range(groups):
        for lane in range(width // 128):
            summed[block, :, lane * 128 : (lane + 1) * 128] = fsum[
                lane, pl.ds(block, row_count, stride=groups), :
            ].astype(BF16)

    def spread_copy(across, ahead):
        to = (xl + across) % 2 * 4 + (quarter + ahead) % 4
        return remote(
            summed.at[to],
            gbuf.at[ahead, xl, chip, core],
            sp_send.at[across, ahead],
            sp_recv.at[ahead // 2],
            blk=to * GROUP + member,
        )

    spreads = [spread_copy(1, 0)]
    spreads += [spread_copy(across, ahead) for ahead in (1, 3, 2) for across in (1, 0)]
    for spread in spreads:
        spread.start()
    own_slot = gbuf.at[0, xl, chip, core]
    pltpu.make_async_copy(summed.at[group], own_slot, sp_recv.at[0]).start()

    def part_view(part, slot):
        return gbuf.at[pl.ds(2 * part, 2), :, slot // 2, slot % 2]

    gathers = [
        GroupGather(
            functools.partial(part_view, part),
            group,
            member,
            gg_send.at[part],
            gg_recv.at[part],
        )
        for part in (0, 1)
    ]
    for part in (0, 1):
        view = part_view(part, member)
        pltpu.make_async_copy(view, view, sp_recv.at[part]).wait()
        gathers[part].own()
    for hop in (1, 2, 3):
        for part in (0, 1):
            gathers[part].hop(hop)

    factor_swap.wait_recv()
    for part in (0, 1):
        gathers[part].finish()
        factor = proot[:, part * 512 : (part + 1) * 512]

        @pl.loop(0, tiles)
        def _(step):
            cols = pl.ds(pl.multiple_of(step * tile, tile), tile)
            grad = gbuf[2 * part : 2 * part + 2, :, :, :, :, cols].reshape(512, tile)
            product = jnp.dot(factor, grad, preferred_element_type=F32)
            if part == 0:
                lacc[:, cols] = product
            else:
                lapp[:, cols] = (product + lacc[:, cols]).astype(BF16)

    qgather.hop(3)

    applied = lapp[...]
    squares[member] = jnp.zeros((16, 128), F32)
    ends = owners // 2
    per_tile = ends // 2

    def update_copy(end):
        return remote(
            usend.at[end], uland.at[group, chip], up_send, up_recv, blk=core * ends + end
        )

    mine = pltpu.make_async_copy(usend.at[b % ends], uland.at[group, chip], up_recv)
    for turn_tile in (1, 0):
        number = (b % ends // per_tile + turn_tile) % 2
        cols = pl.ds(pl.multiple_of(number * tile, tile), tile)
        part = jnp.dot(
            applied, qbuf[:, :, cols].reshape(width, tile), preferred_element_type=F32
        )
        flipped = part.T
        usend[pl.ds(number * per_tile, per_tile)] = flipped.astype(BF16).reshape(
            per_tile, tile // per_tile, 2 * slab
        )
        squares[member, 8:16] += jnp.sum(
            (flipped * flipped).reshape(tile // 8, 8, 2, slab), axis=(0, 2)
        )
        if turn_tile == 0:
            pl.when(xl == core)(lambda: mine.start())
            pl.when(xl != core)(lambda: update_copy(b % ends).start())

        @pl.loop(1 if turn_tile == 0 else 0, per_tile)
        def _(off):
            update_copy(number * per_tile + (b + off) % per_tile).start()

    my_quad = (quarter - member % 4 + 4) % 4
    rows = gbuf[my_quad, member // 4].reshape(slab, width)
    wide = rows.astype(F32)
    squares[member, 0:8] = jnp.sum(
        (wide * wide).reshape(slab // 8, 8, width // 128, 128), axis=(0, 2)
    )

    def square_copy(off):
        to = (member + off) % GROUP
        return remote(
            squares.at[member],
            squares.at[member],
            sq_send.at[off],
            sq_recv.at[off],
            blk=group * GROUP + to,
        )

    for off in range(1, GROUP):
        square_copy(off).start()

    loads[2].wait()

    @pl.loop(0, tiles)
    def _(step):
        other = gbuf[step].reshape(tile, width)
        gram = lax.dot_general(
            rows, other, (((1,), (1,)), ((), ())), preferred_element_type=F32
        )
        for side in range(2):
            natural = side * 4 + (quarter - step + 4) % 4
            cols = pl.ds(pl.multiple_of(natural * 128, 128), 128)
            lstat[:, cols] = (
                STAT_DECAY * lstat[:, cols]
                + (1.0 - STAT_DECAY) * gram[:, side * 128 : (side + 1) * 128]
            )

    store_left = pltpu.make_async_copy(lstat, newl_ref, out_sem.at[0])
    store_left.start()

    for off in range(1, GROUP):
        square_copy(off).wait_recv()
    total = jnp.sum(squares[...], axis=0)
    grad_square = jnp.sum(total[0:8], keepdims=True)
    update_square = jnp.sum(total[8:16], keepdims=True)
    scale = jnp.sqrt((grad_square + GRAFT_EPS) / (update_square + GRAFT_EPS))
    scales[group] = jnp.broadcast_to(scale, (8, 128))

    def scale_copy(off):
        to = (group + off) % groups
        return remote(
            scales.at[group],
            scales.at[group],
            sc_send.at[off],
            sc_recv.at[off],
            blk=to * GROUP + member,
        )

    for off in range(1, groups):
        scale_copy(off).start()

    loads[3].wait()
    first = pl.ds(pl.multiple_of(member * slab, slab), slab)
    columns = gbuf[:, :, :, :, :, first].reshape(width, slab).T

    @pl.loop(0, tiles)
    def _(step):
        cols = pl.ds(pl.multiple_of(step * tile, tile), tile)
        grad = gbuf[:, :, :, :, :, cols].reshape(width, tile)
        gram = jnp.dot(columns, grad, preferred_element_type=F32)
        rstat[:, cols] = STAT_DECAY * rstat[:, cols] + (1.0 - STAT_DECAY) * gram

    store_right = pltpu.make_async_copy(rstat, newr_ref, out_sem.at[1])
    store_right.start()

    for kind in range(3):
        for way in ways:
            for which in (0, 1):
                y_copy(kind, way, which).wait_send()
    for route in ways:
        x_copy(0, route).wait_send()
        x_copy(1, route).wait_send()
    qgather.drain()
    root_swap.wait_send()
    factor_swap.wait_send()
    for spread in spreads:
        spread.wait_send()
    for part in (0, 1):
        gathers[part].drain()
    for off in range(1, GROUP):
        square_copy(off).wait_send()
    for off in range(1, groups):
        scale_copy(off).wait_send()
        scale_copy(off).wait_recv()

    pltpu.make_async_copy(uland, uland, up_recv).wait()
    for block in range(groups):
        factor = scales[block, 0:1]
        for part in range(GROUP):
            piece = uland[block, part // 2, :, part % 2 * slab : (part % 2 + 1) * slab]
            ubuf[block, :, part * slab : (part + 1) * slab] = (
                piece.astype(F32) * factor
            ).astype(BF16)
    store_update = pltpu.make_async_copy(ubuf, update_ref, out_sem.at[2])
    store_update.start()
    others = usend.at[pl.ds(0, ends - 1)]
    pl.when(xl == core)(lambda: pltpu.make_async_copy(others, others, up_send).wait())
    pl.when(xl != core)(lambda: pltpu.make_async_copy(usend, usend, up_send).wait())
    store_left.wait()
    store_right.wait()
    store_update.wait()


def on_device(replicas, owners, gradients, left_stat, right_stat, left_root, right_root):
    _, row_count, block_count, width = gradients.shape
    local = block_count // replicas
    slab = width // GROUP
    part = width // owners
    groups = owners // GROUP
    dma = pltpu.SemaphoreType.DMA
    update, new_left, new_right = pl.pallas_call(
        functools.partial(kernel, replicas, owners),
        out_shape=(
            jax.ShapeDtypeStruct((local, part, width), BF16),
            jax.ShapeDtypeStruct((slab, width), F32),
            jax.ShapeDtypeStruct((slab, width), F32),
        ),
        in_specs=[pl.BlockSpec(memory_space=pltpu.HBM)] * 5,
        out_specs=[pl.BlockSpec(memory_space=pl.ANY)] * 3,
        scratch_shapes=[
            pltpu.VMEM((row_count, replicas, local, width), BF16),
            *[pltpu.VMEM((2, 2, row_count // 2, local, width), BF16)] * 4,
            *[pltpu.VMEM((2, row_count // 2, local, width), BF16)] * 3,
            pltpu.VMEM((width // 128, row_count * local, 128), F32),
            pltpu.VMEM((local, row_count, width), BF16),
            pltpu.VMEM((4, 2, 4, 2, row_count, width), BF16),
            pltpu.VMEM((4, 2 * slab, width // 2), BF16),
            pltpu.VMEM((2 * slab, width), BF16),
            pltpu.VMEM((slab, width), F32),
            pltpu.VMEM((slab, width), F32),
            pltpu.VMEM((2 * slab, width), F32),
            pltpu.VMEM((2 * slab, width), BF16),
            pltpu.VMEM((owners // 2, part, 2 * slab), BF16),
            pltpu.VMEM((groups, 4, part, 2 * slab), BF16),
            pltpu.VMEM((GROUP, 16, 128), F32),
            pltpu.VMEM((groups, 8, 128), F32),
            pltpu.VMEM((local, part, width), BF16),
            dma((4,)),
            dma((GROUP,)),
            dma((3, 2, 2)),
            dma((3, 2, 2)),
            dma((2, 2)),
            dma((2, 2)),
            dma((2,)),
            dma((2,)),
            dma((4, 2)),
            dma((4,)),
            dma((2, 4)),
            dma((2,)),
            dma((2, GROUP, 3)),
            dma((2, GROUP)),
            dma((GROUP,)),
            dma((GROUP,)),
            dma((groups,)),
            dma((groups,)),
            dma,
            dma,
            dma((3,)),
        ],
        compiler_params=pltpu.CompilerParams(
            collective_id=0, has_side_effects=True, vmem_limit_bytes=40 * 2**20
        ),
        cost_estimate=pl.CostEstimate(
            flops=8 * slab * width * width, bytes_accessed=8 * 2**20, transcendentals=0
        ),
    )(
        *(
            pltpu.with_memory_space_constraint(x, pltpu.HBM)
            for x in (
                gradients.reshape(row_count, replicas, local, width),
                left_stat[0],
                right_stat[0],
                left_root[0],
                right_root[0],
            )
        )
    )
    return jnp.swapaxes(update, 1, 2), new_left[None], new_right[None]


def solution(mesh):
    specs = (P("dp", "blk", None, None),) + (P(("dp", "blk"), None, None),) * 4
    out_specs = (P("dp", None, "blk"), P(("dp", "blk"), None, None), P(("dp", "blk"), None, None))
    return jax.shard_map(
        functools.partial(on_device, mesh.shape["dp"], mesh.shape["blk"]),
        mesh=mesh,
        in_specs=specs,
        out_specs=out_specs,
        check_vma=False,
    )
```

```python
import functools

import jax
import jax.numpy as jnp
from jax import lax
from jax.experimental import pallas as pl
from jax.experimental.pallas import tpu as pltpu
from jax.sharding import PartitionSpec as P

GROUP = 8
STAT_DECAY = 0.95
GRAFT_EPS = 1e-06
MESH = pl.DeviceIdType.MESH
F32 = jnp.float32
BF16 = jnp.bfloat16


def remote(src, dst, send, recv, **where):
    return pltpu.make_async_remote_copy(
        src_ref=src,
        dst_ref=dst,
        send_sem=send,
        recv_sem=recv,
        device_id=where,
        device_id_type=MESH,
    )


class LineGather:
    def __init__(self, view, first, chip, send, recv):
        self.view, self.first, self.chip = view, first, chip
        self.send, self.recv = send, recv

    def copy(self, slot, way):
        target = self.chip + (1 if way == 0 else -1)
        return remote(
            self.view(slot),
            self.view(slot),
            self.send.at[slot, way],
            self.recv.at[slot],
            blk=self.first + 2 * target,
        )

    def own(self):
        pl.when(self.chip < 3)(lambda: self.copy(self.chip, 0).start())
        pl.when(self.chip > 0)(lambda: self.copy(self.chip, 1).start())

    def hop(self, hop):
        left, right = self.chip - hop, self.chip + hop

        @pl.when(left >= 0)
        def _():
            self.copy(left, 0).wait_recv()
            pl.when(self.chip < 3)(lambda: self.copy(left, 0).start())

        @pl.when(right <= 3)
        def _():
            self.copy(right, 1).wait_recv()
            pl.when(self.chip > 0)(lambda: self.copy(right, 1).start())

    def drain(self):
        chip = self.chip
        pl.when(chip < 3)(lambda: self.copy(chip, 0).wait_send())
        pl.when(chip > 0)(lambda: self.copy(chip, 1).wait_send())
        for hop in range(1, 4):
            left, right = chip - hop, chip + hop
            pl.when((left >= 0) & (chip < 3))(lambda: self.copy(left, 0).wait_send())
            pl.when((right <= 3) & (chip > 0))(lambda: self.copy(right, 1).wait_send())


class GroupGather:
    def __init__(self, view, group, member, send, recv):
        self.view, self.group, self.member = view, group, member
        self.send, self.recv = send, recv
        self.chip, self.core = member // 2, member % 2

    def copy(self, slot, target, way):
        return remote(
            self.view(slot),
            self.view(slot),
            self.send.at[slot, way],
            self.recv.at[slot],
            blk=self.group * GROUP + target,
        )

    def to_right(self, slot):
        return self.copy(slot, self.member + 2, 0)

    def to_left(self, slot):
        return self.copy(slot, self.member - 2, 1)

    def to_sibling(self, slot):
        return self.copy(slot, self.chip * 2 + 1 - self.core, 2)

    def own(self):
        slot = self.member
        pl.when(self.chip < 3)(lambda: self.to_right(slot).start())
        pl.when(self.chip > 0)(lambda: self.to_left(slot).start())
        self.to_sibling(slot).start()

    def hop(self, hop):
        left, right = self.member - 2 * hop, self.member + 2 * hop

        @pl.when(self.chip >= hop)
        def _():
            self.to_right(left).wait_recv()
            pl.when(self.chip < 3)(lambda: self.to_right(left).start())
            self.to_sibling(left).start()

        @pl.when(self.chip + hop <= 3)
        def _():
            self.to_left(right).wait_recv()
            pl.when(self.chip > 0)(lambda: self.to_left(right).start())
            self.to_sibling(right).start()

    def finish(self):
        for other in range(4):
            self.to_sibling(other * 2 + 1 - self.core).wait_recv()

    def drain(self):
        chip = self.chip
        pl.when(chip < 3)(lambda: self.to_right(self.member).wait_send())
        pl.when(chip > 0)(lambda: self.to_left(self.member).wait_send())
        self.to_sibling(self.member).wait_send()
        for hop in range(1, 4):
            left, right = self.member - 2 * hop, self.member + 2 * hop

            @pl.when(chip >= hop)
            def _():
                pl.when(chip < 3)(lambda: self.to_right(left).wait_send())
                self.to_sibling(left).wait_send()

            @pl.when(chip + hop <= 3)
            def _():
                pl.when(chip > 0)(lambda: self.to_left(right).wait_send())
                self.to_sibling(right).wait_send()


def kernel(
    replicas,
    owners,
    grad_ref,
    left_ref,
    right_ref,
    lroot_ref,
    rroot_ref,
    update_ref,
    newl_ref,
    newr_ref,
    gown,
    yfar,
    ynear,
    ymix,
    yadd,
    xout,
    xpass,
    xland,
    fsum,
    summed,
    gbuf,
    qbuf,
    proot,
    lstat,
    rstat,
    lacc,
    lapp,
    usend,
    uland,
    squares,
    scales,
    local_sem,
    root_sem,
    y_send,
    y_recv,
    x_send,
    x_recv,
    pair_send,
    pair_recv,
    qg_send,
    qg_recv,
    sp_send,
    sp_recv,
    gg_send,
    gg_recv,
    sq_send,
    sq_recv,
    sc_send,
    sc_recv,
    up_send,
    up_recv,
    out_sem,
):
    p = lax.axis_index("dp")
    b = lax.axis_index("blk")
    groups = owners // GROUP
    group, member = b // GROUP, b % GROUP
    chip, core = member // 2, member % 2
    y, xh = p // 2, p % 2
    xl, quarter = group // 4, group % 4
    row_count, width = grad_ref.shape[0], grad_ref.shape[3]
    half = row_count // 2
    slab = width // GROUP
    tile = 256
    tiles = width // tile

    pair = group * GROUP + chip * 2
    sibling = pair + 1 - core

    def half_of(which):
        return pl.ds(pl.multiple_of(which * (width // 2), width // 2), width // 2)

    def part_of(which):
        return pl.ds(pl.multiple_of(which * slab, slab), slab)

    loads = [
        pltpu.make_async_copy(grad_ref, gown, local_sem.at[0]),
        pltpu.make_async_copy(
            rroot_ref.at[:, half_of(core)], qbuf.at[chip, part_of(core)], local_sem.at[1]
        ),
        pltpu.make_async_copy(left_ref, lstat, local_sem.at[2]),
        pltpu.make_async_copy(right_ref, rstat, local_sem.at[3]),
    ]
    for block in range(GROUP):
        natural = (block % 2) * 4 + (quarter - block // 2 + 4) % 4
        loads.append(
            pltpu.make_async_copy(
                lroot_ref.at[:, pl.ds(pl.multiple_of(natural * 128, 128), 128)],
                proot.at[part_of(core), pl.ds(block * 128, 128)],
                root_sem.at[block],
            )
        )
    for load in loads:
        load.start()

    flip = (b + owners // 2) % owners
    turn = y * 2 + 1 - xh
    near_a = {"dp": p, "blk": flip}
    near_b = {"dp": turn, "blk": flip}

    def at_y(step, which):
        return ((y + step) % 4) * 2 + which

    barrier = pltpu.get_barrier_semaphore()
    partners = [{"dp": at_y(1, xh)}, {"dp": at_y(3, xh)}, near_b]
    partners += [{"blk": group * GROUP + (member + off) % GROUP} for off in range(1, GROUP)]
    partners += [{"blk": (group + off) % groups * GROUP + member} for off in range(1, groups)]
    for partner in partners:
        pl.semaphore_signal(barrier, inc=1, device_id=partner, device_id_type=MESH)
    pl.semaphore_wait(barrier, len(partners))

    sides = (1 - xh, xh)
    steps = (1, 3)

    def rows_of(way):
        return pl.ds(way * half, half)

    def y_copy(kind, way, which):
        to = at_y(steps[way], xh)
        if kind == 0:
            src = grad_ref.at[rows_of(way), at_y(2, sides[which])]
            dst = yfar.at[way, which]
        elif kind == 1:
            src = grad_ref.at[rows_of(1 - way), at_y(steps[way], sides[which])]
            dst = ynear.at[way, which]
        else:
            src = yadd.at[way, which]
            dst = ymix.at[way, which]
        return remote(
            src, dst, y_send.at[kind, way, which], y_recv.at[kind, way, which], dp=to
        )

    def x_copy(stage, route):
        if stage == 0:
            where = (near_a, near_b)[route]
            src, dst = xout.at[route], xpass.at[route]
        else:
            where = (near_b, near_a)[route]
            src, dst = xpass.at[route], xland.at[route]
        return remote(src, dst, x_send.at[stage, route], x_recv.at[stage, route], **where)

    ways = (0, 1)
    for way in ways:
        y_copy(0, way, 0).start()
    for way in ways:
        y_copy(1, way, 0).start()

    root_swap = remote(
        rroot_ref.at[:, half_of(1 - core)],
        qbuf.at[chip, part_of(core)],
        pair_send.at[0],
        pair_recv.at[0],
        blk=sibling,
    )
    root_swap.start()
    for load in loads[4:]:
        load.wait()
    factor_swap = remote(
        proot.at[part_of(core)],
        proot.at[part_of(core)],
        pair_send.at[1],
        pair_recv.at[1],
        blk=sibling,
    )
    factor_swap.start()
    loads[1].wait()
    root_swap.wait_recv()
    qgather = LineGather(
        lambda s: qbuf.at[s], group * GROUP + core, chip, qg_send, qg_recv
    )
    qgather.own()
    loads[0].wait()

    def y_add(way, which):
        y_copy(0, way, which).wait_recv()

        @pl.loop(0, half)
        def _(row):
            mine = gown[way * half + row, at_y(steps[way], sides[which])]
            passed = yfar[way, which, row]
            yadd[way, which, row] = (mine.astype(F32) + passed.astype(F32)).astype(BF16)

    for way in ways:
        y_add(way, 0)
        y_copy(2, way, 0).start()
    for kind in (0, 1):
        for way in ways:
            y_copy(kind, way, 1).start()

    def y_total(part, which, row):
        return (
            gown[part * half + row, at_y(0, sides[which])].astype(F32)
            + ymix[part, which, row].astype(F32)
            + ynear[1 - part, which, row].astype(F32)
        )

    for part in ways:
        y_copy(2, part, 0).wait_recv()
        y_copy(1, 1 - part, 0).wait_recv()

        @pl.loop(0, half)
        def _(row):
            xout[part, row] = y_total(part, 0, row).astype(BF16)

        x_copy(0, part).start()
    for way in ways:
        y_add(way, 1)
        y_copy(2, way, 1).start()
    qgather.hop(1)
    for route in ways:
        x_copy(0, route).wait_recv()
        x_copy(1, route).start()
    qgather.hop(2)

    for part in ways:
        y_copy(2, part, 1).wait_recv()
        y_copy(1, 1 - part, 1).wait_recv()
        x_copy(1, part).wait_recv()

        @pl.loop(0, half)
        def _(row):
            total = y_total(part, 1, row) + xland[part, row].astype(F32)
            place = pl.ds(pl.multiple_of((part * half + row) * groups, groups), groups)
            for lane in range(width // 128):
                fsum[lane, place, :] = total[:, lane * 128 : (lane + 1) * 128]

    for block in range(groups):
        for lane in range(width // 128):
            summed[block, :, lane * 128 : (lane + 1) * 128] = fsum[
                lane, pl.ds(block, row_count, stride=groups), :
            ].astype(BF16)

    def spread_copy(across, ahead):
        to = (xl + across) % 2 * 4 + (quarter + ahead) % 4
        return remote(
            summed.at[to],
            gbuf.at[ahead, xl, chip, core],
            sp_send.at[across, ahead],
            sp_recv.at[ahead // 2],
            blk=to * GROUP + member,
        )

    spreads = [spread_copy(1, 0)]
    spreads += [spread_copy(across, ahead) for ahead in (1, 3, 2) for across in (1, 0)]
    for spread in spreads:
        spread.start()
    own_slot = gbuf.at[0, xl, chip, core]
    pltpu.make_async_copy(summed.at[group], own_slot, sp_recv.at[0]).start()

    def part_view(part, slot):
        return gbuf.at[pl.ds(2 * part, 2), :, slot // 2, slot % 2]

    gathers = [
        GroupGather(
            functools.partial(part_view, part),
            group,
            member,
            gg_send.at[part],
            gg_recv.at[part],
        )
        for part in (0, 1)
    ]
    for part in (0, 1):
        view = part_view(part, member)
        pltpu.make_async_copy(view, view, sp_recv.at[part]).wait()
        gathers[part].own()
    for hop in (1, 2, 3):
        for part in (0, 1):
            gathers[part].hop(hop)

    factor_swap.wait_recv()
    for part in (0, 1):
        gathers[part].finish()
        factor = proot[:, part * 512 : (part + 1) * 512]

        @pl.loop(0, tiles)
        def _(step):
            cols = pl.ds(pl.multiple_of(step * tile, tile), tile)
            grad = gbuf[2 * part : 2 * part + 2, :, :, :, :, cols].reshape(512, tile)
            product = jnp.dot(factor, grad, preferred_element_type=F32)
            if part == 0:
                lacc[:, cols] = product
            else:
                lapp[:, cols] = (product + lacc[:, cols]).astype(BF16)

    qgather.hop(3)

    applied = lapp[...]
    squares[member] = jnp.zeros((16, 128), F32)
    ends = owners // 2
    per_tile = ends // 2

    def update_copy(end):
        return remote(
            usend.at[end], uland.at[group, chip], up_send, up_recv, blk=core * ends + end
        )

    mine = pltpu.make_async_copy(usend.at[b % ends], uland.at[group, chip], up_recv)
    for turn_tile in (1, 0):
        number = (b % ends // per_tile + turn_tile) % 2
        cols = pl.ds(pl.multiple_of(number * tile, tile), tile)
        part = jnp.dot(
            applied, qbuf[:, :, cols].reshape(width, tile), preferred_element_type=F32
        )
        flipped = part.T
        usend[pl.ds(number * per_tile, per_tile)] = flipped.astype(BF16).reshape(
            per_tile, tile // per_tile, 2 * slab
        )
        squares[member, 8:16] += jnp.sum(
            (flipped * flipped).reshape(tile // 8, 8, 2, slab), axis=(0, 2)
        )
        if turn_tile == 0:
            pl.when(xl == core)(lambda: mine.start())
            pl.when(xl != core)(lambda: update_copy(b % ends).start())

        @pl.loop(1 if turn_tile == 0 else 0, per_tile)
        def _(off):
            update_copy(number * per_tile + (b + off) % per_tile).start()

    my_quad = (quarter - member % 4 + 4) % 4
    rows = gbuf[my_quad, member // 4].reshape(slab, width)
    wide = rows.astype(F32)
    squares[member, 0:8] = jnp.sum(
        (wide * wide).reshape(slab // 8, 8, width // 128, 128), axis=(0, 2)
    )

    def square_copy(off):
        to = (member + off) % GROUP
        return remote(
            squares.at[member],
            squares.at[member],
            sq_send.at[off],
            sq_recv.at[off],
            blk=group * GROUP + to,
        )

    for off in range(1, GROUP):
        square_copy(off).start()

    loads[2].wait()

    @pl.loop(0, tiles)
    def _(step):
        other = gbuf[step].reshape(tile, width)
        gram = lax.dot_general(
            rows, other, (((1,), (1,)), ((), ())), preferred_element_type=F32
        )
        for side in range(2):
            natural = side * 4 + (quarter - step + 4) % 4
            cols = pl.ds(pl.multiple_of(natural * 128, 128), 128)
            lstat[:, cols] = (
                STAT_DECAY * lstat[:, cols]
                + (1.0 - STAT_DECAY) * gram[:, side * 128 : (side + 1) * 128]
            )

    store_left = pltpu.make_async_copy(lstat, newl_ref, out_sem.at[0])
    store_left.start()

    for off in range(1, GROUP):
        square_copy(off).wait_recv()
    total = jnp.sum(squares[...], axis=0)
    grad_square = jnp.sum(total[0:8], keepdims=True)
    update_square = jnp.sum(total[8:16], keepdims=True)
    scale = jnp.sqrt((grad_square + GRAFT_EPS) / (update_square + GRAFT_EPS))
    scales[group] = jnp.broadcast_to(scale, (8, 128))

    def scale_copy(off):
        to = (group + off) % groups
        return remote(
            scales.at[group],
            scales.at[group],
            sc_send.at[off],
            sc_recv.at[off],
            blk=to * GROUP + member,
        )

    for off in range(1, groups):
        scale_copy(off).start()

    loads[3].wait()
    first = pl.ds(pl.multiple_of(member * slab, slab), slab)
    columns = gbuf[:, :, :, :, :, first].reshape(width, slab).T

    @pl.loop(0, tiles)
    def _(step):
        cols = pl.ds(pl.multiple_of(step * tile, tile), tile)
        grad = gbuf[:, :, :, :, :, cols].reshape(width, tile)
        gram = jnp.dot(columns, grad, preferred_element_type=F32)
        rstat[:, cols] = STAT_DECAY * rstat[:, cols] + (1.0 - STAT_DECAY) * gram

    store_right = pltpu.make_async_copy(rstat, newr_ref, out_sem.at[1])
    store_right.start()

    for kind in range(3):
        for way in ways:
            for which in (0, 1):
                y_copy(kind, way, which).wait_send()
    for route in ways:
        x_copy(0, route).wait_send()
        x_copy(1, route).wait_send()
    qgather.drain()
    root_swap.wait_send()
    factor_swap.wait_send()
    for spread in spreads:
        spread.wait_send()
    for part in (0, 1):
        gathers[part].drain()
    for off in range(1, GROUP):
        square_copy(off).wait_send()
    for off in range(1, groups):
        scale_copy(off).wait_send()
        scale_copy(off).wait_recv()

    pltpu.make_async_copy(uland, uland, up_recv).wait()
    for block in range(groups):
        factor = scales[block, 0:1]
        for part in range(GROUP):
            piece = uland[block, part // 2, :, part % 2 * slab : (part % 2 + 1) * slab]
            update_ref[block, :, part * slab : (part + 1) * slab] = (
                piece.astype(F32) * factor
            ).astype(BF16)
    others = usend.at[pl.ds(0, ends - 1)]
    pl.when(xl == core)(lambda: pltpu.make_async_copy(others, others, up_send).wait())
    pl.when(xl != core)(lambda: pltpu.make_async_copy(usend, usend, up_send).wait())
    store_left.wait()
    store_right.wait()


def on_device(replicas, owners, gradients, left_stat, right_stat, left_root, right_root):
    _, row_count, block_count, width = gradients.shape
    local = block_count // replicas
    slab = width // GROUP
    part = width // owners
    groups = owners // GROUP
    dma = pltpu.SemaphoreType.DMA
    update, new_left, new_right = pl.pallas_call(
        functools.partial(kernel, replicas, owners),
        out_shape=(
            jax.ShapeDtypeStruct((local, part, width), BF16),
            jax.ShapeDtypeStruct((slab, width), F32),
            jax.ShapeDtypeStruct((slab, width), F32),
        ),
        in_specs=[pl.BlockSpec(memory_space=pltpu.HBM)] * 5,
        out_specs=[pl.BlockSpec(memory_space=pltpu.VMEM)] + [pl.BlockSpec(memory_space=pl.ANY)] * 2,
        scratch_shapes=[
            pltpu.VMEM((row_count, replicas, local, width), BF16),
            *[pltpu.VMEM((2, 2, row_count // 2, local, width), BF16)] * 4,
            *[pltpu.VMEM((2, row_count // 2, local, width), BF16)] * 3,
            pltpu.VMEM((width // 128, row_count * local, 128), F32),
            pltpu.VMEM((local, row_count, width), BF16),
            pltpu.VMEM((4, 2, 4, 2, row_count, width), BF16),
            pltpu.VMEM((4, 2 * slab, width // 2), BF16),
            pltpu.VMEM((2 * slab, width), BF16),
            pltpu.VMEM((slab, width), F32),
            pltpu.VMEM((slab, width), F32),
            pltpu.VMEM((2 * slab, width), F32),
            pltpu.VMEM((2 * slab, width), BF16),
            pltpu.VMEM((owners // 2, part, 2 * slab), BF16),
            pltpu.VMEM((groups, 4, part, 2 * slab), BF16),
            pltpu.VMEM((GROUP, 16, 128), F32),
            pltpu.VMEM((groups, 8, 128), F32),
            dma((4,)),
            dma((GROUP,)),
            dma((3, 2, 2)),
            dma((3, 2, 2)),
            dma((2, 2)),
            dma((2, 2)),
            dma((2,)),
            dma((2,)),
            dma((4, 2)),
            dma((4,)),
            dma((2, 4)),
            dma((2,)),
            dma((2, GROUP, 3)),
            dma((2, GROUP)),
            dma((GROUP,)),
            dma((GROUP,)),
            dma((groups,)),
            dma((groups,)),
            dma,
            dma,
            dma((3,)),
        ],
        compiler_params=pltpu.CompilerParams(
            collective_id=0, has_side_effects=True, vmem_limit_bytes=40 * 2**20
        ),
        cost_estimate=pl.CostEstimate(
            flops=8 * slab * width * width, bytes_accessed=8 * 2**20, transcendentals=0
        ),
    )(
        *(
            pltpu.with_memory_space_constraint(x, pltpu.HBM)
            for x in (
                gradients.reshape(row_count, replicas, local, width),
                left_stat[0],
                right_stat[0],
                left_root[0],
                right_root[0],
            )
        )
    )
    return jnp.swapaxes(update, 1, 2), new_left[None], new_right[None]


def solution(mesh):
    specs = (P("dp", "blk", None, None),) + (P(("dp", "blk"), None, None),) * 4
    out_specs = (P("dp", None, "blk"), P(("dp", "blk"), None, None), P(("dp", "blk"), None, None))
    return jax.shard_map(
        functools.partial(on_device, mesh.shape["dp"], mesh.shape["blk"]),
        mesh=mesh,
        in_specs=specs,
        out_specs=out_specs,
        check_vma=False,
    )
```

```python
import functools

import jax
import jax.numpy as jnp
from jax import lax
from jax.experimental import pallas as pl
from jax.experimental.pallas import tpu as pltpu
from jax.sharding import PartitionSpec as P

GROUP = 8
STAT_DECAY = 0.95
GRAFT_EPS = 1e-06
MESH = pl.DeviceIdType.MESH
F32 = jnp.float32
BF16 = jnp.bfloat16


def remote(src, dst, send, recv, **where):
    return pltpu.make_async_remote_copy(
        src_ref=src,
        dst_ref=dst,
        send_sem=send,
        recv_sem=recv,
        device_id=where,
        device_id_type=MESH,
    )


class LineGather:
    def __init__(self, view, first, chip, send, recv):
        self.view, self.first, self.chip = view, first, chip
        self.send, self.recv = send, recv

    def copy(self, slot, way):
        target = self.chip + (1 if way == 0 else -1)
        return remote(
            self.view(slot),
            self.view(slot),
            self.send.at[slot, way],
            self.recv.at[slot],
            blk=self.first + 2 * target,
        )

    def own(self):
        pl.when(self.chip < 3)(lambda: self.copy(self.chip, 0).start())
        pl.when(self.chip > 0)(lambda: self.copy(self.chip, 1).start())

    def hop(self, hop):
        left, right = self.chip - hop, self.chip + hop

        @pl.when(left >= 0)
        def _():
            self.copy(left, 0).wait_recv()
            pl.when(self.chip < 3)(lambda: self.copy(left, 0).start())

        @pl.when(right <= 3)
        def _():
            self.copy(right, 1).wait_recv()
            pl.when(self.chip > 0)(lambda: self.copy(right, 1).start())

    def drain(self):
        chip = self.chip
        pl.when(chip < 3)(lambda: self.copy(chip, 0).wait_send())
        pl.when(chip > 0)(lambda: self.copy(chip, 1).wait_send())
        for hop in range(1, 4):
            left, right = chip - hop, chip + hop
            pl.when((left >= 0) & (chip < 3))(lambda: self.copy(left, 0).wait_send())
            pl.when((right <= 3) & (chip > 0))(lambda: self.copy(right, 1).wait_send())


class GroupGather:
    def __init__(self, view, group, member, send, recv):
        self.view, self.group, self.member = view, group, member
        self.send, self.recv = send, recv
        self.chip, self.core = member // 2, member % 2

    def copy(self, slot, target, way):
        return remote(
            self.view(slot),
            self.view(slot),
            self.send.at[slot, way],
            self.recv.at[slot],
            blk=self.group * GROUP + target,
        )

    def to_right(self, slot):
        return self.copy(slot, self.member + 2, 0)

    def to_left(self, slot):
        return self.copy(slot, self.member - 2, 1)

    def to_sibling(self, slot):
        return self.copy(slot, self.chip * 2 + 1 - self.core, 2)

    def own(self):
        slot = self.member
        pl.when(self.chip < 3)(lambda: self.to_right(slot).start())
        pl.when(self.chip > 0)(lambda: self.to_left(slot).start())
        self.to_sibling(slot).start()

    def hop(self, hop):
        left, right = self.member - 2 * hop, self.member + 2 * hop

        @pl.when(self.chip >= hop)
        def _():
            self.to_right(left).wait_recv()
            pl.when(self.chip < 3)(lambda: self.to_right(left).start())
            self.to_sibling(left).start()

        @pl.when(self.chip + hop <= 3)
        def _():
            self.to_left(right).wait_recv()
            pl.when(self.chip > 0)(lambda: self.to_left(right).start())
            self.to_sibling(right).start()

    def finish(self):
        for other in range(4):
            self.to_sibling(other * 2 + 1 - self.core).wait_recv()

    def drain(self):
        chip = self.chip
        pl.when(chip < 3)(lambda: self.to_right(self.member).wait_send())
        pl.when(chip > 0)(lambda: self.to_left(self.member).wait_send())
        self.to_sibling(self.member).wait_send()
        for hop in range(1, 4):
            left, right = self.member - 2 * hop, self.member + 2 * hop

            @pl.when(chip >= hop)
            def _():
                pl.when(chip < 3)(lambda: self.to_right(left).wait_send())
                self.to_sibling(left).wait_send()

            @pl.when(chip + hop <= 3)
            def _():
                pl.when(chip > 0)(lambda: self.to_left(right).wait_send())
                self.to_sibling(right).wait_send()


def kernel(
    replicas,
    owners,
    grad_ref,
    left_ref,
    right_ref,
    lroot_ref,
    rroot_ref,
    update_ref,
    newl_ref,
    newr_ref,
    gown,
    yfar,
    ynear,
    ymix,
    yadd,
    xout,
    xpass,
    xland,
    fsum,
    summed,
    gbuf,
    qbuf,
    proot,
    lstat,
    rstat,
    lacc,
    lapp,
    usend,
    uland,
    squares,
    scales,
    ubuf,
    local_sem,
    root_sem,
    y_send,
    y_recv,
    x_send,
    x_recv,
    pair_send,
    pair_recv,
    qg_send,
    qg_recv,
    sp_send,
    sp_recv,
    gg_send,
    gg_recv,
    sq_send,
    sq_recv,
    sc_send,
    sc_recv,
    up_send,
    up_recv,
    out_sem,
):
    p = lax.axis_index("dp")
    b = lax.axis_index("blk")
    groups = owners // GROUP
    group, member = b // GROUP, b % GROUP
    chip, core = member // 2, member % 2
    y, xh = p // 2, p % 2
    xl, quarter = group // 4, group % 4
    row_count, width = grad_ref.shape[0], grad_ref.shape[3]
    half = row_count // 2
    slab = width // GROUP
    tile = 256
    tiles = width // tile

    pair = group * GROUP + chip * 2
    sibling = pair + 1 - core

    def half_of(which):
        return pl.ds(pl.multiple_of(which * (width // 2), width // 2), width // 2)

    def part_of(which):
        return pl.ds(pl.multiple_of(which * slab, slab), slab)

    loads = [
        pltpu.make_async_copy(grad_ref, gown, local_sem.at[0]),
        pltpu.make_async_copy(
            rroot_ref.at[:, half_of(core)], qbuf.at[chip, part_of(core)], local_sem.at[1]
        ),
        pltpu.make_async_copy(left_ref, lstat, local_sem.at[2]),
        pltpu.make_async_copy(right_ref, rstat, local_sem.at[3]),
    ]
    for block in range(GROUP):
        natural = (block % 2) * 4 + (quarter - block // 2 + 4) % 4
        loads.append(
            pltpu.make_async_copy(
                lroot_ref.at[:, pl.ds(pl.multiple_of(natural * 128, 128), 128)],
                proot.at[part_of(core), pl.ds(block * 128, 128)],
                root_sem.at[block],
            )
        )
    for load in loads:
        load.start()

    flip = (b + owners // 2) % owners
    turn = y * 2 + 1 - xh
    near_a = {"dp": p, "blk": flip}
    near_b = {"dp": turn, "blk": flip}

    def at_y(step, which):
        return ((y + step) % 4) * 2 + which

    barrier = pltpu.get_barrier_semaphore()
    partners = [{"dp": at_y(1, xh)}, {"dp": at_y(3, xh)}, near_b]
    partners += [{"blk": group * GROUP + (member + off) % GROUP} for off in range(1, GROUP)]
    partners += [{"blk": (group + off) % groups * GROUP + member} for off in range(1, groups)]
    for partner in partners:
        pl.semaphore_signal(barrier, inc=1, device_id=partner, device_id_type=MESH)
    pl.semaphore_wait(barrier, len(partners))

    sides = (1 - xh, xh)
    steps = (1, 3)

    def rows_of(way):
        return pl.ds(way * half, half)

    def y_copy(kind, way, which):
        to = at_y(steps[way], xh)
        if kind == 0:
            src = grad_ref.at[rows_of(way), at_y(2, sides[which])]
            dst = yfar.at[way, which]
        elif kind == 1:
            src = grad_ref.at[rows_of(1 - way), at_y(steps[way], sides[which])]
            dst = ynear.at[way, which]
        else:
            src = yadd.at[way, which]
            dst = ymix.at[way, which]
        return remote(
            src, dst, y_send.at[kind, way, which], y_recv.at[kind, way, which], dp=to
        )

    def x_copy(stage, route):
        if stage == 0:
            where = (near_a, near_b)[route]
            src, dst = xout.at[route], xpass.at[route]
        else:
            where = (near_b, near_a)[route]
            src, dst = xpass.at[route], xland.at[route]
        return remote(src, dst, x_send.at[stage, route], x_recv.at[stage, route], **where)

    ways = (0, 1)
    for way in ways:
        y_copy(0, way, 0).start()
    for way in ways:
        y_copy(1, way, 0).start()
        y_copy(0, way, 1).start()

    root_swap = remote(
        rroot_ref.at[:, half_of(1 - core)],
        qbuf.at[chip, part_of(core)],
        pair_send.at[0],
        pair_recv.at[0],
        blk=sibling,
    )
    root_swap.start()
    qgathers = [
        LineGather(
            functools.partial(lambda which, s: qbuf.at[s, part_of(which)], which),
            group * GROUP + core,
            chip,
            qg_send.at[piece],
            qg_recv.at[piece],
        )
        for piece, which in ((0, core), (1, 1 - core))
    ]
    loads[1].wait()
    qgathers[0].own()
    root_swap.wait_recv()
    qgathers[1].own()
    for load in loads[4:]:
        load.wait()
    factor_swap = remote(
        proot.at[part_of(core)],
        proot.at[part_of(core)],
        pair_send.at[1],
        pair_recv.at[1],
        blk=sibling,
    )
    factor_swap.start()
    loads[0].wait()

    def y_add(way, which):
        y_copy(0, way, which).wait_recv()

        @pl.loop(0, half)
        def _(row):
            mine = gown[way * half + row, at_y(steps[way], sides[which])]
            passed = yfar[way, which, row]
            yadd[way, which, row] = (mine.astype(F32) + passed.astype(F32)).astype(BF16)

    for way in ways:
        y_add(way, 0)
        y_copy(2, way, 0).start()
    for way in ways:
        y_copy(1, way, 1).start()
    for way in ways:
        y_add(way, 1)
        y_copy(2, way, 1).start()

    def y_total(part, which, row):
        return (
            gown[part * half + row, at_y(0, sides[which])].astype(F32)
            + ymix[part, which, row].astype(F32)
            + ynear[1 - part, which, row].astype(F32)
        )

    for part in ways:
        y_copy(2, part, 0).wait_recv()
        y_copy(1, 1 - part, 0).wait_recv()

        @pl.loop(0, half)
        def _(row):
            xout[part, row] = y_total(part, 0, row).astype(BF16)

        x_copy(0, part).start()
    for qgather in qgathers:
        qgather.hop(1)
    for route in ways:
        x_copy(0, route).wait_recv()
        x_copy(1, route).start()
    for qgather in qgathers:
        qgather.hop(2)

    for part in ways:
        y_copy(2, part, 1).wait_recv()
        y_copy(1, 1 - part, 1).wait_recv()
        x_copy(1, part).wait_recv()

        @pl.loop(0, half)
        def _(row):
            total = y_total(part, 1, row) + xland[part, row].astype(F32)
            place = pl.ds(pl.multiple_of((part * half + row) * groups, groups), groups)
            for lane in range(width // 128):
                fsum[lane, place, :] = total[:, lane * 128 : (lane + 1) * 128]

    for block in range(groups):
        for lane in range(width // 128):
            summed[block, :, lane * 128 : (lane + 1) * 128] = fsum[
                lane, pl.ds(block, row_count, stride=groups), :
            ].astype(BF16)

    def spread_copy(across, ahead):
        to = (xl + across) % 2 * 4 + (quarter + ahead) % 4
        return remote(
            summed.at[to],
            gbuf.at[ahead, xl, chip, core],
            sp_send.at[across, ahead],
            sp_recv.at[ahead // 2],
            blk=to * GROUP + member,
        )

    spreads = [spread_copy(1, 0)]
    spreads += [spread_copy(across, ahead) for ahead in (1, 3, 2) for across in (1, 0)]
    for spread in spreads:
        spread.start()
    own_slot = gbuf.at[0, xl, chip, core]
    pltpu.make_async_copy(summed.at[group], own_slot, sp_recv.at[0]).start()

    def part_view(part, slot):
        return gbuf.at[pl.ds(2 * part, 2), :, slot // 2, slot % 2]

    gathers = [
        GroupGather(
            functools.partial(part_view, part),
            group,
            member,
            gg_send.at[part],
            gg_recv.at[part],
        )
        for part in (0, 1)
    ]
    for part in (0, 1):
        view = part_view(part, member)
        pltpu.make_async_copy(view, view, sp_recv.at[part]).wait()
        gathers[part].own()
    for hop in (1, 2, 3):
        for part in (0, 1):
            gathers[part].hop(hop)

    factor_swap.wait_recv()
    for part in (0, 1):
        gathers[part].finish()
        factor = proot[:, part * 512 : (part + 1) * 512]

        @pl.loop(0, tiles)
        def _(step):
            cols = pl.ds(pl.multiple_of(step * tile, tile), tile)
            grad = gbuf[2 * part : 2 * part + 2, :, :, :, :, cols].reshape(512, tile)
            product = jnp.dot(factor, grad, preferred_element_type=F32)
            if part == 0:
                lacc[:, cols] = product
            else:
                lapp[:, cols] = (product + lacc[:, cols]).astype(BF16)

    for qgather in qgathers:
        qgather.hop(3)

    applied = lapp[...]
    squares[member] = jnp.zeros((16, 128), F32)
    ends = owners // 2
    per_tile = ends // 2

    def update_copy(end):
        return remote(
            usend.at[end], uland.at[group, chip], up_send, up_recv, blk=core * ends + end
        )

    mine = pltpu.make_async_copy(usend.at[b % ends], uland.at[group, chip], up_recv)
    for turn_tile in (1, 0):
        number = (b % ends // per_tile + turn_tile) % 2
        cols = pl.ds(pl.multiple_of(number * tile, tile), tile)
        part = jnp.dot(
            applied, qbuf[:, :, cols].reshape(width, tile), preferred_element_type=F32
        )
        flipped = part.T
        usend[pl.ds(number * per_tile, per_tile)] = flipped.astype(BF16).reshape(
            per_tile, tile // per_tile, 2 * slab
        )
        squares[member, 8:16] += jnp.sum(
            (flipped * flipped).reshape(tile // 8, 8, 2, slab), axis=(0, 2)
        )
        if turn_tile == 0:
            pl.when(xl == core)(lambda: mine.start())
            pl.when(xl != core)(lambda: update_copy(b % ends).start())

        @pl.loop(1 if turn_tile == 0 else 0, per_tile)
        def _(off):
            update_copy(number * per_tile + (b + off) % per_tile).start()

    my_quad = (quarter - member % 4 + 4) % 4
    rows = gbuf[my_quad, member // 4].reshape(slab, width)
    wide = rows.astype(F32)
    squares[member, 0:8] = jnp.sum(
        (wide * wide).reshape(slab // 8, 8, width // 128, 128), axis=(0, 2)
    )

    def square_copy(off):
        to = (member + off) % GROUP
        return remote(
            squares.at[member],
            squares.at[member],
            sq_send.at[off],
            sq_recv.at[off],
            blk=group * GROUP + to,
        )

    for off in range(1, GROUP):
        square_copy(off).start()

    loads[2].wait()

    @pl.loop(0, tiles)
    def _(step):
        other = gbuf[step].reshape(tile, width)
        gram = lax.dot_general(
            rows, other, (((1,), (1,)), ((), ())), preferred_element_type=F32
        )
        for side in range(2):
            natural = side * 4 + (quarter - step + 4) % 4
            cols = pl.ds(pl.multiple_of(natural * 128, 128), 128)
            lstat[:, cols] = (
                STAT_DECAY * lstat[:, cols]
                + (1.0 - STAT_DECAY) * gram[:, side * 128 : (side + 1) * 128]
            )

    store_left = pltpu.make_async_copy(lstat, newl_ref, out_sem.at[0])
    store_left.start()

    for off in range(1, GROUP):
        square_copy(off).wait_recv()
    total = jnp.sum(squares[...], axis=0)
    grad_square = jnp.sum(total[0:8], keepdims=True)
    update_square = jnp.sum(total[8:16], keepdims=True)
    scale = jnp.sqrt((grad_square + GRAFT_EPS) / (update_square + GRAFT_EPS))
    scales[group] = jnp.broadcast_to(scale, (8, 128))

    def scale_copy(off):
        to = (group + off) % groups
        return remote(
            scales.at[group],
            scales.at[group],
            sc_send.at[off],
            sc_recv.at[off],
            blk=to * GROUP + member,
        )

    for off in range(1, groups):
        scale_copy(off).start()

    loads[3].wait()
    first = pl.ds(pl.multiple_of(member * slab, slab), slab)
    columns = gbuf[:, :, :, :, :, first].reshape(width, slab).T

    @pl.loop(0, tiles)
    def _(step):
        cols = pl.ds(pl.multiple_of(step * tile, tile), tile)
        grad = gbuf[:, :, :, :, :, cols].reshape(width, tile)
        gram = jnp.dot(columns, grad, preferred_element_type=F32)
        rstat[:, cols] = STAT_DECAY * rstat[:, cols] + (1.0 - STAT_DECAY) * gram

    store_right = pltpu.make_async_copy(rstat, newr_ref, out_sem.at[1])
    store_right.start()

    for kind in range(3):
        for way in ways:
            for which in (0, 1):
                y_copy(kind, way, which).wait_send()
    for route in ways:
        x_copy(0, route).wait_send()
        x_copy(1, route).wait_send()
    for qgather in qgathers:
        qgather.drain()
    root_swap.wait_send()
    factor_swap.wait_send()
    for spread in spreads:
        spread.wait_send()
    for part in (0, 1):
        gathers[part].drain()
    for off in range(1, GROUP):
        square_copy(off).wait_send()
    for off in range(1, groups):
        scale_copy(off).wait_send()
        scale_copy(off).wait_recv()

    pltpu.make_async_copy(uland, uland, up_recv).wait()
    for block in range(groups):
        factor = scales[block, 0:1]
        for part in range(GROUP):
            piece = uland[block, part // 2, :, part % 2 * slab : (part % 2 + 1) * slab]
            ubuf[block, :, part * slab : (part + 1) * slab] = (
                piece.astype(F32) * factor
            ).astype(BF16)
    store_update = pltpu.make_async_copy(ubuf, update_ref, out_sem.at[2])
    store_update.start()
    others = usend.at[pl.ds(0, ends - 1)]
    pl.when(xl == core)(lambda: pltpu.make_async_copy(others, others, up_send).wait())
    pl.when(xl != core)(lambda: pltpu.make_async_copy(usend, usend, up_send).wait())
    store_left.wait()
    store_right.wait()
    store_update.wait()


def on_device(replicas, owners, gradients, left_stat, right_stat, left_root, right_root):
    _, row_count, block_count, width = gradients.shape
    local = block_count // replicas
    slab = width // GROUP
    part = width // owners
    groups = owners // GROUP
    dma = pltpu.SemaphoreType.DMA
    update, new_left, new_right = pl.pallas_call(
        functools.partial(kernel, replicas, owners),
        out_shape=(
            jax.ShapeDtypeStruct((local, part, width), BF16),
            jax.ShapeDtypeStruct((slab, width), F32),
            jax.ShapeDtypeStruct((slab, width), F32),
        ),
        in_specs=[pl.BlockSpec(memory_space=pltpu.HBM)] * 5,
        out_specs=[pl.BlockSpec(memory_space=pl.ANY)] * 3,
        scratch_shapes=[
            pltpu.VMEM((row_count, replicas, local, width), BF16),
            *[pltpu.VMEM((2, 2, row_count // 2, local, width), BF16)] * 4,
            *[pltpu.VMEM((2, row_count // 2, local, width), BF16)] * 3,
            pltpu.VMEM((width // 128, row_count * local, 128), F32),
            pltpu.VMEM((local, row_count, width), BF16),
            pltpu.VMEM((4, 2, 4, 2, row_count, width), BF16),
            pltpu.VMEM((4, 2 * slab, width // 2), BF16),
            pltpu.VMEM((2 * slab, width), BF16),
            pltpu.VMEM((slab, width), F32),
            pltpu.VMEM((slab, width), F32),
            pltpu.VMEM((2 * slab, width), F32),
            pltpu.VMEM((2 * slab, width), BF16),
            pltpu.VMEM((owners // 2, part, 2 * slab), BF16),
            pltpu.VMEM((groups, 4, part, 2 * slab), BF16),
            pltpu.VMEM((GROUP, 16, 128), F32),
            pltpu.VMEM((groups, 8, 128), F32),
            pltpu.VMEM((local, part, width), BF16),
            dma((4,)),
            dma((GROUP,)),
            dma((3, 2, 2)),
            dma((3, 2, 2)),
            dma((2, 2)),
            dma((2, 2)),
            dma((2,)),
            dma((2,)),
            dma((2, 4, 2)),
            dma((2, 4)),
            dma((2, 4)),
            dma((2,)),
            dma((2, GROUP, 3)),
            dma((2, GROUP)),
            dma((GROUP,)),
            dma((GROUP,)),
            dma((groups,)),
            dma((groups,)),
            dma,
            dma,
            dma((3,)),
        ],
        compiler_params=pltpu.CompilerParams(
            collective_id=0, has_side_effects=True, vmem_limit_bytes=40 * 2**20
        ),
        cost_estimate=pl.CostEstimate(
            flops=8 * slab * width * width, bytes_accessed=8 * 2**20, transcendentals=0
        ),
    )(
        *(
            pltpu.with_memory_space_constraint(x, pltpu.HBM)
            for x in (
                gradients.reshape(row_count, replicas, local, width),
                left_stat[0],
                right_stat[0],
                left_root[0],
                right_root[0],
            )
        )
    )
    return jnp.swapaxes(update, 1, 2), new_left[None], new_right[None]


def solution(mesh):
    specs = (P("dp", "blk", None, None),) + (P(("dp", "blk"), None, None),) * 4
    out_specs = (P("dp", None, "blk"), P(("dp", "blk"), None, None), P(("dp", "blk"), None, None))
    return jax.shard_map(
        functools.partial(on_device, mesh.shape["dp"], mesh.shape["blk"]),
        mesh=mesh,
        in_specs=specs,
        out_specs=out_specs,
        check_vma=False,
    )
```
